512 devices in a mesh: dp: 32 (over z, core), tensor: 16 (over x, y).
Axes of the slice: x: 4, y: 4, z: 16, core: 2. Of those that a mesh axis runs over, the one named last changes fastest.
Arguments:
- buffer: float32 [8192, 26624], P('dp', 'tensor'), may hold values from -300 to 300
- factor: float32 [26624, 512], P('tensor', 'dp'), may hold values from -6 to 6
Outputs:
- momentum_new: float32 [8192, 26624], P('dp', 'tensor')
- update: bfloat16 [8192, 26624], P('dp', 'tensor')
- factor_new: float32 [26624, 512], P('tensor', 'dp')
The draws below stay inside these ranges and needn't reach their ends.
All inputs are finite; a program needn't handle non-finite values.
Results may differ from the reference program's by a relative error of at most 0.0018.
Values sent between devices are 32-bit elements; how exact they have to be, the bound alone decides.
A program may use at most 64 MiB of HBM per device.

```python
import jax
import jax.numpy as jnp
from jax import lax

ROWS = 8192
COLS = 26624
RANK = 512


def draw_buffer(key, part):
    key = jax.random.fold_in(key, 11)
    first, second, third = jax.random.split(key, 3)
    row_pos = jnp.arange(ROWS, dtype=jnp.float32) / ROWS
    col_pos = jnp.arange(COLS, dtype=jnp.float32) / COLS
    base = jax.random.normal(first, (ROWS, COLS), jnp.float32)
    spread = 1.15
    row_scale = 3.0 ** (row_pos - 0.5) * jnp.exp(jax.random.uniform(second, (ROWS,), jnp.float32, -spread, spread))
    col_scale = 3.0 ** (col_pos - 0.5) * jnp.exp(jax.random.uniform(third, (COLS,), jnp.float32, -spread, spread))
    return base * row_scale[:, None] * col_scale[None, :]


def levels(own_key, shape, shards, least, high):
    gain = 1.0
    for axis_at, blocks in shards:
        heights = jax.random.uniform(jax.random.fold_in(jax.random.fold_in(own_key, 6), axis_at), (blocks,), jnp.float32, least / len(shards), high / len(shards))
        gain = gain * jnp.repeat(jnp.exp(heights), shape[axis_at] // blocks).reshape((-1,) + (1,) * (len(shape) - 1 - axis_at))
    return gain


def gaussian(rng, shape, width, bound, cuts=(), held_as=jnp.bfloat16):
    entries = width * jax.random.normal(rng, shape, jnp.float32)
    if cuts:
        entries = entries * levels(rng, shape, cuts, -0.22, 0.18)
    return jnp.clip(entries, -bound, bound).astype(held_as)


def setup_inputs(seed: int = 0) -> dict:
    streams_of = jax.random.split(jax.random.key(seed), 3)
    return {
        "buffer": draw_buffer(jax.random.fold_in(streams_of[2], 71), 0),
        "factor": gaussian(streams_of[1], (COLS, RANK), 1.0, 6.0, ((0, 16), (1, 32)), jnp.float32),
    }


def reference(buffer, factor):
    high = lax.Precision.HIGHEST
    power = jnp.dot(buffer.astype(jnp.float32), factor.astype(jnp.float32), preferred_element_type=jnp.float32, precision=high) / jnp.sqrt(jnp.float32(COLS))
    gram = jnp.dot(power.T.astype(jnp.float32), power.astype(jnp.float32), preferred_element_type=jnp.float32, precision=high)
    lower = jnp.linalg.cholesky(gram)
    basis = lax.linalg.triangular_solve(lower, power, left_side=False, lower=True, transpose_a=True)
    right = jnp.dot(buffer.T.astype(jnp.float32), basis.astype(jnp.float32), preferred_element_type=jnp.float32, precision=high)
    scales = 1.0 / jnp.sqrt(lax.optimization_barrier(jnp.sum(right * right, axis=0)) / COLS + 1e-06)
    factor_new = right * scales[None, :]
    momentum_new = buffer - 0.05 * jnp.dot(basis.astype(jnp.float32), right.T.astype(jnp.float32), preferred_element_type=jnp.float32, precision=high)
    update = jnp.sqrt(jnp.float32(ROWS) / RANK) * jnp.dot(basis.astype(jnp.float32), factor_new.T.astype(jnp.float32), preferred_element_type=jnp.float32, precision=high)
    return (momentum_new, update.astype(jnp.bfloat16), factor_new)
```

```python
import functools
import math

import jax
import jax.numpy as jnp
from jax import lax
from jax.experimental import pallas as pl
from jax.experimental.pallas import tpu as pltpu
from jax.sharding import PartitionSpec as P

MESH = pl.DeviceIdType.MESH
HIGHEST = lax.Precision.HIGHEST
HIGH = lax.Precision.HIGH
NT = (((1,), (1,)), ((), ()))
NN = (((1,), (0,)), ((), ()))
LIMIT = 56 * 1024 * 1024


def dot(a, b, dims, precision):
    return lax.dot_general(
        a, b, dims, precision=precision, preferred_element_type=jnp.float32
    )


class Place:
    def __init__(self, chips, peers):
        dp = lax.axis_index("dp")
        self.z, self.c = dp // 2, dp % 2
        self.t = lax.axis_index("tensor")
        self.chips, self.peers = chips, peers

    def chip(self, offset):
        return lax.rem(self.z + offset + self.chips, self.chips)

    def at(self, offset):
        return {"dp": 2 * self.chip(offset) + self.c}

    def partner(self):
        return {"dp": 2 * self.z + 1 - self.c}

    def peer(self, k):
        return lax.rem(self.t + k, self.peers)


def remote(src, dst, send, recv, device):
    return pltpu.make_async_remote_copy(
        src_ref=src,
        dst_ref=dst,
        send_sem=send,
        recv_sem=recv,
        device_id=device,
        device_id_type=MESH,
    )


def await_bytes(ref, sem):
    pltpu.make_async_copy(ref, ref, sem).wait()


def enter(here, ring):
    barrier = pltpu.get_barrier_semaphore()

    def greet(device):
        pl.semaphore_signal(barrier, inc=1, device_id=device, device_id_type=MESH)

    @pl.loop(1, here.peers)
    def _(k):
        greet({"tensor": here.peer(k)})

    greet(here.partner())
    if ring:

        @pl.loop(1, here.chips)
        def _(k):
            greet(here.at(k))

        count = here.chips - 1
    else:
        greet(here.at(1))
        greet(here.at(-1))
        count = 2
    pl.semaphore_wait(barrier, here.peers - 1 + 1 + count)


def offset_of(n):
    return ((n + 1) // 2) * (2 * (n % 2) - 1)


def rows16(ref, chip, core, sub=None):
    start = 32 * chip + 16 * core
    if sub is None:
        return ref.at[pl.ds(pl.multiple_of(start, 16), 16)]
    return ref.at[pl.ds(pl.multiple_of(start + 8 * sub, 8), 8)]


class Gather:
    def __init__(self, here, buf, send, recv, pair_recv):
        self.here, self.buf = here, buf
        self.send, self.recv, self.pair_recv = send, recv, pair_recv
        self.half = here.chips // 2

    def subs(self, step, way):
        if step < self.half:
            return (0, 1)
        return (way,) if step == self.half else ()

    def forward(self, step, way, sub):
        here, sign = self.here, 1 - 2 * way
        ref = rows16(self.buf, here.chip(-sign * (step - 1)), here.c, sub)
        remote(
            ref, ref, self.send, self.recv.at[way, step - 1, sub], here.at(sign)
        ).start()

    def share(self, offset, slot):
        here = self.here
        ref = rows16(self.buf, here.chip(offset), here.c)
        remote(ref, ref, self.send, self.pair_recv.at[slot], here.partner()).start()

    def begin(self):
        for sub in (0, 1):
            for way in (0, 1):
                self.forward(1, way, sub)
        self.share(0, 0)

    def step(self, step):
        here = self.here
        for sub in (0, 1):
            for way in (0, 1):
                if sub in self.subs(step, way):
                    sign = 1 - 2 * way
                    ref = rows16(self.buf, here.chip(-sign * step), here.c, sub)
                    await_bytes(ref, self.recv.at[way, step - 1, sub])
                    if sub in self.subs(step + 1, way):
                        self.forward(step + 1, way, sub)
        if step < self.half:
            self.share(step, 2 * step - 1)
            self.share(-step, 2 * step)
        else:
            self.share(step, 2 * step - 1)

    def shared(self, n):
        here = self.here
        ref = rows16(self.buf, here.chip(offset_of(n)), 1 - here.c)
        await_bytes(ref, self.pair_recv.at[n])

    def end(self):
        rows = 16 * (2 * here_chips(self) - 1)
        await_bytes(self.buf.at[pl.ds(0, rows)], self.send)


def here_chips(gather):
    return gather.here.chips


def power_kernel(
    chips,
    peers,
    scale,
    b_ref,
    f_ref,
    pt_ref,
    gram_ref,
    fall,
    part,
    parts,
    gpart,
    gpair,
    gsplit,
    gsplits,
    gsum,
    gsums,
    f_send,
    f_recv,
    f_pair,
    rs_send,
    rs_recv,
    ag_send,
    ag_recv,
    g_send,
    g_recv,
):
    here = Place(chips, peers)
    enter(here, True)
    groups = chips // 4
    piece = 128 // peers
    per_chip = peers // 4
    own = rows16(fall, here.z, here.c)
    own[...] = f_ref[...]
    gather = Gather(here, fall, f_send, f_recv, f_pair)
    gather.begin()

    def product(g):
        for n in range(4 * g, 4 * g + 4):
            gather.shared(n)
        rows = [
            fall[pl.ds(pl.multiple_of(32 * here.chip(offset_of(n)), 32), 32), :]
            for n in range(4 * g, 4 * g + 4)
        ]
        part[g] = dot(jnp.concatenate(rows, axis=0), b_ref[...], NT, HIGHEST)

        @pl.loop(1, peers)
        def _(k):
            other = here.peer(k)
            remote(
                part.at[g, pl.ds(pl.multiple_of(piece * other, piece), piece)],
                parts.at[g, k],
                rs_send,
                rs_recv.at[g],
                {"tensor": other},
            ).start()

    def total(g):
        mine = pl.ds(pl.multiple_of(piece * here.t, piece), piece)
        parts[g, 0] = part[g, mine, :]
        await_bytes(parts.at[g, pl.ds(1, peers - 1)], rs_recv.at[g])
        chip = here.chip(offset_of(4 * g + here.t // per_chip))
        start = 32 * chip + piece * lax.rem(here.t, per_chip)
        place = pt_ref.at[pl.ds(pl.multiple_of(start, piece), piece)]
        place[...] = jnp.sum(parts[g], axis=0) * scale

        @pl.loop(1, peers)
        def _(k):
            remote(
                place, place, ag_send, ag_recv.at[g], {"tensor": here.peer(k)}
            ).start()

    for step in range(1, chips // 2 + 1):
        gather.step(step)
        if step > 2 and step % 2 == 1:
            total((step - 3) // 2)
        if step % 2 == 0:
            product(step // 2 - 1)
    total(groups - 1)
    for g in range(groups):
        await_bytes(parts.at[g, pl.ds(1, peers - 1)], ag_recv.at[g])

    rank = 32 * chips
    block = rank // peers
    half = block // 2
    each = half // chips
    mine = pl.ds(pl.multiple_of(block * here.t, block), block)
    gpart[...] = dot(pt_ref[mine, :], pt_ref[...], NT, HIGHEST)
    theirs = pl.ds(pl.multiple_of(half * (1 - here.c), half), half)
    keep = pl.ds(pl.multiple_of(half * here.c, half), half)
    pair = remote(gpart.at[theirs], gpair, g_send.at[0], g_recv.at[0], here.partner())
    pair.start()
    pair.wait()
    chip_sum = gpart[keep, :] + gpair[...]
    for k in range(chips):
        gsplit[k] = chip_sum[each * k : each * (k + 1), :]

    @pl.loop(1, chips)
    def _(k):
        remote(
            gsplit.at[here.chip(k)],
            gsplits.at[k],
            g_send.at[1],
            g_recv.at[1],
            here.at(k),
        ).start()

    gsplits[0] = gsplit[here.z]
    await_bytes(gsplits.at[pl.ds(1, chips - 1)], g_recv.at[1])
    await_bytes(gsplits.at[pl.ds(1, chips - 1)], g_send.at[1])
    gsums[here.z] = jnp.sum(gsplits[...], axis=0)

    @pl.loop(1, chips)
    def _(k):
        place = gsums.at[here.z]
        remote(place, place, g_send.at[2], g_recv.at[2], here.at(k)).start()

    await_bytes(gsums.at[pl.ds(0, chips - 1)], g_recv.at[2])
    await_bytes(gsums.at[pl.ds(0, chips - 1)], g_send.at[2])
    gram_ref[here.t, here.c] = gsums[...].reshape(half, rank)

    @pl.loop(1, peers)
    def _(k):
        place = gram_ref.at[here.t, here.c]
        remote(
            place, place, g_send.at[3], g_recv.at[3], {"tensor": here.peer(k)}
        ).start()

    await_bytes(gram_ref.at[pl.ds(0, peers - 1), 0], g_recv.at[3])
    halves = gram_ref.at[:, here.c]
    pair = remote(halves, halves, g_send.at[4], g_recv.at[4], here.partner())
    pair.start()
    pair.wait()

    await_bytes(gram_ref.at[pl.ds(0, peers - 1), 0], g_send.at[3])
    gather.end()
    for sem in (rs_send, ag_send):
        await_bytes(parts.at[:, pl.ds(1, peers - 1)], sem)


def splat(value):
    return jnp.broadcast_to(value, (8, 128))


def diagonal_block(a_ref, w_ref, start):
    where = pl.ds(start, 128)
    s = a_ref[where, where]
    rows = lax.broadcasted_iota(jnp.int32, (128, 128), 0)
    lanes = lax.broadcasted_iota(jnp.int32, (128, 128), 1)
    x = jnp.where(rows == lanes, 1.0, 0.0).astype(jnp.float32)
    for m in range(16):
        columns = [
            jnp.broadcast_to(s[:, 8 * m + j : 8 * m + j + 1], s.shape) for j in range(8)
        ]
        d = {
            (i, j): splat(columns[j][i : i + 1, :]) for j in range(8) for i in range(j, 8)
        }
        r = [splat(s[i : i + 1, :]) for i in range(8)]
        q = [splat(x[i : i + 1, :]) for i in range(8)]
        inverse = []
        for k in range(8):
            inv = lax.rsqrt(d[k, k])
            inverse.append(inv)
            r[k] = r[k] * inv
            q[k] = q[k] * inv
            for i in range(k + 1, 8):
                d[i, k] = d[i, k] * inv
            for i in range(k + 1, 8):
                for j in range(k + 1, i + 1):
                    d[i, j] = d[i, j] - d[i, k] * d[j, k]
                r[i] = r[i] - d[i, k] * r[k]
                q[i] = q[i] - d[i, k] * q[k]
        for k in range(8):
            w_ref[pl.ds(start + 8 * m + k, 1), where] = q[k][0:1, :]
        if m == 15:
            break
        for k in range(7, -1, -1):
            for i in range(k + 1, 8):
                r[k] = r[k] - d[i, k] * r[i]
                q[k] = q[k] - d[i, k] * q[i]
            r[k] = r[k] * inverse[k]
            q[k] = q[k] * inverse[k]
        s, x = s[8:], x[8:]
        for j in range(8):
            c = columns[j][8:]
            s = s - c * r[j][0:1, :]
            x = x - c * q[j][0:1, :]


def factor_kernel(gram_ref, w_ref, a_ref):
    rank = gram_ref.shape[0]
    a_ref[...] = gram_ref[...]
    w_ref[...] = jnp.zeros_like(w_ref)
    for start in range(0, rank, 128):
        stop = start + 128
        diagonal_block(a_ref, w_ref, start)
        here = slice(start, stop)
        w11 = w_ref[here, here]
        if start:
            w_ref[here, 0:start] = dot(w11, w_ref[here, 0:start], NN, HIGHEST)
        if stop < rank:
            below = slice(stop, rank)
            lower = dot(a_ref[below, here], w11, NT, HIGHEST)
            a_ref[below, below] = a_ref[below, below] - dot(lower, lower, NT, HIGHEST)
            w_ref[below, 0:stop] = w_ref[below, 0:stop] - dot(
                lower, w_ref[here, 0:stop], NN, HIGHEST
            )


def column_tiles(columns):
    return [(at, min(256, columns - at)) for at in range(0, columns, 256)]


def right_kernel(
    chips,
    peers,
    mean,
    gain,
    b_ref,
    pt_ref,
    w_ref,
    momentum_ref,
    update_ref,
    factor_ref,
    rpart,
    rpair,
    moving,
    rall,
    squares,
    pair_send,
    pair_recv,
    rs_send,
    rs_recv,
    send,
    recv,
    ag_pair,
    sq_send,
    sq_recv,
):
    here = Place(chips, peers)
    enter(here, False)
    ring = chips // 2
    rank = 32 * chips
    tiles = column_tiles(b_ref.shape[1])
    last = chips // 4 - 1

    def product(g):
        chipped = [here.chip(offset_of(n)) for n in range(4 * g, 4 * g + 4)]
        rows = [pt_ref[pl.ds(pl.multiple_of(32 * i, 32), 32), :] for i in chipped]
        p = jnp.concatenate(rows, axis=0)
        for at, width in tiles:
            r = dot(p, b_ref[:, at : at + width], NN, HIGH)
            for n, i in enumerate(chipped):
                place = pl.ds(pl.multiple_of(32 * i, 32), 32)
                rpart[place, at : at + width] = r[32 * n : 32 * n + 32, :]
        for n, i in enumerate(chipped):
            remote(
                rows16(rpart, i, 1 - here.c),
                rpair.at[4 * g + n],
                pair_send,
                pair_recv.at[g],
                here.partner(),
            ).start()

    def own(n, sub):
        chip = here.chip(offset_of(n))
        return rows16(rpart, chip, here.c, sub)[...] + rpair[n, 8 * sub : 8 * sub + 8, :]

    def subs(k, way):
        return (0, 1) if k < ring else (way,)

    def scatter(k):
        for sub in (0, 1):
            for way in (0, 1):
                if sub not in subs(k, way):
                    continue
                sign = 1 - 2 * way
                place = moving.at[way, k, pl.ds(8 * sub, 8)]
                n = 2 * k - 1 if (way == 0 or k == ring) else 2 * k
                if k < ring and sub in subs(k + 1, way):
                    await_bytes(place, rs_recv.at[way, k, sub])
                    place[...] = place[...] + own(n, sub)
                else:
                    place[...] = own(n, sub)
                remote(
                    place,
                    moving.at[way, k - 1, pl.ds(8 * sub, 8)],
                    rs_send,
                    rs_recv.at[way, k - 1, sub],
                    here.at(sign),
                ).start()

    for g in range(last, -1, -1):
        product(g)
        await_bytes(rpair.at[pl.ds(4 * g, 4)], pair_recv.at[g])
        scatter(2 * g + 2)
        scatter(2 * g + 1)
    for sub in (0, 1):
        for way in (0, 1):
            place = moving.at[way, 0, pl.ds(8 * sub, 8)]
            await_bytes(place, rs_recv.at[way, 0, sub])
        rows16(rall, here.z, here.c, sub)[...] = (
            own(0, sub)
            + moving[0, 0, 8 * sub : 8 * sub + 8, :]
            + moving[1, 0, 8 * sub : 8 * sub + 8, :]
        )
    gather = Gather(here, rall, send, recv, ag_pair)
    gather.begin()
    q = dot(pt_ref[...].T, w_ref[...], NT, HIGH)
    for step in range(1, ring + 1):
        gather.step(step)
    for n in range(chips):
        gather.shared(n)

    await_bytes(rpart.at[pl.ds(0, rank // 2)], pair_send)
    depth = min(128, rank)
    total = jnp.zeros((8, rank), jnp.float32)
    for at, width in tiles:
        for row in range(0, rank, depth):
            rpart[row : row + depth, at : at + width] = dot(
                w_ref[row : row + depth, 0 : row + depth],
                rall[0 : row + depth, at : at + width],
                NN,
                HIGH,
            )
        right = rpart[:, at : at + width]
        total = total + dot(
            jnp.ones((8, width), jnp.float32), right * right, NT, HIGHEST
        )
    squares[0] = total[0:1, :]

    @pl.loop(1, peers)
    def _(k):
        remote(
            squares.at[0], squares.at[k], sq_send, sq_recv, {"tensor": here.peer(k)}
        ).start()

    q1 = (q * -0.05).astype(jnp.bfloat16)
    for at, width in tiles:
        momentum_ref[:, at : at + width] = b_ref[:, at : at + width] + dot(
            q1, rpart[:, at : at + width].astype(jnp.bfloat16), NN, None
        )
    await_bytes(squares.at[pl.ds(1, peers - 1)], sq_recv)
    scales = lax.rsqrt(jnp.sum(squares[...], axis=0) * mean + 1e-06)
    scaled = q * (scales * gain)
    for at, width in tiles:
        update_ref[:, at : at + width] = dot(
            scaled, rpart[:, at : at + width], NN, HIGH
        ).astype(jnp.bfloat16)
    start = 32 * here.z + 16 * here.c
    lanes = lax.broadcasted_iota(jnp.int32, (16, rank), 1)
    rows = lax.broadcasted_iota(jnp.int32, (16, rank), 0)
    picked = jnp.where(lanes == rows + start, jnp.broadcast_to(scales, (16, rank)), 0.0)
    factor_ref[...] = rows16(rpart, here.z, here.c)[...] * jnp.sum(
        picked, axis=1, keepdims=True
    )

    gather.end()
    await_bytes(rall.at[pl.ds(0, 16 * (chips - 1))], rs_send)
    await_bytes(squares.at[pl.ds(1, peers - 1)], sq_send)


def body(chips, peers, buffer, factor):
    rows, columns = buffer.shape
    rank = 32 * chips
    half = rank // peers // 2
    each = half // chips
    total_columns = columns * peers
    groups = chips // 4
    ring = chips // 2
    f32 = jnp.float32
    dma = pltpu.SemaphoreType.DMA
    vmem = pl.BlockSpec(memory_space=pltpu.VMEM)

    def params(collective):
        return pltpu.CompilerParams(
            collective_id=collective, has_side_effects=True, vmem_limit_bytes=LIMIT
        )

    power_t, gram = pl.pallas_call(
        functools.partial(power_kernel, chips, peers, 1.0 / math.sqrt(total_columns)),
        out_shape=(
            jax.ShapeDtypeStruct((rank, rows), f32),
            jax.ShapeDtypeStruct((peers, 2, half, rank), f32),
        ),
        in_specs=[vmem] * 2,
        out_specs=(vmem, vmem),
        scratch_shapes=[
            pltpu.VMEM((rank, columns), f32),
            pltpu.VMEM((groups, 128, rows), f32),
            pltpu.VMEM((groups, peers, 128 // peers, rows), f32),
            pltpu.VMEM((2 * half, rank), f32),
            pltpu.VMEM((half, rank), f32),
            pltpu.VMEM((chips, each, rank), f32),
            pltpu.VMEM((chips, each, rank), f32),
            pltpu.VMEM((each, rank), f32),
            pltpu.VMEM((chips, each, rank), f32),
            dma,
            dma((2, ring, 2)),
            dma((chips,)),
            dma,
            dma((groups,)),
            dma,
            dma((groups,)),
            dma((5,)),
            dma((5,)),
        ],
        compiler_params=params(0),
        name="power",
    )(buffer, factor.T)

    w = pl.pallas_call(
        factor_kernel,
        out_shape=jax.ShapeDtypeStruct((rank, rank), f32),
        in_specs=[vmem],
        out_specs=vmem,
        scratch_shapes=[pltpu.VMEM((rank, rank), f32)],
        compiler_params=pltpu.CompilerParams(vmem_limit_bytes=LIMIT),
        name="factor",
    )(gram.reshape(rank, rank))

    momentum, update, factor_t = pl.pallas_call(
        functools.partial(
            right_kernel,
            chips,
            peers,
            1.0 / total_columns,
            math.sqrt(rows * 2 * chips / rank),
        ),
        out_shape=(
            jax.ShapeDtypeStruct((rows, columns), f32),
            jax.ShapeDtypeStruct((rows, columns), jnp.bfloat16),
            jax.ShapeDtypeStruct((16, columns), f32),
        ),
        in_specs=[vmem] * 3,
        out_specs=(vmem,) * 3,
        scratch_shapes=[
            pltpu.VMEM((rank, columns), f32),
            pltpu.VMEM((chips, 16, columns), f32),
            pltpu.VMEM((2, ring + 1, 16, columns), f32),
            pltpu.VMEM((rank, columns), f32),
            pltpu.VMEM((peers, 1, rank), f32),
            dma,
            dma((groups,)),
            dma,
            dma((2, ring, 2)),
            dma,
            dma((2, ring, 2)),
            dma((chips,)),
            dma,
            dma,
        ],
        compiler_params=params(1),
        name="right",
    )(buffer, power_t, w)
    return momentum, update, factor_t.T


def solution(mesh):
    chips, peers = mesh.shape["dp"] // 2, mesh.shape["tensor"]
    placed = (P("dp", "tensor"), P("tensor", "dp"))
    return jax.shard_map(
        functools.partial(body, chips, peers),
        mesh=mesh,
        in_specs=placed,
        out_specs=(P("dp", "tensor"), P("dp", "tensor"), P("tensor", "dp")),
        check_vma=False,
    )
```

```python
import functools
import math

import jax
import jax.numpy as jnp
from jax import lax
from jax.experimental import pallas as pl
from jax.experimental.pallas import tpu as pltpu
from jax.sharding import PartitionSpec as P

MESH = pl.DeviceIdType.MESH
HIGHEST = lax.Precision.HIGHEST
NT = (((1,), (1,)), ((), ()))
NN = (((1,), (0,)), ((), ()))
LIMIT = 56 * 1024 * 1024


def dot(a, b, dims, precision):
    return lax.dot_general(
        a, b, dims, precision=precision, preferred_element_type=jnp.float32
    )


class Place:
    def __init__(self, chips, peers):
        dp = lax.axis_index("dp")
        self.z, self.c = dp // 2, dp % 2
        self.t = lax.axis_index("tensor")
        self.chips, self.peers = chips, peers

    def chip(self, offset):
        return lax.rem(self.z + offset + self.chips, self.chips)

    def at(self, offset):
        return {"dp": 2 * self.chip(offset) + self.c}

    def partner(self):
        return {"dp": 2 * self.z + 1 - self.c}

    def peer(self, k):
        return lax.rem(self.t + k, self.peers)


def remote(src, dst, send, recv, device):
    return pltpu.make_async_remote_copy(
        src_ref=src,
        dst_ref=dst,
        send_sem=send,
        recv_sem=recv,
        device_id=device,
        device_id_type=MESH,
    )


def await_bytes(ref, sem):
    pltpu.make_async_copy(ref, ref, sem).wait()


def enter(here, ring):
    barrier = pltpu.get_barrier_semaphore()

    def greet(device):
        pl.semaphore_signal(barrier, inc=1, device_id=device, device_id_type=MESH)

    @pl.loop(1, here.peers)
    def _(k):
        greet({"tensor": here.peer(k)})

    greet(here.partner())
    if ring:

        @pl.loop(1, here.chips)
        def _(k):
            greet(here.at(k))

        count = here.chips - 1
    else:
        greet(here.at(1))
        greet(here.at(-1))
        count = 2
    pl.semaphore_wait(barrier, here.peers - 1 + 1 + count)


def offset_of(n):
    return ((n + 1) // 2) * (2 * (n % 2) - 1)


def rows16(ref, chip, core, sub=None):
    start = 32 * chip + 16 * core
    if sub is None:
        return ref.at[pl.ds(pl.multiple_of(start, 16), 16)]
    return ref.at[pl.ds(pl.multiple_of(start + 8 * sub, 8), 8)]


class Gather:
    def __init__(self, here, buf, send, recv, pair_recv):
        self.here, self.buf = here, buf
        self.send, self.recv, self.pair_recv = send, recv, pair_recv
        self.half = here.chips // 2

    def subs(self, step, way):
        if step < self.half:
            return (0, 1)
        return (way,) if step == self.half else ()

    def forward(self, step, way, sub):
        here, sign = self.here, 1 - 2 * way
        ref = rows16(self.buf, here.chip(-sign * (step - 1)), here.c, sub)
        remote(
            ref, ref, self.send, self.recv.at[way, step - 1, sub], here.at(sign)
        ).start()

    def share(self, offset, slot):
        here = self.here
        ref = rows16(self.buf, here.chip(offset), here.c)
        remote(ref, ref, self.send, self.pair_recv.at[slot], here.partner()).start()

    def begin(self):
        for sub in (0, 1):
            for way in (0, 1):
                self.forward(1, way, sub)
        self.share(0, 0)

    def step(self, step):
        here = self.here
        for sub in (0, 1):
            for way in (0, 1):
                if sub in self.subs(step, way):
                    sign = 1 - 2 * way
                    ref = rows16(self.buf, here.chip(-sign * step), here.c, sub)
                    await_bytes(ref, self.recv.at[way, step - 1, sub])
                    if sub in self.subs(step + 1, way):
                        self.forward(step + 1, way, sub)
        if step < self.half:
            self.share(step, 2 * step - 1)
            self.share(-step, 2 * step)
        else:
            self.share(step, 2 * step - 1)

    def shared(self, n):
        here = self.here
        ref = rows16(self.buf, here.chip(offset_of(n)), 1 - here.c)
        await_bytes(ref, self.pair_recv.at[n])

    def end(self):
        rows = 16 * (2 * self.here.chips - 1)
        await_bytes(self.buf.at[pl.ds(0, rows)], self.send)


def split(value):
    high = value.astype(jnp.bfloat16)
    return high, (value - high.astype(jnp.float32)).astype(jnp.bfloat16)


def dot3(a, b, dims):
    return (
        dot(a[0], b[0], dims, None) + dot(a[0], b[1], dims, None)
    ) + dot(a[1], b[0], dims, None)


def splat(value):
    return jnp.broadcast_to(value, (8, 128))


def eliminate(m, carry, w_ref, start):
    s, x = carry
    columns = [jnp.broadcast_to(s[:, j : j + 1], s.shape) for j in range(8)]
    d = {(i, j): splat(columns[j][i : i + 1, :]) for j in range(8) for i in range(j, 8)}
    r = [splat(s[i : i + 1, :]) for i in range(8)]
    q = [splat(x[i : i + 1, :]) for i in range(8)]
    inverse = []
    for k in range(8):
        inv = lax.rsqrt(d[k, k])
        inverse.append(inv)
        r[k] = r[k] * inv
        q[k] = q[k] * inv
        for i in range(k + 1, 8):
            d[i, k] = d[i, k] * inv
        for i in range(k + 1, 8):
            for j in range(k + 1, i + 1):
                d[i, j] = d[i, j] - d[i, k] * d[j, k]
            r[i] = r[i] - d[i, k] * r[k]
            q[i] = q[i] - d[i, k] * q[k]
    sublane = lax.broadcasted_iota(jnp.int32, (8, 128), 0)
    done = q[0]
    for k in range(1, 8):
        done = jnp.where(sublane == k, q[k], done)
    w_ref[pl.ds(pl.multiple_of(start + 8 * m, 8), 8), start : start + 128] = done
    for k in range(7, -1, -1):
        for i in range(k + 1, 8):
            r[k] = r[k] - d[i, k] * r[i]
            q[k] = q[k] - d[i, k] * q[i]
        r[k] = r[k] * inverse[k]
        q[k] = q[k] * inverse[k]
    s, x = s[8:], x[8:]
    for j in range(8):
        c = columns[j][8:]
        s = s - c * r[j][0:1, :]
        x = x - c * q[j][0:1, :]
    blank = jnp.zeros((8, 128), jnp.float32)
    s = pltpu.roll(jnp.concatenate([s, blank], axis=0), 120, 1)
    return s, jnp.concatenate([x, blank], axis=0)


def invert_factor(a_ref, w_ref, between, after):
    rank = a_ref.shape[0]
    rows = lax.broadcasted_iota(jnp.int32, (128, 128), 0)
    lanes = lax.broadcasted_iota(jnp.int32, (128, 128), 1)
    w_ref[...] = jnp.zeros_like(w_ref)
    for start in range(0, rank, 128):
        stop = start + 128
        here = slice(start, stop)
        carry = (a_ref[here, here], jnp.where(rows == lanes, 1.0, 0.0).astype(jnp.float32))
        for quarter in range(4):
            carry = lax.fori_loop(
                4 * quarter,
                4 * quarter + 4,
                functools.partial(eliminate, w_ref=w_ref, start=start),
                carry,
            )
            between()
        w11 = w_ref[here, here]
        if start:
            w_ref[here, 0:start] = dot(w11, w_ref[here, 0:start], NN, HIGHEST)
        if stop < rank:
            below = slice(stop, rank)
            lower = dot(a_ref[below, here], w11, NT, HIGHEST)
            a_ref[below, below] = a_ref[below, below] - dot(lower, lower, NT, HIGHEST)
            w_ref[below, 0:stop] = w_ref[below, 0:stop] - dot(
                lower, w_ref[here, 0:stop], NN, HIGHEST
            )
        after(here)


def column_tiles(columns):
    return [(at, min(256, columns - at)) for at in range(0, columns, 256)]


def kernel(
    chips,
    peers,
    scale,
    mean,
    gain,
    b_ref,
    f_ref,
    momentum_ref,
    update_ref,
    factor_ref,
    bsplit,
    fall,
    part,
    first_parts,
    last_parts,
    arrived,
    pt,
    psplit,
    gpart,
    gpair,
    gsplit,
    gsplits,
    gsums,
    gram,
    a_ref,
    w_ref,
    wsplit,
    rpart,
    rpair,
    moving,
    rall,
    rsplit,
    squares,
    f_send,
    f_recv,
    f_pair,
    p_send,
    p_recv,
    g_send,
    g_recv,
    pair_send,
    pair_recv,
    rs_send,
    rs_recv,
    ag_send,
    ag_recv,
    ag_pair,
    sq_send,
    sq_recv,
):
    here = Place(chips, peers)
    rank = 32 * chips
    ring = chips // 2
    groups = chips // 4
    last = groups - 1
    tiles = column_tiles(b_ref.shape[1])
    own = rows16(fall, here.z, here.c)
    own[...] = f_ref[...]
    enter(here, True)
    gather = Gather(here, fall, f_send, f_recv, f_pair)
    gather.begin()
    bsplit[0], bsplit[1] = split(b_ref[...])

    def product(g):
        for n in range(4 * g, 4 * g + 4):
            gather.shared(n)
        rows = [
            fall[pl.ds(pl.multiple_of(32 * here.chip(offset_of(n)), 32), 32), :]
            for n in range(4 * g, 4 * g + 4)
        ]
        f = split(jnp.concatenate(rows, axis=0))
        part[128 * g : 128 * g + 128, :] = dot3(f, (bsplit[0], bsplit[1]), NT)

    def spread(base, rows, parts, turn):
        piece = rows // peers

        @pl.loop(1, peers)
        def _(k):
            other = here.peer(k)
            start = pl.multiple_of(base + piece * other, 8)
            remote(
                part.at[pl.ds(start, piece)],
                parts.at[k],
                p_send.at[turn],
                p_recv.at[turn],
                {"tensor": other},
            ).start()

    def total(base, rows, parts, turn):
        piece = rows // peers
        mine = pl.ds(pl.multiple_of(base + piece * here.t, 8), piece)
        parts[0] = part[mine, :]
        await_bytes(parts.at[pl.ds(1, peers - 1)], p_recv.at[turn])
        arrived[mine, :] = jnp.sum(parts[...], axis=0) * scale

        @pl.loop(1, peers)
        def _(k):
            place = arrived.at[mine]
            remote(
                place,
                place,
                p_send.at[turn + 1],
                p_recv.at[turn + 1],
                {"tensor": here.peer(k)},
            ).start()

    early = 128 * last
    for step in range(1, ring + 1):
        gather.step(step)
        if step % 2 == 0:
            product(step // 2 - 1)
            if step // 2 == last:
                spread(0, early, first_parts, 0)
        elif last and step == ring - 1:
            total(0, early, first_parts, 0)
    spread(early, 128, last_parts, 2)
    total(early, 128, last_parts, 2)
    if last:
        await_bytes(first_parts.at[pl.ds(1, peers - 1)], p_recv.at[1])
    await_bytes(last_parts.at[pl.ds(1, peers - 1)], p_recv.at[3])
    for n in range(chips):
        place = pl.ds(pl.multiple_of(32 * here.chip(offset_of(n)), 32), 32)
        pt[place, :] = arrived[32 * n : 32 * n + 32, :]

    def right_product(g):
        chipped = [here.chip(offset_of(n)) for n in range(4 * g, 4 * g + 4)]
        p = split(arrived[128 * g : 128 * g + 128, :])
        for at, width in tiles:
            b = (bsplit[0, :, at : at + width], bsplit[1, :, at : at + width])
            r = dot3(p, b, NN)
            for n, i in enumerate(chipped):
                place = pl.ds(pl.multiple_of(32 * i, 32), 32)
                rpart[place, at : at + width] = r[32 * n : 32 * n + 32, :]
        for n, i in enumerate(chipped):
            remote(
                rows16(rpart, i, 1 - here.c),
                rpair.at[4 * g + n],
                pair_send,
                pair_recv.at[g],
                here.partner(),
            ).start()

    def right_own(n, sub):
        chip = here.chip(offset_of(n))
        return rows16(rpart, chip, here.c, sub)[...] + rpair[n, 8 * sub : 8 * sub + 8, :]

    def scatter(k):
        if k % 2 == 0:
            g = k // 2 - 1
            await_bytes(rpair.at[pl.ds(4 * g, 4)], pair_recv.at[g])
        for sub in (0, 1):
            for way in (0, 1):
                if k == ring and sub != way:
                    continue
                place = moving.at[way, k, pl.ds(8 * sub, 8)]
                n = 2 * k - 1 if (way == 0 or k == ring) else 2 * k
                if k < ring - 1 or (k == ring - 1 and sub == way):
                    await_bytes(place, rs_recv.at[way, k, sub])
                    place[...] = place[...] + right_own(n, sub)
                else:
                    place[...] = right_own(n, sub)
                remote(
                    place,
                    moving.at[way, k - 1, pl.ds(8 * sub, 8)],
                    rs_send,
                    rs_recv.at[way, k - 1, sub],
                    here.at(1 - 2 * way),
                ).start()

    collect = Gather(here, rall, ag_send, ag_recv, ag_pair)

    def settle():
        for sub in (0, 1):
            for way in (0, 1):
                place = moving.at[way, 0, pl.ds(8 * sub, 8)]
                await_bytes(place, rs_recv.at[way, 0, sub])
            rows16(rall, here.z, here.c, sub)[...] = (
                right_own(0, sub)
                + moving[0, 0, 8 * sub : 8 * sub + 8, :]
                + moving[1, 0, 8 * sub : 8 * sub + 8, :]
            )
        collect.begin()

    def halve(n):
        collect.shared(n)
        place = pl.ds(pl.multiple_of(32 * here.chip(offset_of(n)), 32), 32)
        rsplit[0, place, :], rsplit[1, place, :] = split(rall[place, :])

    def onward(step):
        collect.step(step)
        if step == 1:
            halve(0)
        else:
            halve(2 * step - 3)
            halve(2 * step - 2)

    events = []
    for g in range(last, -1, -1):
        events.append(functools.partial(right_product, g))
        events.append(functools.partial(scatter, 2 * g + 2))
        events.append(functools.partial(scatter, 2 * g + 1))
    events.append(settle)
    events += [functools.partial(onward, step) for step in range(1, ring + 1)]
    events.reverse()

    def advance(count=1):
        for _ in range(count):
            if events:
                events.pop()()

    advance()
    block = rank // peers
    half = block // 2
    each = half // chips
    mine = pl.ds(pl.multiple_of(block * here.t, block), block)
    gpart[...] = dot(pt[mine, :], pt[...], NT, HIGHEST)
    theirs = pl.ds(pl.multiple_of(half * (1 - here.c), half), half)
    keep = pl.ds(pl.multiple_of(half * here.c, half), half)
    pair = remote(gpart.at[theirs], gpair, g_send.at[0], g_recv.at[0], here.partner())
    pair.start()
    advance()
    psplit[0], psplit[1] = split(pt[...].T)
    pair.wait()
    chip_sum = gpart[keep, :] + gpair[...]
    for k in range(chips):
        gsplit[k] = chip_sum[each * k : each * (k + 1), :]

    @pl.loop(1, chips)
    def _(k):
        remote(
            gsplit.at[here.chip(k)],
            gsplits.at[k],
            g_send.at[1],
            g_recv.at[1],
            here.at(k),
        ).start()

    advance(2)
    gsplits[0] = gsplit[here.z]
    await_bytes(gsplits.at[pl.ds(1, chips - 1)], g_recv.at[1])
    gsums[here.z] = jnp.sum(gsplits[...], axis=0)

    @pl.loop(1, chips)
    def _(k):
        place = gsums.at[here.z]
        remote(place, place, g_send.at[2], g_recv.at[2], here.at(k)).start()

    advance(2)
    await_bytes(gsums.at[pl.ds(0, chips - 1)], g_recv.at[2])
    gram[here.t, here.c] = gsums[...].reshape(half, rank)

    @pl.loop(1, peers)
    def _(k):
        place = gram.at[here.t, here.c]
        remote(
            place, place, g_send.at[3], g_recv.at[3], {"tensor": here.peer(k)}
        ).start()

    advance(2)
    await_bytes(gram.at[pl.ds(0, peers - 1), 0], g_recv.at[3])
    halves = gram.at[:, here.c]
    pair = remote(halves, halves, g_send.at[4], g_recv.at[4], here.partner())
    pair.start()
    advance()
    pair.wait()
    a_ref[...] = gram[...].reshape(rank, rank)

    def after(rows):
        wsplit[0, rows, :], wsplit[1, rows, :] = split(w_ref[rows, :])

    invert_factor(a_ref, w_ref, advance, after)
    advance(len(events))
    halve(chips - 1)

    await_bytes(rpart.at[pl.ds(0, rank // 2)], pair_send)
    sums = jnp.zeros((rank, 128), jnp.float32)
    for at, width in tiles:
        columns = slice(at, at + width)
        blocks = []
        for row in range(0, rank, 128):
            stop = row + 128
            blocks.append(
                dot3(
                    (wsplit[0, row:stop, 0:stop], wsplit[1, row:stop, 0:stop]),
                    (rsplit[0, 0:stop, columns], rsplit[1, 0:stop, columns]),
                    NN,
                )
            )
        right = jnp.concatenate(blocks, axis=0)
        rpart[:, columns] = right
        for lane in range(0, width, 128):
            one = right[:, lane : lane + 128]
            sums = sums + one * one
        rsplit[0, :, columns], rsplit[1, :, columns] = split(right)
    squares[0] = jnp.sum(sums.T, axis=0, keepdims=True)

    @pl.loop(1, peers)
    def _(k):
        remote(
            squares.at[0], squares.at[k], sq_send, sq_recv, {"tensor": here.peer(k)}
        ).start()

    q = dot3((psplit[0], psplit[1]), (wsplit[0], wsplit[1]), NT)
    q1 = (q * -0.05).astype(jnp.bfloat16)
    for at, width in tiles:
        columns = slice(at, at + width)
        momentum_ref[:, columns] = b_ref[:, columns] + dot(
            q1, rsplit[0, :, columns], NN, None
        )
    await_bytes(squares.at[pl.ds(1, peers - 1)], sq_recv)
    scales = lax.rsqrt(jnp.sum(squares[...], axis=0) * mean + 1e-06)
    scaled = split(q * (scales * gain))
    for at, width in tiles:
        columns = slice(at, at + width)
        update_ref[:, columns] = dot3(
            scaled, (rsplit[0, :, columns], rsplit[1, :, columns]), NN
        ).astype(jnp.bfloat16)
    lanes = lax.broadcasted_iota(jnp.int32, (16, rank), 1)
    rows = lax.broadcasted_iota(jnp.int32, (16, rank), 0) + (32 * here.z + 16 * here.c)
    picked = jnp.where(lanes == rows, jnp.broadcast_to(scales, (16, rank)), 0.0)
    factor_ref[...] = rows16(rpart, here.z, here.c)[...] * jnp.sum(
        picked, axis=1, keepdims=True
    )

    gather.end()
    collect.end()
    if last:
        for turn in (0, 1):
            await_bytes(first_parts.at[pl.ds(1, peers - 1)], p_send.at[turn])
    for turn in (2, 3):
        await_bytes(last_parts.at[pl.ds(1, peers - 1)], p_send.at[turn])
    await_bytes(gsplits.at[pl.ds(1, chips - 1)], g_send.at[1])
    await_bytes(gsums.at[pl.ds(0, chips - 1)], g_send.at[2])
    await_bytes(gram.at[pl.ds(0, peers - 1), 0], g_send.at[3])
    await_bytes(rall.at[pl.ds(0, 16 * (chips - 1))], rs_send)
    await_bytes(squares.at[pl.ds(1, peers - 1)], sq_send)


def body(chips, peers, buffer, factor):
    rows, columns = buffer.shape
    rank = 32 * chips
    half = rank // peers // 2
    each = half // chips
    total_columns = columns * peers
    groups = chips // 4
    ring = chips // 2
    f32, bf16 = jnp.float32, jnp.bfloat16
    dma = pltpu.SemaphoreType.DMA
    vmem = pl.BlockSpec(memory_space=pltpu.VMEM)
    momentum, update, factor_t = pl.pallas_call(
        functools.partial(
            kernel,
            chips,
            peers,
            1.0 / math.sqrt(total_columns),
            1.0 / total_columns,
            math.sqrt(rows * 2 * chips / rank),
        ),
        out_shape=(
            jax.ShapeDtypeStruct((rows, columns), f32),
            jax.ShapeDtypeStruct((rows, columns), bf16),
            jax.ShapeDtypeStruct((16, columns), f32),
        ),
        in_specs=[vmem] * 2,
        out_specs=(vmem,) * 3,
        scratch_shapes=[
            pltpu.VMEM((2, rows, columns), bf16),
            pltpu.VMEM((rank, columns), f32),
            pltpu.VMEM((rank, rows), f32),
            pltpu.VMEM((peers, max(groups - 1, 1) * 128 // peers, rows), f32),
            pltpu.VMEM((peers, 128 // peers, rows), f32),
            pltpu.VMEM((rank, rows), f32),
            pltpu.VMEM((rank, rows), f32),
            pltpu.VMEM((2, rows, rank), bf16),
            pltpu.VMEM((2 * half, rank), f32),
            pltpu.VMEM((half, rank), f32),
            pltpu.VMEM((chips, each, rank), f32),
            pltpu.VMEM((chips, each, rank), f32),
            pltpu.VMEM((chips, each, rank), f32),
            pltpu.VMEM((peers, 2, half, rank), f32),
            pltpu.VMEM((rank, rank), f32),
            pltpu.VMEM((rank, rank), f32),
            pltpu.VMEM((2, rank, rank), bf16),
            pltpu.VMEM((rank, columns), f32),
            pltpu.VMEM((chips, 16, columns), f32),
            pltpu.VMEM((2, ring + 1, 16, columns), f32),
            pltpu.VMEM((rank, columns), f32),
            pltpu.VMEM((2, rank, columns), bf16),
            pltpu.VMEM((peers, 1, rank), f32),
            dma,
            dma((2, ring, 2)),
            dma((chips,)),
            dma((4,)),
            dma((4,)),
            dma((5,)),
            dma((5,)),
            dma,
            dma((groups,)),
            dma,
            dma((2, ring, 2)),
            dma,
            dma((2, ring, 2)),
            dma((chips,)),
            dma,
            dma,
        ],
        compiler_params=pltpu.CompilerParams(
            collective_id=0, has_side_effects=True, vmem_limit_bytes=LIMIT
        ),
        name="low_rank_update",
    )(buffer, factor.T)
    return momentum, update, factor_t.T


def solution(mesh):
    chips, peers = mesh.shape["dp"] // 2, mesh.shape["tensor"]
    placed = (P("dp", "tensor"), P("tensor", "dp"))
    return jax.shard_map(
        functools.partial(body, chips, peers),
        mesh=mesh,
        in_specs=placed,
        out_specs=(P("dp", "tensor"), P("dp", "tensor"), P("tensor", "dp")),
        check_vma=False,
    )
```

```python
import functools
import math

import jax
import jax.numpy as jnp
from jax import lax
from jax.experimental import pallas as pl
from jax.experimental.pallas import tpu as pltpu
from jax.sharding import PartitionSpec as P

MESH = pl.DeviceIdType.MESH
HIGHEST = lax.Precision.HIGHEST
NN = (((1,), (0,)), ((), ()))
LIMIT = 56 * 1024 * 1024


def dot(a, b, dims, precision):
    return lax.dot_general(
        a, b, dims, precision=precision, preferred_element_type=jnp.float32
    )


class Place:
    def __init__(self, chips, peers):
        dp = lax.axis_index("dp")
        self.z, self.c = dp // 2, dp % 2
        self.t = lax.axis_index("tensor")
        self.chips, self.peers = chips, peers

    def chip(self, offset):
        return lax.rem(self.z + offset + self.chips, self.chips)

    def at(self, offset):
        return {"dp": 2 * self.chip(offset) + self.c}

    def partner(self):
        return {"dp": 2 * self.z + 1 - self.c}

    def peer(self, k):
        return lax.rem(self.t + k, self.peers)


def remote(src, dst, send, recv, device):
    return pltpu.make_async_remote_copy(
        src_ref=src,
        dst_ref=dst,
        send_sem=send,
        recv_sem=recv,
        device_id=device,
        device_id_type=MESH,
    )


def await_bytes(ref, sem):
    pltpu.make_async_copy(ref, ref, sem).wait()


def enter(here, ring):
    barrier = pltpu.get_barrier_semaphore()

    def greet(device):
        pl.semaphore_signal(barrier, inc=1, device_id=device, device_id_type=MESH)

    @pl.loop(1, here.peers)
    def _(k):
        greet({"tensor": here.peer(k)})

    greet(here.partner())
    if ring:

        @pl.loop(1, here.chips)
        def _(k):
            greet(here.at(k))

        count = here.chips - 1
    else:
        greet(here.at(1))
        greet(here.at(-1))
        count = 2
    pl.semaphore_wait(barrier, here.peers - 1 + 1 + count)


def offset_of(n):
    return ((n + 1) // 2) * (2 * (n % 2) - 1)


def rows16(ref, chip, core, sub=None):
    start = 32 * chip + 16 * core
    if sub is None:
        return ref.at[pl.ds(pl.multiple_of(start, 16), 16)]
    return ref.at[pl.ds(pl.multiple_of(start + 8 * sub, 8), 8)]


class Gather:
    def __init__(self, here, buf, send, recv, pair_recv):
        self.here, self.buf = here, buf
        self.send, self.recv, self.pair_recv = send, recv, pair_recv
        self.half = here.chips // 2

    def subs(self, step, way):
        if step < self.half:
            return (0, 1)
        return (way,) if step == self.half else ()

    def forward(self, step, way, sub):
        here, sign = self.here, 1 - 2 * way
        ref = rows16(self.buf, here.chip(-sign * (step - 1)), here.c, sub)
        remote(
            ref, ref, self.send, self.recv.at[way, step - 1, sub], here.at(sign)
        ).start()

    def share(self, offset, slot):
        here = self.here
        ref = rows16(self.buf, here.chip(offset), here.c)
        remote(ref, ref, self.send, self.pair_recv.at[slot], here.partner()).start()

    def begin(self):
        for sub in (0, 1):
            for way in (0, 1):
                self.forward(1, way, sub)
        self.share(0, 0)

    def step(self, step):
        here = self.here
        for sub in (0, 1):
            for way in (0, 1):
                if sub in self.subs(step, way):
                    sign = 1 - 2 * way
                    ref = rows16(self.buf, here.chip(-sign * step), here.c, sub)
                    await_bytes(ref, self.recv.at[way, step - 1, sub])
                    if sub in self.subs(step + 1, way):
                        self.forward(step + 1, way, sub)
        if step < self.half:
            self.share(step, 2 * step - 1)
            self.share(-step, 2 * step)
        else:
            self.share(step, 2 * step - 1)

    def shared(self, n):
        here = self.here
        ref = rows16(self.buf, here.chip(offset_of(n)), 1 - here.c)
        await_bytes(ref, self.pair_recv.at[n])

    def end(self):
        rows = 16 * (2 * self.here.chips - 1)
        await_bytes(self.buf.at[pl.ds(0, rows)], self.send)


def split(value):
    high = value.astype(jnp.bfloat16)
    return high, (value - high.astype(jnp.float32)).astype(jnp.bfloat16)


def dot3(a, b, dims):
    return (
        dot(a[0], b[0], dims, None) + dot(a[0], b[1], dims, None)
    ) + dot(a[1], b[0], dims, None)


def splat(value):
    return jnp.broadcast_to(value, (8, 128))


def eliminate(turn, carry, w_ref):
    s = carry
    lane = lax.broadcasted_iota(jnp.int32, (8, 128), 1)
    sublane = lax.broadcasted_iota(jnp.int32, (8, 128), 0)
    for half in (0, 8):
        block = (lane >= half) & (lane < half + 8)
        columns = [
            jnp.broadcast_to(s[:, half + j : half + j + 1], s.shape) for j in range(8)
        ]
        d = {
            (i, j): splat(columns[j][i : i + 1, :]) for j in range(8) for i in range(j, 8)
        }
        top = jnp.where(block, jnp.where(lane == sublane + half, 1.0, 0.0), s[0:8])
        r = [splat(top[i : i + 1, :]) for i in range(8)]
        root, inverse, t = [], [], {}
        for k in range(8):
            root.append(lax.rsqrt(d[k, k]))
            inverse.append(root[k] * root[k])
            for i in range(k + 1, 8):
                t[i, k] = d[i, k] * inverse[k]
                for j in range(k + 1, i + 1):
                    d[i, j] = d[i, j] - t[i, k] * d[j, k]
                r[i] = r[i] - t[i, k] * r[k]
        done = r[0] * root[0]
        for k in range(1, 8):
            done = jnp.where(sublane == k, r[k] * root[k], done)
        keep = (lane >= 128 - 16 * turn) | (lane < half + 8)
        w_ref[pl.ds(pl.multiple_of(16 * turn + half, 8), 8), :] = jnp.where(
            keep, done, 0.0
        )
        for k in range(7, -1, -1):
            r[k] = r[k] * inverse[k]
            for i in range(7, k, -1):
                r[k] = r[k] - t[i, k] * r[i]
        lanes = lax.broadcasted_iota(jnp.int32, (s.shape[0] - 8, 128), 1)
        s = jnp.where((lanes >= half) & (lanes < half + 8), 0.0, s[8:])
        for j in range(8):
            s = s - columns[j][8:] * r[j][0:1, :]
    blank = jnp.zeros((16, 128), jnp.float32)
    return pltpu.roll(jnp.concatenate([s, blank], axis=0), 112, 1)


def invert_factor(m_ref, block_ref, between, after):
    rank = m_ref.shape[0]
    for start in range(0, rank, 128):
        stop = start + 128
        here = slice(start, stop)
        carry = m_ref[here, here]
        for quarter in range(4):
            carry = lax.fori_loop(
                2 * quarter,
                2 * quarter + 2,
                functools.partial(eliminate, w_ref=block_ref),
                carry,
            )
            between()
        w = [
            pltpu.roll(block_ref[16 * i : 16 * i + 16, :], 16 * i, 1) if i else block_ref[0:16, :]
            for i in range(8)
        ]
        w = jnp.concatenate(w, axis=0)
        if rank > 128:
            m_ref[here, :] = dot(w, m_ref[here, :], NN, HIGHEST)
        m_ref[here, here] = w
        if stop < rank:
            below = slice(stop, rank)
            lower = m_ref[here, below].T
            m_ref[below, here] = jnp.zeros((rank - stop, 128), jnp.float32)
            m_ref[below, :] = m_ref[below, :] - dot(lower, m_ref[here, :], NN, HIGHEST)
        after(start, m_ref[here, 0:stop])


def column_tiles(columns):
    return [(at, min(256, columns - at)) for at in range(0, columns, 256)]


def kernel(
    chips,
    peers,
    scale,
    mean,
    gain,
    b_ref,
    f_ref,
    momentum_ref,
    update_ref,
    factor_ref,
    bsplit,
    tsplit,
    fall,
    part,
    first_parts,
    last_parts,
    arrived,
    pt,
    psplit,
    gpart,
    gpair,
    gsplit,
    gsplits,
    gsums,
    gram,
    m_ref,
    block_ref,
    wsplit,
    rpart,
    rpair,
    moving,
    rall,
    rsplit,
    squares,
    f_send,
    f_recv,
    f_pair,
    p_send,
    p_recv,
    g_send,
    g_recv,
    pair_send,
    pair_recv,
    rs_send,
    rs_recv,
    ag_send,
    ag_recv,
    ag_pair,
    sq_send,
    sq_recv,
):
    here = Place(chips, peers)
    rank = 32 * chips
    ring = chips // 2
    groups = chips // 4
    last = groups - 1
    tiles = column_tiles(b_ref.shape[1])
    own = rows16(fall, here.z, here.c)
    own[...] = f_ref[...]
    enter(here, True)
    gather = Gather(here, fall, f_send, f_recv, f_pair)
    gather.begin()
    tsplit[0], tsplit[1] = split(b_ref[...].T)
    bsplit[0], bsplit[1] = split(b_ref[...])

    def product(g):
        for n in range(4 * g, 4 * g + 4):
            gather.shared(n)
        rows = [
            fall[pl.ds(pl.multiple_of(32 * here.chip(offset_of(n)), 32), 32), :]
            for n in range(4 * g, 4 * g + 4)
        ]
        f = split(jnp.concatenate(rows, axis=0))
        part[128 * g : 128 * g + 128, :] = dot3(f, (tsplit[0], tsplit[1]), NN)

    def spread(base, rows, parts, turn):
        piece = rows // peers

        @pl.loop(1, peers)
        def _(k):
            other = here.peer(k)
            start = pl.multiple_of(base + piece * other, 8)
            remote(
                part.at[pl.ds(start, piece)],
                parts.at[k],
                p_send.at[turn],
                p_recv.at[turn],
                {"tensor": other},
            ).start()

    def total(base, rows, parts, turn):
        piece = rows // peers
        mine = pl.ds(pl.multiple_of(base + piece * here.t, 8), piece)
        parts[0] = part[mine, :]
        await_bytes(parts.at[pl.ds(1, peers - 1)], p_recv.at[turn])
        arrived[mine, :] = jnp.sum(parts[...], axis=0) * scale

        @pl.loop(1, peers)
        def _(k):
            place = arrived.at[mine]
            remote(
                place,
                place,
                p_send.at[turn + 1],
                p_recv.at[turn + 1],
                {"tensor": here.peer(k)},
            ).start()

    early = 128 * last
    for step in range(1, ring + 1):
        gather.step(step)
        if step % 2 == 0:
            product(step // 2 - 1)
            if step // 2 == last:
                spread(0, early, first_parts, 0)
        elif last and step == ring - 1:
            total(0, early, first_parts, 0)
    spread(early, 128, last_parts, 2)
    total(early, 128, last_parts, 2)
    if last:
        await_bytes(first_parts.at[pl.ds(1, peers - 1)], p_recv.at[1])
    await_bytes(last_parts.at[pl.ds(1, peers - 1)], p_recv.at[3])
    for n in range(chips):
        place = pl.ds(pl.multiple_of(32 * here.chip(offset_of(n)), 32), 32)
        pt[place, :] = arrived[32 * n : 32 * n + 32, :]

    def right_product(g):
        chipped = [here.chip(offset_of(n)) for n in range(4 * g, 4 * g + 4)]
        p = split(arrived[128 * g : 128 * g + 128, :])
        for at, width in tiles:
            b = (bsplit[0, :, at : at + width], bsplit[1, :, at : at + width])
            r = dot3(p, b, NN)
            for n, i in enumerate(chipped):
                place = pl.ds(pl.multiple_of(32 * i, 32), 32)
                rpart[place, at : at + width] = r[32 * n : 32 * n + 32, :]
        for n, i in enumerate(chipped):
            remote(
                rows16(rpart, i, 1 - here.c),
                rpair.at[4 * g + n],
                pair_send,
                pair_recv.at[g],
                here.partner(),
            ).start()

    def right_own(n, sub):
        chip = here.chip(offset_of(n))
        return rows16(rpart, chip, here.c, sub)[...] + rpair[n, 8 * sub : 8 * sub + 8, :]

    def scatter(k):
        if k % 2 == 0:
            g = k // 2 - 1
            await_bytes(rpair.at[pl.ds(4 * g, 4)], pair_recv.at[g])
        for sub in (0, 1):
            for way in (0, 1):
                if k == ring and sub != way:
                    continue
                place = moving.at[way, k, pl.ds(8 * sub, 8)]
                n = 2 * k - 1 if (way == 0 or k == ring) else 2 * k
                if k < ring - 1 or (k == ring - 1 and sub == way):
                    await_bytes(place, rs_recv.at[way, k, sub])
                    place[...] = place[...] + right_own(n, sub)
                else:
                    place[...] = right_own(n, sub)
                remote(
                    place,
                    moving.at[way, k - 1, pl.ds(8 * sub, 8)],
                    rs_send,
                    rs_recv.at[way, k - 1, sub],
                    here.at(1 - 2 * way),
                ).start()

    collect = Gather(here, rall, ag_send, ag_recv, ag_pair)

    def settle():
        for sub in (0, 1):
            for way in (0, 1):
                place = moving.at[way, 0, pl.ds(8 * sub, 8)]
                await_bytes(place, rs_recv.at[way, 0, sub])
            rows16(rall, here.z, here.c, sub)[...] = (
                right_own(0, sub)
                + moving[0, 0, 8 * sub : 8 * sub + 8, :]
                + moving[1, 0, 8 * sub : 8 * sub + 8, :]
            )
        collect.begin()

    def halve(n):
        collect.shared(n)
        place = pl.ds(pl.multiple_of(32 * here.chip(offset_of(n)), 32), 32)
        rsplit[0, place, :], rsplit[1, place, :] = split(rall[place, :])

    def onward(step):
        collect.step(step)
        if step == 1:
            halve(0)
        else:
            halve(2 * step - 3)
            halve(2 * step - 2)

    events = []
    for g in range(last, -1, -1):
        events.append(functools.partial(right_product, g))
        events.append(functools.partial(scatter, 2 * g + 2))
        events.append(functools.partial(scatter, 2 * g + 1))
    events.append(settle)
    events += [functools.partial(onward, step) for step in range(1, ring + 1)]
    events.reverse()

    def advance(count=1):
        for _ in range(count):
            if events:
                events.pop()()

    advance()
    block = rank // peers
    half = block // 2
    each = half // chips
    mine = pl.ds(pl.multiple_of(block * here.t, block), block)
    gpart[...] = dot(pt[mine, :], pt[...].T, NN, HIGHEST)
    theirs = pl.ds(pl.multiple_of(half * (1 - here.c), half), half)
    keep = pl.ds(pl.multiple_of(half * here.c, half), half)
    pair = remote(gpart.at[theirs], gpair, g_send.at[0], g_recv.at[0], here.partner())
    pair.start()
    advance()
    psplit[0], psplit[1] = split(pt[...])
    pair.wait()
    chip_sum = gpart[keep, :] + gpair[...]
    for k in range(chips):
        gsplit[k] = chip_sum[each * k : each * (k + 1), :]

    @pl.loop(1, chips)
    def _(k):
        remote(
            gsplit.at[here.chip(k)],
            gsplits.at[k],
            g_send.at[1],
            g_recv.at[1],
            here.at(k),
        ).start()

    advance(2)
    gsplits[0] = gsplit[here.z]
    await_bytes(gsplits.at[pl.ds(1, chips - 1)], g_recv.at[1])
    gsums[here.z] = jnp.sum(gsplits[...], axis=0)

    @pl.loop(1, chips)
    def _(k):
        place = gsums.at[here.z]
        remote(place, place, g_send.at[2], g_recv.at[2], here.at(k)).start()

    advance(2)
    await_bytes(gsums.at[pl.ds(0, chips - 1)], g_recv.at[2])
    gram[here.t, here.c] = gsums[...].reshape(half, rank)

    @pl.loop(1, peers)
    def _(k):
        place = gram.at[here.t, here.c]
        remote(
            place, place, g_send.at[3], g_recv.at[3], {"tensor": here.peer(k)}
        ).start()

    advance(2)
    await_bytes(gram.at[pl.ds(0, peers - 1), 0], g_recv.at[3])
    halves = gram.at[:, here.c]
    pair = remote(halves, halves, g_send.at[4], g_recv.at[4], here.partner())
    pair.start()
    advance()
    pair.wait()
    m_ref[...] = gram[...].reshape(rank, rank)
    wsplit[...] = jnp.zeros_like(wsplit)

    def after(start, w):
        rows, columns = slice(start, start + 128), slice(0, start + 128)
        wsplit[0, rows, columns], wsplit[1, rows, columns] = split(w)

    invert_factor(m_ref, block_ref, advance, after)
    advance(len(events))
    halve(chips - 1)

    await_bytes(rpart.at[pl.ds(0, rank // 2)], pair_send)
    sums = jnp.zeros((rank, 128), jnp.float32)
    for at, width in tiles:
        columns = slice(at, at + width)
        blocks = []
        for row in range(0, rank, 256):
            stop = row + 256
            blocks.append(
                dot3(
                    (wsplit[0, row:stop, 0:stop], wsplit[1, row:stop, 0:stop]),
                    (rsplit[0, 0:stop, columns], rsplit[1, 0:stop, columns]),
                    NN,
                )
            )
        right = jnp.concatenate(blocks, axis=0)
        rpart[:, columns] = right
        for lane in range(0, width, 128):
            one = right[:, lane : lane + 128]
            sums = sums + one * one
        rsplit[0, :, columns], rsplit[1, :, columns] = split(right)
    squares[0] = jnp.sum(sums.T, axis=0, keepdims=True)

    @pl.loop(1, peers)
    def _(k):
        remote(
            squares.at[0], squares.at[k], sq_send, sq_recv, {"tensor": here.peer(k)}
        ).start()

    blocks = []
    for row in range(0, rank, 256):
        stop = row + 256
        blocks.append(
            dot3(
                (wsplit[0, row:stop, 0:stop], wsplit[1, row:stop, 0:stop]),
                (psplit[0, 0:stop, :], psplit[1, 0:stop, :]),
                NN,
            )
        )
    q = jnp.concatenate(blocks, axis=0).T
    q1 = (q * -0.05).astype(jnp.bfloat16)
    for at, width in tiles:
        columns = slice(at, at + width)
        momentum_ref[:, columns] = b_ref[:, columns] + dot(
            q1, rsplit[0, :, columns], NN, None
        )
    await_bytes(squares.at[pl.ds(1, peers - 1)], sq_recv)
    scales = lax.rsqrt(jnp.sum(squares[...], axis=0) * mean + 1e-06)
    scaled = split(q * (scales * gain))
    for at, width in tiles:
        columns = slice(at, at + width)
        update_ref[:, columns] = dot3(
            scaled, (rsplit[0, :, columns], rsplit[1, :, columns]), NN
        ).astype(jnp.bfloat16)
    lanes = lax.broadcasted_iota(jnp.int32, (16, rank), 1)
    rows = lax.broadcasted_iota(jnp.int32, (16, rank), 0) + (32 * here.z + 16 * here.c)
    picked = jnp.where(lanes == rows, jnp.broadcast_to(scales, (16, rank)), 0.0)
    factor_ref[...] = rows16(rpart, here.z, here.c)[...] * jnp.sum(
        picked, axis=1, keepdims=True
    )

    gather.end()
    collect.end()
    if last:
        for turn in (0, 1):
            await_bytes(first_parts.at[pl.ds(1, peers - 1)], p_send.at[turn])
    for turn in (2, 3):
        await_bytes(last_parts.at[pl.ds(1, peers - 1)], p_send.at[turn])
    await_bytes(gsplits.at[pl.ds(1, chips - 1)], g_send.at[1])
    await_bytes(gsums.at[pl.ds(0, chips - 1)], g_send.at[2])
    await_bytes(gram.at[pl.ds(0, peers - 1), 0], g_send.at[3])
    await_bytes(rall.at[pl.ds(0, 16 * (chips - 1))], rs_send)
    await_bytes(squares.at[pl.ds(1, peers - 1)], sq_send)


def body(chips, peers, buffer, factor):
    rows, columns = buffer.shape
    rank = 32 * chips
    half = rank // peers // 2
    each = half // chips
    total_columns = columns * peers
    groups = chips // 4
    ring = chips // 2
    f32, bf16 = jnp.float32, jnp.bfloat16
    dma = pltpu.SemaphoreType.DMA
    vmem = pl.BlockSpec(memory_space=pltpu.VMEM)
    momentum, update, factor_t = pl.pallas_call(
        functools.partial(
            kernel,
            chips,
            peers,
            1.0 / math.sqrt(total_columns),
            1.0 / total_columns,
            math.sqrt(rows * 2 * chips / rank),
        ),
        out_shape=(
            jax.ShapeDtypeStruct((rows, columns), f32),
            jax.ShapeDtypeStruct((rows, columns), bf16),
            jax.ShapeDtypeStruct((16, columns), f32),
        ),
        in_specs=[vmem] * 2,
        out_specs=(vmem,) * 3,
        scratch_shapes=[
            pltpu.VMEM((2, rows, columns), bf16),
            pltpu.VMEM((2, columns, rows), bf16),
            pltpu.VMEM((rank, columns), f32),
            pltpu.VMEM((rank, rows), f32),
            pltpu.VMEM((peers, max(groups - 1, 1) * 128 // peers, rows), f32),
            pltpu.VMEM((peers, 128 // peers, rows), f32),
            pltpu.VMEM((rank, rows), f32),
            pltpu.VMEM((rank, rows), f32),
            pltpu.VMEM((2, rank, rows), bf16),
            pltpu.VMEM((2 * half, rank), f32),
            pltpu.VMEM((half, rank), f32),
            pltpu.VMEM((chips, each, rank), f32),
            pltpu.VMEM((chips, each, rank), f32),
            pltpu.VMEM((chips, each, rank), f32),
            pltpu.VMEM((peers, 2, half, rank), f32),
            pltpu.VMEM((rank, rank), f32),
            pltpu.VMEM((128, 128), f32),
            pltpu.VMEM((2, rank, rank), bf16),
            pltpu.VMEM((rank, columns), f32),
            pltpu.VMEM((chips, 16, columns), f32),
            pltpu.VMEM((2, ring + 1, 16, columns), f32),
            pltpu.VMEM((rank, columns), f32),
            pltpu.VMEM((2, rank, columns), bf16),
            pltpu.VMEM((peers, 1, rank), f32),
            dma,
            dma((2, ring, 2)),
            dma((chips,)),
            dma((4,)),
            dma((4,)),
            dma((5,)),
            dma((5,)),
            dma,
            dma((groups,)),
            dma,
            dma((2, ring, 2)),
            dma,
            dma((2, ring, 2)),
            dma((chips,)),
            dma,
            dma,
        ],
        compiler_params=pltpu.CompilerParams(
            collective_id=0, has_side_effects=True, vmem_limit_bytes=LIMIT
        ),
        name="low_rank_update",
    )(buffer, factor.T)
    return momentum, update, factor_t.T


def solution(mesh):
    chips, peers = mesh.shape["dp"] // 2, mesh.shape["tensor"]
    placed = (P("dp", "tensor"), P("tensor", "dp"))
    return jax.shard_map(
        functools.partial(body, chips, peers),
        mesh=mesh,
        in_specs=placed,
        out_specs=(P("dp", "tensor"), P("dp", "tensor"), P("tensor", "dp")),
        check_vma=False,
    )
```

```python
import functools
import math

import jax
import jax.numpy as jnp
from jax import lax
from jax.experimental import pallas as pl
from jax.experimental.pallas import tpu as pltpu
from jax.sharding import PartitionSpec as P

MESH = pl.DeviceIdType.MESH
HIGHEST = lax.Precision.HIGHEST
NN = (((1,), (0,)), ((), ()))
LIMIT = 56 * 1024 * 1024


def dot(a, b, dims, precision):
    return lax.dot_general(
        a, b, dims, precision=precision, preferred_element_type=jnp.float32
    )


class Place:
    def __init__(self, chips, peers):
        dp = lax.axis_index("dp")
        self.z, self.c = dp // 2, dp % 2
        self.t = lax.axis_index("tensor")
        self.chips, self.peers = chips, peers

    def chip(self, offset):
        return lax.rem(self.z + offset + self.chips, self.chips)

    def at(self, offset):
        return {"dp": 2 * self.chip(offset) + self.c}

    def partner(self):
        return {"dp": 2 * self.z + 1 - self.c}

    def peer(self, k):
        return lax.rem(self.t + k, self.peers)


def remote(src, dst, send, recv, device):
    return pltpu.make_async_remote_copy(
        src_ref=src,
        dst_ref=dst,
        send_sem=send,
        recv_sem=recv,
        device_id=device,
        device_id_type=MESH,
    )


def await_bytes(ref, sem):
    pltpu.make_async_copy(ref, ref, sem).wait()


def enter(here, ring):
    barrier = pltpu.get_barrier_semaphore()

    def greet(device):
        pl.semaphore_signal(barrier, inc=1, device_id=device, device_id_type=MESH)

    @pl.loop(1, here.peers)
    def _(k):
        greet({"tensor": here.peer(k)})

    greet(here.partner())
    if ring:

        @pl.loop(1, here.chips)
        def _(k):
            greet(here.at(k))

        count = here.chips - 1
    else:
        greet(here.at(1))
        greet(here.at(-1))
        count = 2
    pl.semaphore_wait(barrier, here.peers - 1 + 1 + count)


def offset_of(n):
    return ((n + 1) // 2) * (2 * (n % 2) - 1)


def rows16(ref, chip, core, sub=None):
    start = 32 * chip + 16 * core
    if sub is None:
        return ref.at[pl.ds(pl.multiple_of(start, 16), 16)]
    return ref.at[pl.ds(pl.multiple_of(start + 8 * sub, 8), 8)]


class Gather:
    def __init__(self, here, buf, send, recv, pair_recv):
        self.here, self.buf = here, buf
        self.send, self.recv, self.pair_recv = send, recv, pair_recv
        self.half = here.chips // 2

    def subs(self, step, way):
        if step < self.half:
            return (0, 1)
        return (way,) if step == self.half else ()

    def forward(self, step, way, sub):
        here, sign = self.here, 1 - 2 * way
        ref = rows16(self.buf, here.chip(-sign * (step - 1)), here.c, sub)
        remote(
            ref, ref, self.send, self.recv.at[way, step - 1, sub], here.at(sign)
        ).start()

    def share(self, offset, slot):
        here = self.here
        ref = rows16(self.buf, here.chip(offset), here.c)
        remote(ref, ref, self.send, self.pair_recv.at[slot], here.partner()).start()

    def begin(self):
        for sub in (0, 1):
            for way in (0, 1):
                self.forward(1, way, sub)
        self.share(0, 0)

    def step(self, step, sub):
        here = self.here
        for way in (0, 1):
            if sub in self.subs(step, way):
                sign = 1 - 2 * way
                ref = rows16(self.buf, here.chip(-sign * step), here.c, sub)
                await_bytes(ref, self.recv.at[way, step - 1, sub])
                if sub in self.subs(step + 1, way):
                    self.forward(step + 1, way, sub)
        if sub == 1:
            self.share(step, 2 * step - 1)
            if step < self.half:
                self.share(-step, 2 * step)

    def shared(self, n):
        here = self.here
        ref = rows16(self.buf, here.chip(offset_of(n)), 1 - here.c)
        await_bytes(ref, self.pair_recv.at[n])

    def end(self):
        rows = 16 * (2 * self.here.chips - 1)
        await_bytes(self.buf.at[pl.ds(0, rows)], self.send)


def split(value):
    high = value.astype(jnp.bfloat16)
    return high, (value - high.astype(jnp.float32)).astype(jnp.bfloat16)


def dot3(a, b, dims):
    return (
        dot(a[0], b[0], dims, None) + dot(a[0], b[1], dims, None)
    ) + dot(a[1], b[0], dims, None)


def splat(value):
    return jnp.broadcast_to(value, (8, 128))


def eliminate(m, s, w_ref):
    at, stop = 8 * m, 8 * m + 8
    lane = lax.broadcasted_iota(jnp.int32, (8, 128), 1)
    sublane = lax.broadcasted_iota(jnp.int32, (8, 128), 0)
    columns = [jnp.broadcast_to(s[:, at + j : at + j + 1], s.shape) for j in range(8)]
    d = {(i, j): splat(columns[j][i : i + 1, :]) for j in range(8) for i in range(j, 8)}
    block = (lane >= at) & (lane < stop)
    top = jnp.where(block, jnp.where(lane == sublane + at, 1.0, 0.0), s[0:8])
    r = [splat(top[i : i + 1, :]) for i in range(8)]
    root, inverse, t = [], [], {}
    for k in range(8):
        root.append(lax.rsqrt(d[k, k]))
        inverse.append(root[k] * root[k])
        for i in range(k + 1, 8):
            t[i, k] = d[i, k] * inverse[k]
            for j in range(k + 1, i + 1):
                d[i, j] = d[i, j] - t[i, k] * d[j, k]
            r[i] = r[i] - t[i, k] * r[k]
    done = r[0] * root[0]
    for k in range(1, 8):
        done = jnp.where(sublane == k, r[k] * root[k], done)
    w_ref[at:stop, :] = jnp.where(lane < stop, done, 0.0)
    if m == 15:
        return None
    for k in range(7, -1, -1):
        r[k] = r[k] * inverse[k]
        for i in range(7, k, -1):
            r[k] = r[k] - t[i, k] * r[i]
    lanes = lax.broadcasted_iota(jnp.int32, (s.shape[0] - 8, 128), 1)
    s = jnp.where((lanes >= at) & (lanes < stop), 0.0, s[8:])
    for j in range(8):
        s = s - columns[j][8:] * r[j][0:1, :]
    return s


def invert_factor(m_ref, block_ref, between, after):
    rank = m_ref.shape[0]
    late = []

    def update(rows, columns, lower, start):
        if rows.start < rows.stop and columns.start < columns.stop:
            m_ref[rows, columns] = m_ref[rows, columns] - dot(
                lower, m_ref[start : start + 128, columns], NN, HIGHEST
            )

    for start in range(0, rank, 128):
        stop = start + 128
        here = slice(start, stop)
        s = m_ref[here, here]
        for m in range(16):
            s = eliminate(m, s, block_ref)
            if late:
                late.pop()()
            if m % 2 == 1:
                between()
        w = block_ref[...]
        if rank > 128:
            m_ref[here, :] = dot(w, m_ref[here, :], NN, HIGHEST)
        m_ref[here, here] = w
        if stop < rank:
            lower = m_ref[here, stop:rank].T
            m_ref[stop:rank, here] = jnp.zeros((rank - stop, 128), jnp.float32)
            near, far = slice(stop, stop + 128), slice(stop + 128, rank)
            update(near, near, lower[0:128], start)
            late = [
                functools.partial(update, *where, start)
                for where in (
                    (far, far, lower[128:]),
                    (far, slice(0, stop + 128), lower[128:]),
                    (near, far, lower[0:128]),
                    (near, slice(0, stop), lower[0:128]),
                )
            ]
        after(start, m_ref[here, 0:stop])


def column_tiles(columns):
    return [(at, min(256, columns - at)) for at in range(0, columns, 256)]


def kernel(
    chips,
    peers,
    scale,
    mean,
    gain,
    b_ref,
    f_ref,
    qlow_ref,
    qsplit_ref,
    rsplit,
    factor_ref,
    bsplit,
    tsplit,
    fall,
    fsplit,
    part,
    first_parts,
    last_parts,
    arrived,
    pt,
    psplit,
    gpart,
    gpair,
    gsplit,
    gsplits,
    gsums,
    gram,
    m_ref,
    block_ref,
    wsplit,
    rpart,
    rpair,
    moving,
    rall,
    squares,
    f_send,
    f_recv,
    f_pair,
    p_send,
    p_recv,
    g_send,
    g_recv,
    pair_send,
    pair_recv,
    rs_send,
    rs_recv,
    ag_send,
    ag_recv,
    ag_pair,
    sq_send,
    sq_recv,
):
    here = Place(chips, peers)
    rank = 32 * chips
    ring = chips // 2
    groups = chips // 4
    last = groups - 1
    tiles = column_tiles(b_ref.shape[1])
    own = rows16(fall, here.z, here.c)
    own[...] = f_ref[...]
    enter(here, True)
    gather = Gather(here, fall, f_send, f_recv, f_pair)
    gather.begin()

    def transpose(low, high):
        columns = slice(128 * low, min(128 * high, b_ref.shape[1]))
        tsplit[0, columns, :], tsplit[1, columns, :] = split(b_ref[:, columns].T)

    def straight(low, high):
        columns = slice(128 * low, min(128 * high, b_ref.shape[1]))
        bsplit[0, :, columns], bsplit[1, :, columns] = split(b_ref[:, columns])

    def join(g):
        for n in range(4 * g, 4 * g + 4):
            gather.shared(n)
        rows = [
            fall[pl.ds(pl.multiple_of(32 * here.chip(offset_of(n)), 32), 32), :]
            for n in range(4 * g, 4 * g + 4)
        ]
        fsplit[0], fsplit[1] = split(jnp.concatenate(rows, axis=0))

    def product(g, turn):
        rows = slice(128 * g, 128 * g + 128)
        one = dot(fsplit[turn // 2], tsplit[turn % 2], NN, None)
        part[rows, :] = part[rows, :] + one if turn else one

    def spread(base, rows, parts, turn):
        piece = rows // peers

        @pl.loop(1, peers)
        def _(k):
            other = here.peer(k)
            start = pl.multiple_of(base + piece * other, 8)
            remote(
                part.at[pl.ds(start, piece)],
                parts.at[k],
                p_send.at[turn],
                p_recv.at[turn],
                {"tensor": other},
            ).start()

    def total(base, rows, parts, turn):
        piece = rows // peers
        mine = pl.ds(pl.multiple_of(base + piece * here.t, 8), piece)
        parts[0] = part[mine, :]
        await_bytes(parts.at[pl.ds(1, peers - 1)], p_recv.at[turn])
        arrived[mine, :] = jnp.sum(parts[...], axis=0) * scale

        @pl.loop(1, peers)
        def _(k):
            place = arrived.at[mine]
            remote(
                place,
                place,
                p_send.at[turn + 1],
                p_recv.at[turn + 1],
                {"tensor": here.peer(k)},
            ).start()

    early = 128 * last
    tile = functools.partial
    pieces = [tile(transpose, at, at + 4) for at in range(0, b_ref.shape[1] // 128, 4)]
    pieces += [lambda: None] * (4 - len(pieces))
    for g in range(groups):
        pieces += [tile(join, g)] + [tile(product, g, turn) for turn in (0, 1, 2)]
    pieces.reverse()
    for step in range(1, ring + 1):
        for sub in (0, 1):
            gather.step(step, sub)
            pieces.pop()()
    if last:
        spread(0, early, first_parts, 0)
    while pieces:
        pieces.pop()()
    spread(early, 128, last_parts, 2)
    if last:
        total(0, early, first_parts, 0)
    middle = b_ref.shape[1] // 256
    straight(0, middle)
    total(early, 128, last_parts, 2)
    straight(middle, 2 * middle + 1)
    if last:
        await_bytes(first_parts.at[pl.ds(1, peers - 1)], p_recv.at[1])
    await_bytes(last_parts.at[pl.ds(1, peers - 1)], p_recv.at[3])
    for n in range(chips):
        place = pl.ds(pl.multiple_of(32 * here.chip(offset_of(n)), 32), 32)
        pt[place, :] = arrived[32 * n : 32 * n + 32, :]

    def right_product(g):
        chipped = [here.chip(offset_of(n)) for n in range(4 * g, 4 * g + 4)]
        p = split(arrived[128 * g : 128 * g + 128, :])
        for at, width in tiles:
            b = (bsplit[0, :, at : at + width], bsplit[1, :, at : at + width])
            r = dot3(p, b, NN)
            for n, i in enumerate(chipped):
                place = pl.ds(pl.multiple_of(32 * i, 32), 32)
                rpart[place, at : at + width] = r[32 * n : 32 * n + 32, :]
        for n, i in enumerate(chipped):
            remote(
                rows16(rpart, i, 1 - here.c),
                rpair.at[4 * g + n],
                pair_send,
                pair_recv.at[g],
                here.partner(),
            ).start()

    def right_own(n, sub):
        chip = here.chip(offset_of(n))
        return rows16(rpart, chip, here.c, sub)[...] + rpair[n, 8 * sub : 8 * sub + 8, :]

    def scatter(k, sub):
        if k % 2 == 0 and sub == 0:
            g = k // 2 - 1
            await_bytes(rpair.at[pl.ds(4 * g, 4)], pair_recv.at[g])
        for way in (0, 1):
            if k == ring and sub != way:
                continue
            place = moving.at[way, k, pl.ds(8 * sub, 8)]
            n = 2 * k - 1 if (way == 0 or k == ring) else 2 * k
            if k < ring - 1 or (k == ring - 1 and sub == way):
                await_bytes(place, rs_recv.at[way, k, sub])
                place[...] = place[...] + right_own(n, sub)
            else:
                place[...] = right_own(n, sub)
            remote(
                place,
                moving.at[way, k - 1, pl.ds(8 * sub, 8)],
                rs_send,
                rs_recv.at[way, k - 1, sub],
                here.at(1 - 2 * way),
            ).start()

    collect = Gather(here, rall, ag_send, ag_recv, ag_pair)

    def settle():
        for sub in (0, 1):
            for way in (0, 1):
                place = moving.at[way, 0, pl.ds(8 * sub, 8)]
                await_bytes(place, rs_recv.at[way, 0, sub])
            rows16(rall, here.z, here.c, sub)[...] = (
                right_own(0, sub)
                + moving[0, 0, 8 * sub : 8 * sub + 8, :]
                + moving[1, 0, 8 * sub : 8 * sub + 8, :]
            )
        collect.begin()

    def halve(n):
        collect.shared(n)
        place = pl.ds(pl.multiple_of(32 * here.chip(offset_of(n)), 32), 32)
        rsplit[0, place, :], rsplit[1, place, :] = split(rall[place, :])

    def onward(step, sub):
        collect.step(step, sub)
        n = 2 * step - 3 + sub
        if n >= 0:
            halve(n)

    events = []
    for g in range(last, -1, -1):
        events.append(functools.partial(right_product, g))
        for k in (2 * g + 2, 2 * g + 1):
            events += [functools.partial(scatter, k, sub) for sub in (0, 1)]
    events.append(settle)
    for step in range(1, ring + 1):
        events += [functools.partial(onward, step, sub) for sub in (0, 1)]
    events.reverse()

    def advance(count=1):
        for _ in range(count):
            if events:
                events.pop()()

    advance()
    block = rank // peers
    half = block // 2
    each = half // chips
    mine = pl.ds(pl.multiple_of(block * here.t, block), block)
    gpart[...] = dot(pt[mine, :], pt[...].T, NN, HIGHEST)
    theirs = pl.ds(pl.multiple_of(half * (1 - here.c), half), half)
    keep = pl.ds(pl.multiple_of(half * here.c, half), half)
    pair = remote(gpart.at[theirs], gpair, g_send.at[0], g_recv.at[0], here.partner())
    pair.start()
    advance(2)
    psplit[0], psplit[1] = split(pt[...])
    pair.wait()
    chip_sum = gpart[keep, :] + gpair[...]
    for k in range(chips):
        gsplit[k] = chip_sum[each * k : each * (k + 1), :]

    @pl.loop(1, chips)
    def _(k):
        remote(
            gsplit.at[here.chip(k)],
            gsplits.at[k],
            g_send.at[1],
            g_recv.at[1],
            here.at(k),
        ).start()

    advance(2)
    gsplits[0] = gsplit[here.z]
    await_bytes(gsplits.at[pl.ds(1, chips - 1)], g_recv.at[1])
    gsums[here.z] = jnp.sum(gsplits[...], axis=0)

    @pl.loop(1, chips)
    def _(k):
        place = gsums.at[here.z]
        remote(place, place, g_send.at[2], g_recv.at[2], here.at(k)).start()

    advance(3)
    await_bytes(gsums.at[pl.ds(0, chips - 1)], g_recv.at[2])
    gram[here.t, here.c] = gsums[...].reshape(half, rank)

    @pl.loop(1, peers)
    def _(k):
        place = gram.at[here.t, here.c]
        remote(
            place, place, g_send.at[3], g_recv.at[3], {"tensor": here.peer(k)}
        ).start()

    advance(2)
    await_bytes(gram.at[pl.ds(0, peers - 1), 0], g_recv.at[3])
    halves = gram.at[:, here.c]
    pair = remote(halves, halves, g_send.at[4], g_recv.at[4], here.partner())
    pair.start()
    advance()
    pair.wait()
    m_ref[...] = gram[...].reshape(rank, rank)
    wsplit[...] = jnp.zeros_like(wsplit)

    def after(start, w):
        rows, columns = slice(start, start + 128), slice(0, start + 128)
        wsplit[0, rows, columns], wsplit[1, rows, columns] = split(w)

    invert_factor(m_ref, block_ref, advance, after)
    advance(len(events))
    halve(chips - 1)

    sums = jnp.zeros((rank, 128), jnp.float32)
    for at, width in tiles:
        columns = slice(at, at + width)
        blocks = []
        for row in range(0, rank, 256):
            stop = row + 256
            blocks.append(
                dot3(
                    (wsplit[0, row:stop, 0:stop], wsplit[1, row:stop, 0:stop]),
                    (rsplit[0, 0:stop, columns], rsplit[1, 0:stop, columns]),
                    NN,
                )
            )
        right = jnp.concatenate(blocks, axis=0)
        for lane in range(0, width, 128):
            one = right[:, lane : lane + 128]
            sums = sums + one * one
        rsplit[0, :, columns], rsplit[1, :, columns] = split(right)
    squares[0] = jnp.sum(sums.T, axis=0, keepdims=True)

    @pl.loop(1, peers)
    def _(k):
        remote(
            squares.at[0], squares.at[k], sq_send, sq_recv, {"tensor": here.peer(k)}
        ).start()

    blocks = []
    for row in range(0, rank, 256):
        stop = row + 256
        blocks.append(
            dot3(
                (wsplit[0, row:stop, 0:stop], wsplit[1, row:stop, 0:stop]),
                (psplit[0, 0:stop, :], psplit[1, 0:stop, :]),
                NN,
            )
        )
    q = jnp.concatenate(blocks, axis=0).T
    qlow_ref[...] = (q * -0.05).astype(jnp.bfloat16)
    await_bytes(squares.at[pl.ds(1, peers - 1)], sq_recv)
    scales = lax.rsqrt(jnp.sum(squares[...], axis=0) * mean + 1e-06)
    qsplit_ref[0], qsplit_ref[1] = split(q * (scales * gain))
    lanes = lax.broadcasted_iota(jnp.int32, (32, rank), 1)
    rows = lax.broadcasted_iota(jnp.int32, (32, rank), 0) + 32 * here.z
    picked = jnp.where(lanes == rows, jnp.broadcast_to(scales, (32, rank)), 0.0)
    place = pl.ds(pl.multiple_of(32 * here.z, 32), 32)
    ours = (
        rsplit[0, place, :].astype(jnp.float32) + rsplit[1, place, :].astype(jnp.float32)
    ) * jnp.sum(picked, axis=1, keepdims=True)
    factor_ref[...] = jnp.where(here.c == 0, ours[0:16], ours[16:32])

    gather.end()
    collect.end()
    if last:
        for turn in (0, 1):
            await_bytes(first_parts.at[pl.ds(1, peers - 1)], p_send.at[turn])
    for turn in (2, 3):
        await_bytes(last_parts.at[pl.ds(1, peers - 1)], p_send.at[turn])
    await_bytes(gsplits.at[pl.ds(1, chips - 1)], g_send.at[1])
    await_bytes(gsums.at[pl.ds(0, chips - 1)], g_send.at[2])
    await_bytes(gram.at[pl.ds(0, peers - 1), 0], g_send.at[3])
    await_bytes(rpart.at[pl.ds(0, rank // 2)], pair_send)
    await_bytes(rall.at[pl.ds(0, 16 * (chips - 1))], rs_send)
    await_bytes(squares.at[pl.ds(1, peers - 1)], sq_send)


def finish(b_ref, qlow_ref, qsplit_ref, rsplit_ref, f_ref, momentum_ref, update_ref, factor_ref):
    right = (rsplit_ref[0], rsplit_ref[1])
    momentum_ref[...] = b_ref[...] + dot(qlow_ref[...], right[0], NN, None)
    update_ref[...] = dot3((qsplit_ref[0], qsplit_ref[1]), right, NN).astype(jnp.bfloat16)
    factor_ref[...] = f_ref[...]


def body(chips, peers, buffer, factor):
    rows, columns = buffer.shape
    rank = 32 * chips
    half = rank // peers // 2
    each = half // chips
    total_columns = columns * peers
    groups = chips // 4
    ring = chips // 2
    f32, bf16 = jnp.float32, jnp.bfloat16
    dma = pltpu.SemaphoreType.DMA
    vmem = pl.BlockSpec(memory_space=pltpu.VMEM)
    qlow, qsplit, rsplit, factor_t = pl.pallas_call(
        functools.partial(
            kernel,
            chips,
            peers,
            1.0 / math.sqrt(total_columns),
            1.0 / total_columns,
            math.sqrt(rows * 2 * chips / rank),
        ),
        out_shape=(
            jax.ShapeDtypeStruct((rows, rank), bf16),
            jax.ShapeDtypeStruct((2, rows, rank), bf16),
            jax.ShapeDtypeStruct((2, rank, columns), bf16),
            jax.ShapeDtypeStruct((16, columns), f32),
        ),
        in_specs=[vmem] * 2,
        out_specs=(vmem,) * 4,
        scratch_shapes=[
            pltpu.VMEM((2, rows, columns), bf16),
            pltpu.VMEM((2, columns, rows), bf16),
            pltpu.VMEM((rank, columns), f32),
            pltpu.VMEM((2, 128, columns), bf16),
            pltpu.VMEM((rank, rows), f32),
            pltpu.VMEM((peers, max(groups - 1, 1) * 128 // peers, rows), f32),
            pltpu.VMEM((peers, 128 // peers, rows), f32),
            pltpu.VMEM((rank, rows), f32),
            pltpu.VMEM((rank, rows), f32),
            pltpu.VMEM((2, rank, rows), bf16),
            pltpu.VMEM((2 * half, rank), f32),
            pltpu.VMEM((half, rank), f32),
            pltpu.VMEM((chips, each, rank), f32),
            pltpu.VMEM((chips, each, rank), f32),
            pltpu.VMEM((chips, each, rank), f32),
            pltpu.VMEM((peers, 2, half, rank), f32),
            pltpu.VMEM((rank, rank), f32),
            pltpu.VMEM((128, 128), f32),
            pltpu.VMEM((2, rank, rank), bf16),
            pltpu.VMEM((rank, columns), f32),
            pltpu.VMEM((chips, 16, columns), f32),
            pltpu.VMEM((2, ring + 1, 16, columns), f32),
            pltpu.VMEM((rank, columns), f32),
            pltpu.VMEM((peers, 1, rank), f32),
            dma,
            dma((2, ring, 2)),
            dma((chips,)),
            dma((4,)),
            dma((4,)),
            dma((5,)),
            dma((5,)),
            dma,
            dma((groups,)),
            dma,
            dma((2, ring, 2)),
            dma,
            dma((2, ring, 2)),
            dma((chips,)),
            dma,
            dma,
        ],
        compiler_params=pltpu.CompilerParams(
            collective_id=0, has_side_effects=True, vmem_limit_bytes=LIMIT
        ),
        name="low_rank_update",
    )(buffer, factor.T)

    def whole(*shape):
        return pl.BlockSpec(shape, lambda i: (0,) * len(shape))

    def tile(*lead):
        return pl.BlockSpec((*lead, 256), lambda i: (0,) * len(lead) + (i,))

    momentum, update, factor_t = pl.pallas_call(
        finish,
        grid=(pl.cdiv(columns, 256),),
        out_shape=(
            jax.ShapeDtypeStruct((rows, columns), f32),
            jax.ShapeDtypeStruct((rows, columns), bf16),
            jax.ShapeDtypeStruct((16, columns), f32),
        ),
        in_specs=[
            tile(rows),
            whole(rows, rank),
            whole(2, rows, rank),
            tile(2, rank),
            tile(16),
        ],
        out_specs=(tile(rows), tile(rows), tile(16)),
        compiler_params=pltpu.CompilerParams(vmem_limit_bytes=LIMIT),
        name="finish",
    )(buffer, qlow, qsplit, rsplit, factor_t)
    return momentum, update, factor_t.T


def solution(mesh):
    chips, peers = mesh.shape["dp"] // 2, mesh.shape["tensor"]
    placed = (P("dp", "tensor"), P("tensor", "dp"))
    return jax.shard_map(
        functools.partial(body, chips, peers),
        mesh=mesh,
        in_specs=placed,
        out_specs=(P("dp", "tensor"), P("dp", "tensor"), P("tensor", "dp")),
        check_vma=False,
    )
```

```python
import functools
import math

import jax
import jax.numpy as jnp
from jax import lax
from jax.experimental import pallas as pl
from jax.experimental.pallas import tpu as pltpu
from jax.sharding import PartitionSpec as P

MESH = pl.DeviceIdType.MESH
HIGHEST = lax.Precision.HIGHEST
NN = (((1,), (0,)), ((), ()))
LIMIT = 56 * 1024 * 1024


def dot(a, b, dims, precision):
    return lax.dot_general(
        a, b, dims, precision=precision, preferred_element_type=jnp.float32
    )


class Place:
    def __init__(self, chips, peers):
        dp = lax.axis_index("dp")
        self.z, self.c = dp // 2, dp % 2
        self.t = lax.axis_index("tensor")
        self.chips, self.peers = chips, peers

    def chip(self, offset):
        return lax.rem(self.z + offset + self.chips, self.chips)

    def at(self, offset):
        return {"dp": 2 * self.chip(offset) + self.c}

    def partner(self):
        return {"dp": 2 * self.z + 1 - self.c}

    def peer(self, k):
        return lax.rem(self.t + k, self.peers)


def remote(src, dst, send, recv, device):
    return pltpu.make_async_remote_copy(
        src_ref=src,
        dst_ref=dst,
        send_sem=send,
        recv_sem=recv,
        device_id=device,
        device_id_type=MESH,
    )


def await_bytes(ref, sem):
    pltpu.make_async_copy(ref, ref, sem).wait()


def enter(here, ring):
    barrier = pltpu.get_barrier_semaphore()

    def greet(device):
        pl.semaphore_signal(barrier, inc=1, device_id=device, device_id_type=MESH)

    @pl.loop(1, here.peers)
    def _(k):
        greet({"tensor": here.peer(k)})

    greet(here.partner())
    if ring:

        @pl.loop(1, here.chips)
        def _(k):
            greet(here.at(k))

        count = here.chips - 1
    else:
        greet(here.at(1))
        greet(here.at(-1))
        count = 2
    pl.semaphore_wait(barrier, here.peers - 1 + 1 + count)


def offset_of(n):
    return ((n + 1) // 2) * (2 * (n % 2) - 1)


def rows16(ref, chip, core, sub=None):
    start = 32 * chip + 16 * core
    if sub is None:
        return ref.at[pl.ds(pl.multiple_of(start, 16), 16)]
    return ref.at[pl.ds(pl.multiple_of(start + 8 * sub, 8), 8)]


class Gather:
    def __init__(self, here, buf, send, recv, pair_recv):
        self.here, self.buf = here, buf
        self.send, self.recv, self.pair_recv = send, recv, pair_recv
        self.half = here.chips // 2

    def forward(self, step, way, sub):
        here, sign = self.here, 1 - 2 * way
        ref = rows16(self.buf, here.chip(-sign * (step - 1)), here.c, sub)
        remote(
            ref, ref, self.send, self.recv.at[way, step - 1, sub], here.at(sign)
        ).start()

    def share(self, offset, slot):
        here = self.here
        ref = rows16(self.buf, here.chip(offset), here.c)
        remote(ref, ref, self.send, self.pair_recv.at[slot], here.partner()).start()

    def begin(self):
        for sub in (0, 1):
            for way in (0, 1):
                self.forward(1, way, sub)
        self.share(0, 0)

    def step(self, step, sub):
        here = self.here

        def take(way):
            sign = 1 - 2 * way
            ref = rows16(self.buf, here.chip(-sign * step), here.c, sub)
            await_bytes(ref, self.recv.at[way, step - 1, sub])

            @pl.when(step + 1 < self.half + (sub == way))
            def _():
                self.forward(step + 1, way, sub)

        take(sub)

        @pl.when(step < self.half)
        def _():
            take(1 - sub)

        if sub == 1:
            self.share(step, 2 * step - 1)

            @pl.when(step < self.half)
            def _():
                self.share(-step, 2 * step)

    def shared(self, n):
        here = self.here
        ref = rows16(self.buf, here.chip(offset_of(n)), 1 - here.c)
        await_bytes(ref, self.pair_recv.at[n])

    def end(self):
        rows = 16 * (2 * self.here.chips - 1)
        await_bytes(self.buf.at[pl.ds(0, rows)], self.send)


def split(value):
    high = value.astype(jnp.bfloat16)
    return high, (value - high.astype(jnp.float32)).astype(jnp.bfloat16)


def dot3(a, b, dims):
    return (
        dot(a[0], b[0], dims, None) + dot(a[0], b[1], dims, None)
    ) + dot(a[1], b[0], dims, None)


def splat(value):
    return jnp.broadcast_to(value, (8, 128))


def eliminate(turn, carry, w_ref):
    s = carry
    lane = lax.broadcasted_iota(jnp.int32, (8, 128), 1)
    sublane = lax.broadcasted_iota(jnp.int32, (8, 128), 0)
    for half in (0, 8):
        block = (lane >= half) & (lane < half + 8)
        columns = [
            jnp.broadcast_to(s[:, half + j : half + j + 1], s.shape) for j in range(8)
        ]
        d = {
            (i, j): splat(columns[j][i : i + 1, :]) for j in range(8) for i in range(j, 8)
        }
        top = jnp.where(block, jnp.where(lane == sublane + half, 1.0, 0.0), s[0:8])
        r = [splat(top[i : i + 1, :]) for i in range(8)]
        root, inverse, t = [], [], {}
        for k in range(8):
            root.append(lax.rsqrt(d[k, k]))
            inverse.append(root[k] * root[k])
            for i in range(k + 1, 8):
                t[i, k] = d[i, k] * inverse[k]
                for j in range(k + 1, i + 1):
                    d[i, j] = d[i, j] - t[i, k] * d[j, k]
                r[i] = r[i] - t[i, k] * r[k]
        done = r[0] * root[0]
        for k in range(1, 8):
            done = jnp.where(sublane == k, r[k] * root[k], done)
        keep = (lane >= 128 - 16 * turn) | (lane < half + 8)
        w_ref[pl.ds(pl.multiple_of(16 * turn + half, 8), 8), :] = jnp.where(
            keep, done, 0.0
        )
        for k in range(7, -1, -1):
            r[k] = r[k] * inverse[k]
            for i in range(7, k, -1):
                r[k] = r[k] - t[i, k] * r[i]
        lanes = lax.broadcasted_iota(jnp.int32, (s.shape[0] - 8, 128), 1)
        s = jnp.where((lanes >= half) & (lanes < half + 8), 0.0, s[8:])
        for j in range(8):
            s = s - columns[j][8:] * r[j][0:1, :]
    blank = jnp.zeros((16, 128), jnp.float32)
    return pltpu.roll(jnp.concatenate([s, blank], axis=0), 112, 1)


def invert_factor(m_ref, block_ref, wsplit, between):
    rank = m_ref.shape[0]

    @pl.loop(0, rank // 128)
    def _(panel):
        here = pl.ds(pl.multiple_of(128 * panel, 128), 128)

        def half(i, carry):
            for sub in (0, 1):
                first = 4 * i + 2 * sub
                carry = lax.fori_loop(
                    first,
                    first + 2,
                    functools.partial(eliminate, w_ref=block_ref),
                    carry,
                )
                between(2 * panel + i + 1, sub)
            return carry

        lax.fori_loop(0, 2, half, m_ref[here, here])
        w = jnp.concatenate(
            [block_ref[0:16, :]]
            + [pltpu.roll(block_ref[16 * i : 16 * i + 16, :], 16 * i, 1) for i in range(1, 8)],
            axis=0,
        )
        m_ref[here, :] = dot(w, m_ref[here, :], NN, HIGHEST)
        m_ref[here, here] = w

        @pl.when(panel < rank // 128 - 1)
        def _():
            rows = lax.broadcasted_iota(jnp.int32, (rank, 128), 0)
            below = rows >= 128 * panel + 128
            lower = jnp.where(below, m_ref[here, :].T, 0.0)
            m_ref[:, here] = jnp.where(below, 0.0, m_ref[:, here])
            m_ref[...] = m_ref[...] - dot(lower, m_ref[here, :], NN, HIGHEST)

        lanes = lax.broadcasted_iota(jnp.int32, (128, rank), 1)
        wsplit[0, here, :], wsplit[1, here, :] = split(
            jnp.where(lanes < 128 * panel + 128, m_ref[here, :], 0.0)
        )


def column_tiles(columns):
    return [(at, min(256, columns - at)) for at in range(0, columns, 256)]


def kernel(
    chips,
    peers,
    scale,
    mean,
    gain,
    b_ref,
    f_ref,
    qlow_ref,
    qsplit_ref,
    rsplit,
    factor_ref,
    bsplit,
    tsplit,
    fall,
    fsplit,
    part,
    first_parts,
    last_parts,
    arrived,
    pt,
    psplit,
    gpart,
    gpair,
    gsplit,
    gsplits,
    gsums,
    gram,
    m_ref,
    block_ref,
    wsplit,
    rpart,
    rpair,
    moving,
    rall,
    sums,
    squares,
    f_send,
    f_recv,
    f_pair,
    p_send,
    p_recv,
    g_send,
    g_recv,
    pair_send,
    pair_recv,
    rs_send,
    rs_recv,
    ag_send,
    ag_recv,
    ag_pair,
    sq_send,
    sq_recv,
):
    here = Place(chips, peers)
    rank = 32 * chips
    ring = chips // 2
    groups = chips // 4
    last = groups - 1
    tiles = column_tiles(b_ref.shape[1])
    own = rows16(fall, here.z, here.c)
    own[...] = f_ref[...]
    enter(here, True)
    gather = Gather(here, fall, f_send, f_recv, f_pair)
    gather.begin()

    def tile(i):
        return pl.ds(pl.multiple_of(128 * i, 128), 128)

    count = b_ref.shape[1] // 128

    def transpose(quarter):
        low, high = quarter * count // 4, (quarter + 1) * count // 4

        @pl.loop(low, high)
        def _(i):
            tsplit[0, tile(i), :], tsplit[1, tile(i), :] = split(b_ref[:, tile(i)].T)

    def straight(low, high):
        @pl.loop(low, high)
        def _(i):
            bsplit[0, :, tile(i)], bsplit[1, :, tile(i)] = split(b_ref[:, tile(i)])

    def join(g):
        order = [4 * g + n for n in range(4)]
        for n in order:
            gather.shared(n)
        rows = [
            fall[pl.ds(pl.multiple_of(32 * here.chip(offset_of(n)), 32), 32), :]
            for n in order
        ]
        fsplit[0], fsplit[1] = split(jnp.concatenate(rows, axis=0))

    def product(g, turn):
        rows = tile(g)
        one = dot(fsplit[turn // 2], tsplit[turn % 2], NN, None)
        part[rows, :] = part[rows, :] + one if turn else one

    def spread(base, rows, parts, turn):
        piece = rows // peers

        @pl.loop(1, peers)
        def _(k):
            other = here.peer(k)
            start = pl.multiple_of(base + piece * other, 8)
            remote(
                part.at[pl.ds(start, piece)],
                parts.at[k],
                p_send.at[turn],
                p_recv.at[turn],
                {"tensor": other},
            ).start()

    def total(base, rows, parts, turn):
        piece = rows // peers
        mine = pl.ds(pl.multiple_of(base + piece * here.t, 8), piece)
        parts[0] = part[mine, :]
        await_bytes(parts.at[pl.ds(1, peers - 1)], p_recv.at[turn])
        arrived[mine, :] = jnp.sum(parts[...], axis=0) * scale

        @pl.loop(1, peers)
        def _(k):
            place = arrived.at[mine]
            remote(
                place,
                place,
                p_send.at[turn + 1],
                p_recv.at[turn + 1],
                {"tensor": here.peer(k)},
            ).start()

    early = 128 * last

    def piece(g, i):
        if i == 0:
            join(g)
        else:
            product(g, i - 1)

    @pl.loop(0, groups)
    def _(g):
        for i in range(4):
            gather.step(2 * g + 1 + i // 2, i % 2)

            @pl.when(g == 0)
            def _():
                transpose(i)

            @pl.when(g > 0)
            def _():
                piece(g - 1, i)

    if last:
        spread(0, early, first_parts, 0)
    for i in range(4):
        piece(last, i)
    spread(early, 128, last_parts, 2)
    if last:
        total(0, early, first_parts, 0)
    straight(0, count // 2)
    total(early, 128, last_parts, 2)
    straight(count // 2, count)
    if last:
        await_bytes(first_parts.at[pl.ds(1, peers - 1)], p_recv.at[1])
    await_bytes(last_parts.at[pl.ds(1, peers - 1)], p_recv.at[3])

    @pl.loop(0, chips)
    def _(n):
        place = pl.ds(pl.multiple_of(32 * here.chip(offset_of(n)), 32), 32)
        pt[place, :] = arrived[pl.ds(pl.multiple_of(32 * n, 32), 32), :]

    def right_product(g):
        chipped = [here.chip(offset_of(4 * g + n)) for n in range(4)]
        p = split(arrived[tile(g), :])
        for at, width in tiles:
            b = (bsplit[0, :, at : at + width], bsplit[1, :, at : at + width])
            r = dot3(p, b, NN)
            for n, i in enumerate(chipped):
                place = pl.ds(pl.multiple_of(32 * i, 32), 32)
                rpart[place, at : at + width] = r[32 * n : 32 * n + 32, :]
        for n, i in enumerate(chipped):
            remote(
                rows16(rpart, i, 1 - here.c),
                rpair.at[4 * g + n],
                pair_send,
                pair_recv.at[g],
                here.partner(),
            ).start()

    def right_own(n, sub):
        chip = here.chip(offset_of(n))
        return rows16(rpart, chip, here.c, sub)[...] + rpair[n, 8 * sub : 8 * sub + 8, :]

    def scatter(k, sub):
        def pass_on(way, come):
            place = moving.at[way, k, pl.ds(8 * sub, 8)]
            n = 2 * k - 1 if way == 0 else 2 * k - 2 * k // chips

            @pl.when(come)
            def _():
                await_bytes(place, rs_recv.at[way, k, sub])
                place[...] = place[...] + right_own(n, sub)

            @pl.when(jnp.logical_not(come))
            def _():
                place[...] = right_own(n, sub)

            remote(
                place,
                moving.at[way, k - 1, pl.ds(8 * sub, 8)],
                rs_send,
                rs_recv.at[way, k - 1, sub],
                here.at(1 - 2 * way),
            ).start()

        pass_on(sub, k < ring)

        @pl.when(k < ring)
        def _():
            pass_on(1 - sub, k < ring - 1)

    collect = Gather(here, rall, ag_send, ag_recv, ag_pair)

    def settle():
        for sub in (0, 1):
            for way in (0, 1):
                place = moving.at[way, 0, pl.ds(8 * sub, 8)]
                await_bytes(place, rs_recv.at[way, 0, sub])
            rows16(rall, here.z, here.c, sub)[...] = (
                right_own(0, sub)
                + moving[0, 0, 8 * sub : 8 * sub + 8, :]
                + moving[1, 0, 8 * sub : 8 * sub + 8, :]
            )
        collect.begin()

    def halve(n):
        collect.shared(n)
        place = pl.ds(pl.multiple_of(32 * here.chip(offset_of(n)), 32), 32)
        rsplit[0, place, :], rsplit[1, place, :] = split(rall[place, :])

    def onward(step, sub):
        collect.step(step, sub)

        @pl.when(2 * step - 3 + sub >= 0)
        def _():
            halve(2 * step - 3 + sub)

    block = rank // peers
    half = block // 2
    each = half // chips
    mine = pl.ds(pl.multiple_of(block * here.t, block), block)
    theirs = pl.ds(pl.multiple_of(half * (1 - here.c), half), half)
    keep = pl.ds(pl.multiple_of(half * here.c, half), half)

    def gram_pair():
        return remote(
            gpart.at[theirs], gpair, g_send.at[0], g_recv.at[0], here.partner()
        )

    def gram_own():
        gpart[...] = dot(pt[mine, :], pt[...].T, NN, HIGHEST)
        gram_pair().start()

    def gram_scatter():
        gram_pair().wait()
        chip_sum = gpart[keep, :] + gpair[...]
        for k in range(chips):
            gsplit[k] = chip_sum[each * k : each * (k + 1), :]

        @pl.loop(1, chips)
        def _(k):
            remote(
                gsplit.at[here.chip(k)],
                gsplits.at[k],
                g_send.at[1],
                g_recv.at[1],
                here.at(k),
            ).start()

        gsplits[0] = gsplit[here.z]

    def gram_gather():
        await_bytes(gsplits.at[pl.ds(1, chips - 1)], g_recv.at[1])
        gsums[here.z] = jnp.sum(gsplits[...], axis=0)

        @pl.loop(1, chips)
        def _(k):
            place = gsums.at[here.z]
            remote(place, place, g_send.at[2], g_recv.at[2], here.at(k)).start()

    def gram_spread():
        await_bytes(gsums.at[pl.ds(0, chips - 1)], g_recv.at[2])
        gram[here.t, here.c] = gsums[...].reshape(half, rank)

        @pl.loop(1, peers)
        def _(k):
            place = gram.at[here.t, here.c]
            remote(
                place, place, g_send.at[3], g_recv.at[3], {"tensor": here.peer(k)}
            ).start()

    gram_steps = (gram_own, gram_scatter, gram_gather, gram_spread)

    @pl.loop(0, groups)
    def _(turn):
        g = last - turn
        right_product(g)
        for i, step in enumerate(gram_steps):
            if i < groups:

                @pl.when(turn == i)
                def _():
                    step()

        await_bytes(rpair.at[pl.ds(4 * g, 4)], pair_recv.at[g])
        for k in (2 * g + 2, 2 * g + 1):
            for sub in (0, 1):
                scatter(k, sub)

    for i, step in enumerate(gram_steps):
        if i >= groups:
            step()
    psplit[0], psplit[1] = split(pt[...])
    await_bytes(gram.at[pl.ds(0, peers - 1), 0], g_recv.at[3])
    halves = gram.at[:, here.c]
    pair = remote(halves, halves, g_send.at[4], g_recv.at[4], here.partner())
    pair.start()
    settle()
    pair.wait()
    m_ref[...] = gram[...].reshape(rank, rank)
    invert_factor(m_ref, block_ref, wsplit, onward)
    halve(chips - 1)

    sums[...] = jnp.zeros_like(sums)

    def right_tile(at, width):
        columns = pl.ds(at, width)
        blocks = []
        for row in range(0, rank, 256):
            stop = row + 256
            blocks.append(
                dot3(
                    (wsplit[0, row:stop, 0:stop], wsplit[1, row:stop, 0:stop]),
                    (rsplit[0, 0:stop, columns], rsplit[1, 0:stop, columns]),
                    NN,
                )
            )
        right = jnp.concatenate(blocks, axis=0)
        for lane in range(0, width, 128):
            one = right[:, lane : lane + 128]
            sums[...] = sums[...] + one * one
        rsplit[0, :, columns], rsplit[1, :, columns] = split(right)

    full = 256 * (b_ref.shape[1] // 256)

    @pl.loop(0, full // 256)
    def _(i):
        right_tile(pl.multiple_of(256 * i, 256), 256)

    if full < b_ref.shape[1]:
        right_tile(full, b_ref.shape[1] - full)
    squares[0] = jnp.sum(sums[...].T, axis=0, keepdims=True)

    @pl.loop(1, peers)
    def _(k):
        remote(
            squares.at[0], squares.at[k], sq_send, sq_recv, {"tensor": here.peer(k)}
        ).start()

    blocks = []
    for row in range(0, rank, 256):
        stop = row + 256
        blocks.append(
            dot3(
                (wsplit[0, row:stop, 0:stop], wsplit[1, row:stop, 0:stop]),
                (psplit[0, 0:stop, :], psplit[1, 0:stop, :]),
                NN,
            )
        )
    q = jnp.concatenate(blocks, axis=0).T
    qlow_ref[...] = (q * -0.05).astype(jnp.bfloat16)
    await_bytes(squares.at[pl.ds(1, peers - 1)], sq_recv)
    scales = lax.rsqrt(jnp.sum(squares[...], axis=0) * mean + 1e-06)
    qsplit_ref[0], qsplit_ref[1] = split(q * (scales * gain))
    lanes = lax.broadcasted_iota(jnp.int32, (32, rank), 1)
    rows = lax.broadcasted_iota(jnp.int32, (32, rank), 0) + 32 * here.z
    picked = jnp.where(lanes == rows, jnp.broadcast_to(scales, (32, rank)), 0.0)
    place = pl.ds(pl.multiple_of(32 * here.z, 32), 32)
    ours = (
        rsplit[0, place, :].astype(jnp.float32) + rsplit[1, place, :].astype(jnp.float32)
    ) * jnp.sum(picked, axis=1, keepdims=True)
    factor_ref[...] = jnp.where(here.c == 0, ours[0:16], ours[16:32])

    gather.end()
    collect.end()
    if last:
        for turn in (0, 1):
            await_bytes(first_parts.at[pl.ds(1, peers - 1)], p_send.at[turn])
    for turn in (2, 3):
        await_bytes(last_parts.at[pl.ds(1, peers - 1)], p_send.at[turn])
    await_bytes(gsplits.at[pl.ds(1, chips - 1)], g_send.at[1])
    await_bytes(gsums.at[pl.ds(0, chips - 1)], g_send.at[2])
    await_bytes(gram.at[pl.ds(0, peers - 1), 0], g_send.at[3])
    await_bytes(rpart.at[pl.ds(0, rank // 2)], pair_send)
    await_bytes(rall.at[pl.ds(0, 16 * (chips - 1))], rs_send)
    await_bytes(squares.at[pl.ds(1, peers - 1)], sq_send)


def finish(b_ref, qlow_ref, qsplit_ref, rsplit_ref, f_ref, momentum_ref, update_ref, factor_ref):
    right = (rsplit_ref[0], rsplit_ref[1])
    momentum_ref[...] = b_ref[...] + dot(qlow_ref[...], right[0], NN, None)
    update_ref[...] = dot3((qsplit_ref[0], qsplit_ref[1]), right, NN).astype(jnp.bfloat16)
    factor_ref[...] = f_ref[...]


def body(chips, peers, buffer, factor):
    rows, columns = buffer.shape
    rank = 32 * chips
    half = rank // peers // 2
    each = half // chips
    total_columns = columns * peers
    groups = chips // 4
    ring = chips // 2
    f32, bf16 = jnp.float32, jnp.bfloat16
    dma = pltpu.SemaphoreType.DMA
    vmem = pl.BlockSpec(memory_space=pltpu.VMEM)
    qlow, qsplit, rsplit, factor_t = pl.pallas_call(
        functools.partial(
            kernel,
            chips,
            peers,
            1.0 / math.sqrt(total_columns),
            1.0 / total_columns,
            math.sqrt(rows * 2 * chips / rank),
        ),
        out_shape=(
            jax.ShapeDtypeStruct((rows, rank), bf16),
            jax.ShapeDtypeStruct((2, rows, rank), bf16),
            jax.ShapeDtypeStruct((2, rank, columns), bf16),
            jax.ShapeDtypeStruct((16, columns), f32),
        ),
        in_specs=[vmem] * 2,
        out_specs=(vmem,) * 4,
        scratch_shapes=[
            pltpu.VMEM((2, rows, columns), bf16),
            pltpu.VMEM((2, columns, rows), bf16),
            pltpu.VMEM((rank, columns), f32),
            pltpu.VMEM((2, 128, columns), bf16),
            pltpu.VMEM((rank, rows), f32),
            pltpu.VMEM((peers, max(groups - 1, 1) * 128 // peers, rows), f32),
            pltpu.VMEM((peers, 128 // peers, rows), f32),
            pltpu.VMEM((rank, rows), f32),
            pltpu.VMEM((rank, rows), f32),
            pltpu.VMEM((2, rank, rows), bf16),
            pltpu.VMEM((2 * half, rank), f32),
            pltpu.VMEM((half, rank), f32),
            pltpu.VMEM((chips, each, rank), f32),
            pltpu.VMEM((chips, each, rank), f32),
            pltpu.VMEM((chips, each, rank), f32),
            pltpu.VMEM((peers, 2, half, rank), f32),
            pltpu.VMEM((rank, rank), f32),
            pltpu.VMEM((128, 128), f32),
            pltpu.VMEM((2, rank, rank), bf16),
            pltpu.VMEM((rank, columns), f32),
            pltpu.VMEM((chips, 16, columns), f32),
            pltpu.VMEM((2, ring + 1, 16, columns), f32),
            pltpu.VMEM((rank, columns), f32),
            pltpu.VMEM((rank, 128), f32),
            pltpu.VMEM((peers, 1, rank), f32),
            dma,
            dma((2, ring, 2)),
            dma((chips,)),
            dma((4,)),
            dma((4,)),
            dma((5,)),
            dma((5,)),
            dma,
            dma((groups,)),
            dma,
            dma((2, ring, 2)),
            dma,
            dma((2, ring, 2)),
            dma((chips,)),
            dma,
            dma,
        ],
        compiler_params=pltpu.CompilerParams(
            collective_id=0, has_side_effects=True, vmem_limit_bytes=LIMIT
        ),
        name="low_rank_update",
    )(buffer, factor.T)

    def whole(*shape):
        return pl.BlockSpec(shape, lambda i: (0,) * len(shape))

    def tile(*lead):
        return pl.BlockSpec((*lead, 256), lambda i: (0,) * len(lead) + (i,))

    momentum, update, factor_t = pl.pallas_call(
        finish,
        grid=(pl.cdiv(columns, 256),),
        out_shape=(
            jax.ShapeDtypeStruct((rows, columns), f32),
            jax.ShapeDtypeStruct((rows, columns), bf16),
            jax.ShapeDtypeStruct((16, columns), f32),
        ),
        in_specs=[
            tile(rows),
            whole(rows, rank),
            whole(2, rows, rank),
            tile(2, rank),
            tile(16),
        ],
        out_specs=(tile(rows), tile(rows), tile(16)),
        compiler_params=pltpu.CompilerParams(vmem_limit_bytes=LIMIT),
        name="finish",
    )(buffer, qlow, qsplit, rsplit, factor_t)
    return momentum, update, factor_t.T


def solution(mesh):
    chips, peers = mesh.shape["dp"] // 2, mesh.shape["tensor"]
    placed = (P("dp", "tensor"), P("tensor", "dp"))
    return jax.shard_map(
        functools.partial(body, chips, peers),
        mesh=mesh,
        in_specs=placed,
        out_specs=(P("dp", "tensor"), P("dp", "tensor"), P("tensor", "dp")),
        check_vma=False,
    )
```

```python
import functools
import math

import jax
import jax.numpy as jnp
from jax import lax
from jax.experimental import pallas as pl
from jax.experimental.pallas import tpu as pltpu
from jax.sharding import PartitionSpec as P

MESH = pl.DeviceIdType.MESH
HIGHEST = lax.Precision.HIGHEST
NN = (((1,), (0,)), ((), ()))
LIMIT = 56 * 1024 * 1024


def dot(a, b, dims, precision):
    return lax.dot_general(
        a, b, dims, precision=precision, preferred_element_type=jnp.float32
    )


class Place:
    def __init__(self, chips, peers):
        dp = lax.axis_index("dp")
        self.z, self.c = dp // 2, dp % 2
        self.t = lax.axis_index("tensor")
        self.chips, self.peers = chips, peers

    def chip(self, offset):
        return lax.rem(self.z + offset + self.chips, self.chips)

    def at(self, offset):
        return {"dp": 2 * self.chip(offset) + self.c}

    def partner(self):
        return {"dp": 2 * self.z + 1 - self.c}

    def peer(self, k):
        return lax.rem(self.t + k, self.peers)


def remote(src, dst, send, recv, device):
    return pltpu.make_async_remote_copy(
        src_ref=src,
        dst_ref=dst,
        send_sem=send,
        recv_sem=recv,
        device_id=device,
        device_id_type=MESH,
    )


def await_bytes(ref, sem):
    pltpu.make_async_copy(ref, ref, sem).wait()


def enter(here, ring):
    barrier = pltpu.get_barrier_semaphore()

    def greet(device):
        pl.semaphore_signal(barrier, inc=1, device_id=device, device_id_type=MESH)

    @pl.loop(1, here.peers)
    def _(k):
        greet({"tensor": here.peer(k)})

    greet(here.partner())
    if ring:

        @pl.loop(1, here.chips)
        def _(k):
            greet(here.at(k))

        count = here.chips - 1
    else:
        greet(here.at(1))
        greet(here.at(-1))
        count = 2
    pl.semaphore_wait(barrier, here.peers - 1 + 1 + count)


def offset_of(n):
    return ((n + 1) // 2) * (2 * (n % 2) - 1)


def rows16(ref, chip, core, sub=None):
    start = 32 * chip + 16 * core
    if sub is None:
        return ref.at[pl.ds(pl.multiple_of(start, 16), 16)]
    return ref.at[pl.ds(pl.multiple_of(start + 8 * sub, 8), 8)]


class Gather:
    def __init__(self, here, buf, send, recv, pair_recv):
        self.here, self.buf = here, buf
        self.send, self.recv, self.pair_recv = send, recv, pair_recv
        self.half = here.chips // 2

    def forward(self, step, way, sub):
        here, sign = self.here, 1 - 2 * way
        ref = rows16(self.buf, here.chip(-sign * (step - 1)), here.c, sub)
        remote(
            ref, ref, self.send, self.recv.at[way, step - 1, sub], here.at(sign)
        ).start()

    def share(self, offset, slot):
        here = self.here
        ref = rows16(self.buf, here.chip(offset), here.c)
        remote(ref, ref, self.send, self.pair_recv.at[slot], here.partner()).start()

    def begin(self):
        for sub in (0, 1):
            for way in (0, 1):
                self.forward(1, way, sub)
        self.share(0, 0)

    def step(self, step, sub):
        here = self.here

        def take(way, last):
            sign = 1 - 2 * way
            ref = rows16(self.buf, here.chip(-sign * step), here.c, sub)
            await_bytes(ref, self.recv.at[way, step - 1, sub])

            @pl.when(step < self.half - last)
            def _():
                self.forward(step + 1, way, sub)

        take(sub, 0)

        @pl.when(step < self.half)
        def _():
            take(1 - sub, 1)

        @pl.when(sub == 1)
        def _():
            self.share(step, 2 * step - 1)

            @pl.when(step < self.half)
            def _():
                self.share(-step, 2 * step)

    def shared(self, n):
        here = self.here
        ref = rows16(self.buf, here.chip(offset_of(n)), 1 - here.c)
        await_bytes(ref, self.pair_recv.at[n])

    def end(self):
        rows = 16 * (2 * self.here.chips - 1)
        await_bytes(self.buf.at[pl.ds(0, rows)], self.send)


def split(value):
    high = value.astype(jnp.bfloat16)
    return high, (value - high.astype(jnp.float32)).astype(jnp.bfloat16)


def dot3(a, b, dims):
    return (
        dot(a[0], b[0], dims, None) + dot(a[0], b[1], dims, None)
    ) + dot(a[1], b[0], dims, None)


def splat(value):
    return jnp.broadcast_to(value, (8, 128))


def eliminate(turn, carry, w_ref):
    s = carry
    lane = lax.broadcasted_iota(jnp.int32, (8, 128), 1)
    sublane = lax.broadcasted_iota(jnp.int32, (8, 128), 0)
    for half in (0, 8):
        block = (lane >= half) & (lane < half + 8)
        columns = [
            jnp.broadcast_to(s[:, half + j : half + j + 1], s.shape) for j in range(8)
        ]
        d = {
            (i, j): splat(columns[j][i : i + 1, :]) for j in range(8) for i in range(j, 8)
        }
        top = jnp.where(block, jnp.where(lane == sublane + half, 1.0, 0.0), s[0:8])
        r = [splat(top[i : i + 1, :]) for i in range(8)]
        root, inverse, t = [], [], {}
        for k in range(8):
            root.append(lax.rsqrt(d[k, k]))
            inverse.append(root[k] * root[k])
            for i in range(k + 1, 8):
                t[i, k] = d[i, k] * inverse[k]
                for j in range(k + 1, i + 1):
                    d[i, j] = d[i, j] - t[i, k] * d[j, k]
                r[i] = r[i] - t[i, k] * r[k]
        done = r[0] * root[0]
        for k in range(1, 8):
            done = jnp.where(sublane == k, r[k] * root[k], done)
        keep = (lane >= 128 - 16 * turn) | (lane < half + 8)
        w_ref[pl.ds(pl.multiple_of(16 * turn + half, 8), 8), :] = jnp.where(
            keep, done, 0.0
        )
        for k in range(7, -1, -1):
            r[k] = r[k] * inverse[k]
            for i in range(7, k, -1):
                r[k] = r[k] - t[i, k] * r[i]
        lanes = lax.broadcasted_iota(jnp.int32, (s.shape[0] - 8, 128), 1)
        s = jnp.where((lanes >= half) & (lanes < half + 8), 0.0, s[8:])
        for j in range(8):
            s = s - columns[j][8:] * r[j][0:1, :]
    blank = jnp.zeros((16, 128), jnp.float32)
    return pltpu.roll(jnp.concatenate([s, blank], axis=0), 112, 1)


def invert_factor(m_ref, block_ref, wsplit, between):
    rank = m_ref.shape[0]

    @pl.loop(0, rank // 128)
    def _(panel):
        here = pl.ds(pl.multiple_of(128 * panel, 128), 128)

        def some(i, carry):
            carry = eliminate(i, carry, block_ref)

            @pl.when(lax.rem(i, 4) < 3)
            def _():
                between(6 * panel + i - i // 4)

            return carry

        lax.fori_loop(0, 8, some, m_ref[here, here])
        w = jnp.concatenate(
            [block_ref[0:16, :]]
            + [pltpu.roll(block_ref[16 * i : 16 * i + 16, :], 16 * i, 1) for i in range(1, 8)],
            axis=0,
        )
        m_ref[here, :] = dot(w, m_ref[here, :], NN, HIGHEST)
        m_ref[here, here] = w

        @pl.when(panel < rank // 128 - 1)
        def _():
            rows = lax.broadcasted_iota(jnp.int32, (rank, 128), 0)
            below = rows >= 128 * panel + 128
            lower = jnp.where(below, m_ref[here, :].T, 0.0)
            m_ref[:, here] = jnp.where(below, 0.0, m_ref[:, here])
            m_ref[...] = m_ref[...] - dot(lower, m_ref[here, :], NN, HIGHEST)

        lanes = lax.broadcasted_iota(jnp.int32, (128, rank), 1)
        wsplit[0, here, :], wsplit[1, here, :] = split(
            jnp.where(lanes < 128 * panel + 128, m_ref[here, :], 0.0)
        )


def column_tiles(columns):
    return [(at, min(256, columns - at)) for at in range(0, columns, 256)]


def kernel(
    chips,
    peers,
    scale,
    mean,
    gain,
    b_ref,
    f_ref,
    qlow_ref,
    qtwice_ref,
    qrest_ref,
    rsplit,
    factor_ref,
    bsplit,
    tsplit,
    fall,
    fsplit,
    part,
    first_parts,
    last_parts,
    arrived,
    pt,
    psplit,
    gpart,
    gpair,
    gsplit,
    gsplits,
    gsums,
    gram,
    m_ref,
    block_ref,
    wsplit,
    rpart,
    rpair,
    moving,
    rall,
    sums,
    squares,
    f_send,
    f_recv,
    f_pair,
    p_send,
    p_recv,
    g_send,
    g_recv,
    pair_send,
    pair_recv,
    rs_send,
    rs_recv,
    ag_send,
    ag_recv,
    ag_pair,
    sq_send,
    sq_recv,
):
    here = Place(chips, peers)
    rank = 32 * chips
    ring = chips // 2
    groups = chips // 4
    last = groups - 1
    tiles = column_tiles(b_ref.shape[1])
    own = rows16(fall, here.z, here.c)
    own[...] = f_ref[...]
    enter(here, True)
    gather = Gather(here, fall, f_send, f_recv, f_pair)
    gather.begin()

    def tile(i):
        return pl.ds(pl.multiple_of(128 * i, 128), 128)

    count = b_ref.shape[1] // 128

    def transpose(quarter):
        low, high = quarter * count // 4, (quarter + 1) * count // 4

        @pl.loop(low, high)
        def _(i):
            tsplit[0, tile(i), :], tsplit[1, tile(i), :] = split(b_ref[:, tile(i)].T)

    def straight(low, high):
        @pl.loop(low, high)
        def _(i):
            bsplit[0, :, tile(i)], bsplit[1, :, tile(i)] = split(b_ref[:, tile(i)])

    def join(g):
        order = [4 * g + n for n in range(4)]
        for n in order:
            gather.shared(n)
        rows = [
            fall[pl.ds(pl.multiple_of(32 * here.chip(offset_of(n)), 32), 32), :]
            for n in order
        ]
        fsplit[0], fsplit[1] = split(jnp.concatenate(rows, axis=0))

    def product(g, turn):
        rows = tile(g)
        one = dot(fsplit[turn // 2], tsplit[turn % 2], NN, None)
        part[rows, :] = part[rows, :] + one if turn else one

    def spread(base, rows, parts, turn):
        piece = rows // peers

        @pl.loop(1, peers)
        def _(k):
            other = here.peer(k)
            start = pl.multiple_of(base + piece * other, 8)
            remote(
                part.at[pl.ds(start, piece)],
                parts.at[k],
                p_send.at[turn],
                p_recv.at[turn],
                {"tensor": other},
            ).start()

    def total(base, rows, parts, turn):
        piece = rows // peers
        mine = pl.ds(pl.multiple_of(base + piece * here.t, 8), piece)
        parts[0] = part[mine, :]
        await_bytes(parts.at[pl.ds(1, peers - 1)], p_recv.at[turn])
        arrived[mine, :] = jnp.sum(parts[...], axis=0) * scale

        @pl.loop(1, peers)
        def _(k):
            place = arrived.at[mine]
            remote(
                place,
                place,
                p_send.at[turn + 1],
                p_recv.at[turn + 1],
                {"tensor": here.peer(k)},
            ).start()

    early = 128 * last

    def piece(g, i):
        if i == 0:
            join(g)
        else:
            product(g, i - 1)

    @pl.loop(0, groups)
    def _(g):
        for i in range(4):
            gather.step(2 * g + 1 + i // 2, i % 2)

            @pl.when(g == 0)
            def _():
                transpose(i)

            @pl.when(g > 0)
            def _():
                piece(g - 1, i)

    if last:
        spread(0, early, first_parts, 0)
    for i in range(4):
        piece(last, i)
    spread(early, 128, last_parts, 2)
    if last:
        total(0, early, first_parts, 0)
    straight(0, count // 2)
    total(early, 128, last_parts, 2)
    straight(count // 2, count)
    if last:
        await_bytes(first_parts.at[pl.ds(1, peers - 1)], p_recv.at[1])
    await_bytes(last_parts.at[pl.ds(1, peers - 1)], p_recv.at[3])

    @pl.loop(0, chips)
    def _(n):
        place = pl.ds(pl.multiple_of(32 * here.chip(offset_of(n)), 32), 32)
        pt[place, :] = arrived[pl.ds(pl.multiple_of(32 * n, 32), 32), :]

    def right_product(g):
        chipped = [here.chip(offset_of(4 * g + n)) for n in range(4)]
        p = split(arrived[tile(g), :])
        for at, width in tiles:
            b = (bsplit[0, :, at : at + width], bsplit[1, :, at : at + width])
            r = dot3(p, b, NN)
            for n, i in enumerate(chipped):
                place = pl.ds(pl.multiple_of(32 * i, 32), 32)
                rpart[place, at : at + width] = r[32 * n : 32 * n + 32, :]
        for n, i in enumerate(chipped):
            remote(
                rows16(rpart, i, 1 - here.c),
                rpair.at[4 * g + n],
                pair_send,
                pair_recv.at[g],
                here.partner(),
            ).start()

    def half_rows(sub):
        return pl.ds(pl.multiple_of(8 * sub, 8), 8)

    def right_own(n, sub):
        chip = here.chip(offset_of(n))
        return rows16(rpart, chip, here.c, sub)[...] + rpair[n, half_rows(sub), :]

    def scatter(k, sub):
        def pass_on(way, come):
            place = moving.at[way, k, half_rows(sub)]
            n = 2 * k - 1 + way * (1 - 2 * k // chips)

            @pl.when(come)
            def _():
                await_bytes(place, rs_recv.at[way, k, sub])
                place[...] = place[...] + right_own(n, sub)

            @pl.when(jnp.logical_not(come))
            def _():
                place[...] = right_own(n, sub)

            remote(
                place,
                moving.at[way, k - 1, half_rows(sub)],
                rs_send,
                rs_recv.at[way, k - 1, sub],
                here.at(1 - 2 * way),
            ).start()

        pass_on(sub, k < ring)

        @pl.when(k < ring)
        def _():
            pass_on(1 - sub, k < ring - 1)

    collect = Gather(here, rall, ag_send, ag_recv, ag_pair)

    def settle():
        for sub in (0, 1):
            for way in (0, 1):
                place = moving.at[way, 0, pl.ds(8 * sub, 8)]
                await_bytes(place, rs_recv.at[way, 0, sub])
            rows16(rall, here.z, here.c, sub)[...] = (
                right_own(0, sub)
                + moving[0, 0, 8 * sub : 8 * sub + 8, :]
                + moving[1, 0, 8 * sub : 8 * sub + 8, :]
            )
        collect.begin()

    def halve(n):
        collect.shared(n)
        place = pl.ds(pl.multiple_of(32 * here.chip(offset_of(n)), 32), 32)
        rsplit[0, place, :], rsplit[1, place, :] = split(rall[place, :])

    def onward(step, sub):
        collect.step(step, sub)

        @pl.when(2 * step - 3 + sub >= 0)
        def _():
            halve(2 * step - 3 + sub)

    block = rank // peers
    half = block // 2
    each = half // chips
    mine = pl.ds(pl.multiple_of(block * here.t, block), block)
    theirs = pl.ds(pl.multiple_of(half * (1 - here.c), half), half)
    keep = pl.ds(pl.multiple_of(half * here.c, half), half)

    def gram_pair():
        return remote(
            gpart.at[theirs], gpair, g_send.at[0], g_recv.at[0], here.partner()
        )

    def gram_own():
        gpart[...] = dot(pt[mine, :], pt[...].T, NN, HIGHEST)
        gram_pair().start()

    def gram_scatter():
        gram_pair().wait()
        chip_sum = gpart[keep, :] + gpair[...]
        for k in range(chips):
            gsplit[k] = chip_sum[each * k : each * (k + 1), :]

        @pl.loop(1, chips)
        def _(k):
            remote(
                gsplit.at[here.chip(k)],
                gsplits.at[k],
                g_send.at[1],
                g_recv.at[1],
                here.at(k),
            ).start()

        gsplits[0] = gsplit[here.z]

    def gram_gather():
        await_bytes(gsplits.at[pl.ds(1, chips - 1)], g_recv.at[1])
        gsums[here.z] = jnp.sum(gsplits[...], axis=0)

        @pl.loop(1, chips)
        def _(k):
            place = gsums.at[here.z]
            remote(place, place, g_send.at[2], g_recv.at[2], here.at(k)).start()

    def gram_spread():
        await_bytes(gsums.at[pl.ds(0, chips - 1)], g_recv.at[2])
        gram[here.t, here.c] = gsums[...].reshape(half, rank)

        @pl.loop(1, peers)
        def _(k):
            place = gram.at[here.t, here.c]
            remote(
                place, place, g_send.at[3], g_recv.at[3], {"tensor": here.peer(k)}
            ).start()

    gram_steps = (gram_scatter, gram_gather, gram_spread)

    def paired(g):
        await_bytes(rpair.at[pl.ds(4 * g, 4)], pair_recv.at[g])

    gram_own()

    @pl.loop(0, groups)
    def _(turn):
        right_product(last - turn)
        for i, step in enumerate(gram_steps):
            if i < groups:

                @pl.when(turn == i)
                def _():
                    step()

        @pl.when(lax.rem(turn, 2) == 0)
        def _():
            paired(last - turn // 2)

        for sub in (0, 1):
            scatter(ring - turn, sub)

    for i, step in enumerate(gram_steps):
        if i >= groups:
            step()
    for g in range(last - (groups + 1) // 2, -1, -1):
        paired(g)
    await_bytes(gram.at[pl.ds(0, peers - 1), 0], g_recv.at[3])
    halves = gram.at[:, here.c]
    pair = remote(halves, halves, g_send.at[4], g_recv.at[4], here.partner())
    pair.start()
    for sub in (0, 1):
        scatter(groups, sub)
    psplit[0], psplit[1] = split(pt[...])
    pair.wait()
    m_ref[...] = gram[...].reshape(rank, rank)

    def between(n):
        sub = lax.rem(n, 2)

        @pl.when(n < 2 * last)
        def _():
            scatter(last - n // 2, sub)

        @pl.when(n == 2 * last)
        def _():
            settle()

        left = n - 2 * last - 1

        @pl.when((left >= 0) & (left < 2 * ring))
        def _():
            onward(left // 2 + 1, 1 - sub)

    invert_factor(m_ref, block_ref, wsplit, between)
    halve(chips - 1)

    sums[...] = jnp.zeros_like(sums)

    def right_tile(at, width):
        columns = pl.ds(at, width)
        blocks = []
        for row in range(0, rank, 256):
            stop = row + 256
            blocks.append(
                dot3(
                    (wsplit[0, row:stop, 0:stop], wsplit[1, row:stop, 0:stop]),
                    (rsplit[0, 0:stop, columns], rsplit[1, 0:stop, columns]),
                    NN,
                )
            )
        right = jnp.concatenate(blocks, axis=0)
        for lane in range(0, width, 128):
            one = right[:, lane : lane + 128]
            sums[...] = sums[...] + one * one
        rsplit[0, :, columns], rsplit[1, :, columns] = split(right)

    full = 256 * (b_ref.shape[1] // 256)

    @pl.loop(0, full // 256)
    def _(i):
        right_tile(pl.multiple_of(256 * i, 256), 256)

    if full < b_ref.shape[1]:
        right_tile(full, b_ref.shape[1] - full)
    squares[0] = jnp.sum(sums[...].T, axis=0, keepdims=True)

    @pl.loop(1, peers)
    def _(k):
        remote(
            squares.at[0], squares.at[k], sq_send, sq_recv, {"tensor": here.peer(k)}
        ).start()

    blocks = []
    for row in range(0, rank, 256):
        stop = row + 256
        blocks.append(
            dot3(
                (wsplit[0, row:stop, 0:stop], wsplit[1, row:stop, 0:stop]),
                (psplit[0, 0:stop, :], psplit[1, 0:stop, :]),
                NN,
            )
        )
    q = jnp.concatenate(blocks, axis=0).T
    qlow_ref[...] = (q * -0.05).astype(jnp.bfloat16)
    await_bytes(squares.at[pl.ds(1, peers - 1)], sq_recv)
    scales = lax.rsqrt(jnp.sum(squares[...], axis=0) * mean + 1e-06)
    high, qrest_ref[...] = split(q * (scales * gain))
    qtwice_ref[:, 0:rank] = high
    qtwice_ref[:, rank : 2 * rank] = high
    lanes = lax.broadcasted_iota(jnp.int32, (32, rank), 1)
    rows = lax.broadcasted_iota(jnp.int32, (32, rank), 0) + 32 * here.z
    picked = jnp.where(lanes == rows, jnp.broadcast_to(scales, (32, rank)), 0.0)
    place = pl.ds(pl.multiple_of(32 * here.z, 32), 32)
    ours = (
        rsplit[0, place, :].astype(jnp.float32) + rsplit[1, place, :].astype(jnp.float32)
    ) * jnp.sum(picked, axis=1, keepdims=True)
    factor_ref[...] = jnp.where(here.c == 0, ours[0:16], ours[16:32])

    gather.end()
    collect.end()
    if last:
        for turn in (0, 1):
            await_bytes(first_parts.at[pl.ds(1, peers - 1)], p_send.at[turn])
    for turn in (2, 3):
        await_bytes(last_parts.at[pl.ds(1, peers - 1)], p_send.at[turn])
    await_bytes(gsplits.at[pl.ds(1, chips - 1)], g_send.at[1])
    await_bytes(gsums.at[pl.ds(0, chips - 1)], g_send.at[2])
    await_bytes(gram.at[pl.ds(0, peers - 1), 0], g_send.at[3])
    await_bytes(rpart.at[pl.ds(0, rank // 2)], pair_send)
    await_bytes(rall.at[pl.ds(0, 16 * (chips - 1))], rs_send)
    await_bytes(squares.at[pl.ds(1, peers - 1)], sq_send)


def finish(
    b_ref, qlow_ref, qtwice_ref, qrest_ref, r_ref, f_ref, momentum_ref, update_ref, factor_ref
):
    high = r_ref[0 : qlow_ref.shape[1], :]
    momentum_ref[...] = b_ref[...] + dot(qlow_ref[...], high, NN, None)
    update = dot(qtwice_ref[...], r_ref[...], NN, None) + dot(qrest_ref[...], high, NN, None)
    update_ref[...] = update.astype(jnp.bfloat16)
    factor_ref[...] = f_ref[...]


def body(chips, peers, buffer, factor):
    rows, columns = buffer.shape
    rank = 32 * chips
    half = rank // peers // 2
    each = half // chips
    total_columns = columns * peers
    groups = chips // 4
    ring = chips // 2
    f32, bf16 = jnp.float32, jnp.bfloat16
    dma = pltpu.SemaphoreType.DMA
    vmem = pl.BlockSpec(memory_space=pltpu.VMEM)
    qlow, qtwice, qrest, rsplit, factor_t = pl.pallas_call(
        functools.partial(
            kernel,
            chips,
            peers,
            1.0 / math.sqrt(total_columns),
            1.0 / total_columns,
            math.sqrt(rows * 2 * chips / rank),
        ),
        out_shape=(
            jax.ShapeDtypeStruct((rows, rank), bf16),
            jax.ShapeDtypeStruct((rows, 2 * rank), bf16),
            jax.ShapeDtypeStruct((rows, rank), bf16),
            jax.ShapeDtypeStruct((2, rank, columns), bf16),
            jax.ShapeDtypeStruct((16, columns), f32),
        ),
        in_specs=[vmem] * 2,
        out_specs=(vmem,) * 5,
        scratch_shapes=[
            pltpu.VMEM((2, rows, columns), bf16),
            pltpu.VMEM((2, columns, rows), bf16),
            pltpu.VMEM((rank, columns), f32),
            pltpu.VMEM((2, 128, columns), bf16),
            pltpu.VMEM((rank, rows), f32),
            pltpu.VMEM((peers, max(groups - 1, 1) * 128 // peers, rows), f32),
            pltpu.VMEM((peers, 128 // peers, rows), f32),
            pltpu.VMEM((rank, rows), f32),
            pltpu.VMEM((rank, rows), f32),
            pltpu.VMEM((2, rank, rows), bf16),
            pltpu.VMEM((2 * half, rank), f32),
            pltpu.VMEM((half, rank), f32),
            pltpu.VMEM((chips, each, rank), f32),
            pltpu.VMEM((chips, each, rank), f32),
            pltpu.VMEM((chips, each, rank), f32),
            pltpu.VMEM((peers, 2, half, rank), f32),
            pltpu.VMEM((rank, rank), f32),
            pltpu.VMEM((128, 128), f32),
            pltpu.VMEM((2, rank, rank), bf16),
            pltpu.VMEM((rank, columns), f32),
            pltpu.VMEM((chips, 16, columns), f32),
            pltpu.VMEM((2, ring + 1, 16, columns), f32),
            pltpu.VMEM((rank, columns), f32),
            pltpu.VMEM((rank, 128), f32),
            pltpu.VMEM((peers, 1, rank), f32),
            dma,
            dma((2, ring, 2)),
            dma((chips,)),
            dma((4,)),
            dma((4,)),
            dma((5,)),
            dma((5,)),
            dma,
            dma((groups,)),
            dma,
            dma((2, ring, 2)),
            dma,
            dma((2, ring, 2)),
            dma((chips,)),
            dma,
            dma,
        ],
        compiler_params=pltpu.CompilerParams(
            collective_id=0, has_side_effects=True, vmem_limit_bytes=LIMIT
        ),
        name="low_rank_update",
    )(buffer, factor.T)

    def whole(*shape):
        return pl.BlockSpec(shape, lambda i: (0,) * len(shape))

    def tile(*lead):
        return pl.BlockSpec((*lead, 256), lambda i: (0,) * len(lead) + (i,))

    momentum, update, factor_t = pl.pallas_call(
        finish,
        grid=(pl.cdiv(columns, 256),),
        out_shape=(
            jax.ShapeDtypeStruct((rows, columns), f32),
            jax.ShapeDtypeStruct((rows, columns), bf16),
            jax.ShapeDtypeStruct((16, columns), f32),
        ),
        in_specs=[
            tile(rows),
            whole(rows, rank),
            whole(rows, 2 * rank),
            whole(rows, rank),
            tile(2 * rank),
            tile(16),
        ],
        out_specs=(tile(rows), tile(rows), tile(16)),
        compiler_params=pltpu.CompilerParams(vmem_limit_bytes=LIMIT),
        name="finish",
    )(buffer, qlow, qtwice, qrest, rsplit.reshape(2 * rank, columns), factor_t)
    return momentum, update, factor_t.T


def solution(mesh):
    chips, peers = mesh.shape["dp"] // 2, mesh.shape["tensor"]
    placed = (P("dp", "tensor"), P("tensor", "dp"))
    return jax.shard_map(
        functools.partial(body, chips, peers),
        mesh=mesh,
        in_specs=placed,
        out_specs=(P("dp", "tensor"), P("dp", "tensor"), P("tensor", "dp")),
        check_vma=False,
    )
```

```python
import functools
import math

import jax
import jax.numpy as jnp
from jax import lax
from jax.experimental import pallas as pl
from jax.experimental.pallas import tpu as pltpu
from jax.sharding import PartitionSpec as P

MESH = pl.DeviceIdType.MESH
HIGHEST = lax.Precision.HIGHEST
NN = (((1,), (0,)), ((), ()))
LIMIT = 56 * 1024 * 1024


def dot(a, b, dims, precision):
    return lax.dot_general(
        a, b, dims, precision=precision, preferred_element_type=jnp.float32
    )


class Place:
    def __init__(self, chips, peers):
        dp = lax.axis_index("dp")
        self.z, self.c = dp // 2, dp % 2
        self.t = lax.axis_index("tensor")
        self.chips, self.peers = chips, peers
        self.next = {"dp": 2 * self.chip(1) + self.c}
        self.back = {"dp": 2 * self.chip(-1) + self.c}
        self.other = {"dp": 2 * self.z + 1 - self.c}

    def chip(self, offset):
        return lax.rem(self.z + offset + self.chips, self.chips)

    def at(self, offset):
        return {"dp": 2 * self.chip(offset) + self.c}

    def partner(self):
        return self.other

    def neighbour(self, way):
        return self.back if way else self.next

    def peer(self, k):
        return lax.rem(self.t + k, self.peers)


def remote(src, dst, send, recv, device):
    return pltpu.make_async_remote_copy(
        src_ref=src,
        dst_ref=dst,
        send_sem=send,
        recv_sem=recv,
        device_id=device,
        device_id_type=MESH,
    )


def await_bytes(ref, sem):
    pltpu.make_async_copy(ref, ref, sem).wait()


def enter(here, ring):
    barrier = pltpu.get_barrier_semaphore()

    def greet(device):
        pl.semaphore_signal(barrier, inc=1, device_id=device, device_id_type=MESH)

    @pl.loop(1, here.peers)
    def _(k):
        greet({"tensor": here.peer(k)})

    greet(here.partner())
    if ring:

        @pl.loop(1, here.chips)
        def _(k):
            greet(here.at(k))

        count = here.chips - 1
    else:
        greet(here.at(1))
        greet(here.at(-1))
        count = 2
    pl.semaphore_wait(barrier, here.peers - 1 + 1 + count)


def offset_of(n):
    return ((n + 1) // 2) * (2 * (n % 2) - 1)


def rows16(ref, chip, core, sub=None):
    start = 32 * chip + 16 * core
    if sub is None:
        return ref.at[pl.ds(pl.multiple_of(start, 16), 16)]
    return ref.at[pl.ds(pl.multiple_of(start + 8 * sub, 8), 8)]


def lane_parts(columns, count):
    tiles = columns // 128
    cuts = [128 * (tiles * i // count) for i in range(count + 1)]
    return [pl.ds(a, b - a) for a, b in zip(cuts, cuts[1:]) if b > a]


class Gather:
    def __init__(self, here, buf, parts, send, recv, pair_recv):
        self.here, self.buf, self.parts = here, buf, parts
        self.send, self.recv, self.pair_recv = send, recv, pair_recv
        self.half = here.chips // 2

    def forward(self, step, way, sub, h):
        here, sign = self.here, 1 - 2 * way
        rows = rows16(self.buf, here.chip(-sign * (step - 1)), here.c, sub)
        ref = rows.at[:, self.parts[h]]
        recv = self.recv.at[way, step - 1, 2 * sub + h]
        remote(ref, ref, self.send, recv, here.neighbour(way)).start()

    def share(self, offset, slot):
        here = self.here
        ref = rows16(self.buf, here.chip(offset), here.c)
        remote(ref, ref, self.send, self.pair_recv.at[slot], here.partner()).start()

    def begin(self):
        for sub in (0, 1):
            for h in range(len(self.parts)):
                for way in (0, 1):
                    self.forward(1, way, sub, h)
        self.share(0, 0)

    def step(self, step, sub):
        here = self.here

        def take(way, h):
            sign = 1 - 2 * way
            rows = rows16(self.buf, here.chip(-sign * step), here.c, sub)
            await_bytes(
                rows.at[:, self.parts[h]], self.recv.at[way, step - 1, 2 * sub + h]
            )

            @pl.when(step + 1 < self.half + (sub == way))
            def _():
                self.forward(step + 1, way, sub, h)

        for h in range(len(self.parts)):
            take(sub, h)

            @pl.when(step < self.half)
            def _():
                take(1 - sub, h)

        if sub == 1:
            self.share(step, 2 * step - 1)

            @pl.when(step < self.half)
            def _():
                self.share(-step, 2 * step)

    def shared(self, n):
        here = self.here
        ref = rows16(self.buf, here.chip(offset_of(n)), 1 - here.c)
        await_bytes(ref, self.pair_recv.at[n])

    def end(self):
        rows = 16 * (2 * self.here.chips - 1)
        await_bytes(self.buf.at[pl.ds(0, rows)], self.send)


def split(value):
    high = value.astype(jnp.bfloat16)
    return high, (value - high.astype(jnp.float32)).astype(jnp.bfloat16)


def dot3(a, b, dims):
    return (
        dot(a[0], b[0], dims, None) + dot(a[0], b[1], dims, None)
    ) + dot(a[1], b[0], dims, None)


def splat(value):
    return jnp.broadcast_to(value, (8, 128))


def eliminate(turn, carry, w_ref):
    s = carry
    lane = lax.broadcasted_iota(jnp.int32, (8, 128), 1)
    sublane = lax.broadcasted_iota(jnp.int32, (8, 128), 0)
    for half in (0, 8):
        block = (lane >= half) & (lane < half + 8)
        columns = [
            jnp.broadcast_to(s[:, half + j : half + j + 1], s.shape) for j in range(8)
        ]
        d = {
            (i, j): splat(columns[j][i : i + 1, :]) for j in range(8) for i in range(j, 8)
        }
        top = jnp.where(block, jnp.where(lane == sublane + half, 1.0, 0.0), s[0:8])
        r = [splat(top[i : i + 1, :]) for i in range(8)]
        root, inverse, t = [], [], {}
        for k in range(8):
            root.append(lax.rsqrt(d[k, k]))
            inverse.append(root[k] * root[k])
            for i in range(k + 1, 8):
                t[i, k] = d[i, k] * inverse[k]
                for j in range(k + 1, i + 1):
                    d[i, j] = d[i, j] - t[i, k] * d[j, k]
                r[i] = r[i] - t[i, k] * r[k]
        done = r[0] * root[0]
        for k in range(1, 8):
            done = jnp.where(sublane == k, r[k] * root[k], done)
        keep = (lane >= 128 - 16 * turn) | (lane < half + 8)
        w_ref[pl.ds(pl.multiple_of(16 * turn + half, 8), 8), :] = jnp.where(
            keep, done, 0.0
        )
        for k in range(7, -1, -1):
            r[k] = r[k] * inverse[k]
            for i in range(7, k, -1):
                r[k] = r[k] - t[i, k] * r[i]
        lanes = lax.broadcasted_iota(jnp.int32, (s.shape[0] - 8, 128), 1)
        s = jnp.where((lanes >= half) & (lanes < half + 8), 0.0, s[8:])
        for j in range(8):
            s = s - columns[j][8:] * r[j][0:1, :]
    blank = jnp.zeros((16, 128), jnp.float32)
    return pltpu.roll(jnp.concatenate([s, blank], axis=0), 112, 1)


def invert_factor(m_ref, block_ref, wsplit, between):
    rank = m_ref.shape[0]

    @pl.loop(0, rank // 128)
    def _(panel):
        here = pl.ds(pl.multiple_of(128 * panel, 128), 128)

        def half(i, carry):
            for sub in (0, 1):
                first = 4 * i + 2 * sub
                carry = lax.fori_loop(
                    first,
                    first + 2,
                    functools.partial(eliminate, w_ref=block_ref),
                    carry,
                )
                between(2 * panel + i + 1, sub)
            return carry

        lax.fori_loop(0, 2, half, m_ref[here, here])
        w = jnp.concatenate(
            [block_ref[0:16, :]]
            + [pltpu.roll(block_ref[16 * i : 16 * i + 16, :], 16 * i, 1) for i in range(1, 8)],
            axis=0,
        )
        m_ref[here, :] = dot(w, m_ref[here, :], NN, HIGHEST)
        m_ref[here, here] = w

        for last in range(rank // 128 - 1):

            @pl.when(panel == last)
            def _():
                start, stop = 128 * last, 128 * last + 128
                lower = m_ref[start:stop, stop:rank].T
                m_ref[stop:rank, start:stop] = jnp.zeros((rank - stop, 128), jnp.float32)
                m_ref[stop:rank, :] = m_ref[stop:rank, :] - dot(
                    lower, m_ref[start:stop, :], NN, HIGHEST
                )

        lanes = lax.broadcasted_iota(jnp.int32, (128, rank), 1)
        wsplit[0, here, :], wsplit[1, here, :] = split(
            jnp.where(lanes < 128 * panel + 128, m_ref[here, :], 0.0)
        )


def column_tiles(columns):
    return [(at, min(256, columns - at)) for at in range(0, columns, 256)]


def kernel(
    chips,
    peers,
    scale,
    mean,
    gain,
    b_hbm,
    f_ref,
    qlow_ref,
    qsplit_ref,
    r_hbm,
    factor_ref,
    b_ref,
    rsplit,
    bsplit,
    tsplit,
    fall,
    fsplit,
    part,
    first_parts,
    last_parts,
    arrived,
    pt,
    psplit,
    gpart,
    gpair,
    gsplit,
    gsplits,
    gsums,
    gram,
    m_ref,
    block_ref,
    wsplit,
    rpart,
    rpair,
    moving,
    rall,
    sums,
    squares,
    f_send,
    f_recv,
    f_pair,
    p_send,
    p_recv,
    g_send,
    g_recv,
    pair_send,
    pair_recv,
    rs_send,
    rs_recv,
    ag_send,
    ag_recv,
    ag_pair,
    sq_send,
    sq_recv,
    in_sem,
    out_sem,
):
    here = Place(chips, peers)
    rank = 32 * chips
    ring = chips // 2
    groups = chips // 4
    last = groups - 1
    tiles = column_tiles(b_ref.shape[1])
    load = pltpu.make_async_copy(b_hbm, b_ref, in_sem)
    load.start()
    own = rows16(fall, here.z, here.c)
    own[...] = f_ref[...]
    enter(here, True)
    halves = lane_parts(b_ref.shape[1], 2)
    gather = Gather(here, fall, halves, f_send, f_recv, f_pair)
    gather.begin()
    load.wait()

    def tile(i):
        return pl.ds(pl.multiple_of(128 * i, 128), 128)

    count = b_ref.shape[1] // 128

    def transpose(quarter):
        low, high = quarter * count // 4, (quarter + 1) * count // 4

        @pl.loop(low, high)
        def _(i):
            tsplit[0, tile(i), :], tsplit[1, tile(i), :] = split(b_ref[:, tile(i)].T)

    def straight(low, high):
        @pl.loop(low, high)
        def _(i):
            bsplit[0, :, tile(i)], bsplit[1, :, tile(i)] = split(b_ref[:, tile(i)])

    def join(g):
        order = [4 * g + n for n in range(4)]
        for n in order:
            gather.shared(n)
        rows = [
            fall[pl.ds(pl.multiple_of(32 * here.chip(offset_of(n)), 32), 32), :]
            for n in order
        ]
        fsplit[0], fsplit[1] = split(jnp.concatenate(rows, axis=0))

    def product(g, turn):
        rows = tile(g)
        one = dot(fsplit[turn // 2], tsplit[turn % 2], NN, None)
        part[rows, :] = part[rows, :] + one if turn else one

    def spread(base, rows, parts, turn):
        piece = rows // peers

        @pl.loop(1, peers)
        def _(k):
            other = here.peer(k)
            start = pl.multiple_of(base + piece * other, 8)
            remote(
                part.at[pl.ds(start, piece)],
                parts.at[k],
                p_send.at[turn],
                p_recv.at[turn],
                {"tensor": other},
            ).start()

    def total(base, rows, parts, turn):
        piece = rows // peers
        mine = pl.ds(pl.multiple_of(base + piece * here.t, 8), piece)
        parts[0] = part[mine, :]
        await_bytes(parts.at[pl.ds(1, peers - 1)], p_recv.at[turn])
        arrived[mine, :] = jnp.sum(parts[...], axis=0) * scale

        @pl.loop(1, peers)
        def _(k):
            place = arrived.at[mine]
            remote(
                place,
                place,
                p_send.at[turn + 1],
                p_recv.at[turn + 1],
                {"tensor": here.peer(k)},
            ).start()

    early = 128 * last

    def piece(g, i):
        if i == 0:
            join(g)
        else:
            product(g, i - 1)

    @pl.loop(0, groups)
    def _(g):
        for i in range(4):
            gather.step(2 * g + 1 + i // 2, i % 2)

            @pl.when(g == 0)
            def _():
                transpose(i)

            @pl.when(g > 0)
            def _():
                piece(g - 1, i)

    if last:
        spread(0, early, first_parts, 0)
    for i in range(4):
        piece(last, i)
    spread(early, 128, last_parts, 2)
    if last:
        total(0, early, first_parts, 0)
    straight(0, count // 2)
    total(early, 128, last_parts, 2)
    straight(count // 2, count)
    if last:
        await_bytes(first_parts.at[pl.ds(1, peers - 1)], p_recv.at[1])
    await_bytes(last_parts.at[pl.ds(1, peers - 1)], p_recv.at[3])

    @pl.loop(0, chips)
    def _(n):
        place = pl.ds(pl.multiple_of(32 * here.chip(offset_of(n)), 32), 32)
        pt[place, :] = arrived[pl.ds(pl.multiple_of(32 * n, 32), 32), :]

    def right_product(g):
        chipped = [here.chip(offset_of(4 * g + n)) for n in range(4)]
        p = split(arrived[tile(g), :])
        for at, width in tiles:
            b = (bsplit[0, :, at : at + width], bsplit[1, :, at : at + width])
            r = dot3(p, b, NN)
            for n, i in enumerate(chipped):
                place = pl.ds(pl.multiple_of(32 * i, 32), 32)
                rpart[place, at : at + width] = r[32 * n : 32 * n + 32, :]
        for n, i in enumerate(chipped):
            remote(
                rows16(rpart, i, 1 - here.c),
                rpair.at[4 * g + n],
                pair_send,
                pair_recv.at[g],
                here.partner(),
            ).start()

    def right_own(n, sub, lanes):
        chip = here.chip(offset_of(n))
        rows = rows16(rpart, chip, here.c, sub)
        return rows[:, lanes] + rpair[n, 8 * sub : 8 * sub + 8, lanes]

    def scatter(k, sub):
        def pass_on(way, come, h):
            lanes = halves[h]
            place = moving.at[way, k, pl.ds(8 * sub, 8), lanes]
            n = 2 * k - 1 if way == 0 else 2 * k - 2 * k // chips

            @pl.when(come)
            def _():
                await_bytes(place, rs_recv.at[way, k, 2 * sub + h])
                place[...] = place[...] + right_own(n, sub, lanes)

            @pl.when(jnp.logical_not(come))
            def _():
                place[...] = right_own(n, sub, lanes)

            remote(
                place,
                moving.at[way, k - 1, pl.ds(8 * sub, 8), lanes],
                rs_send,
                rs_recv.at[way, k - 1, 2 * sub + h],
                here.neighbour(way),
            ).start()

        for h in range(len(halves)):
            pass_on(sub, k < ring, h)

            @pl.when(k < ring)
            def _():
                pass_on(1 - sub, k < ring - 1, h)

    collect = Gather(here, rall, lane_parts(b_ref.shape[1], 1), ag_send, ag_recv, ag_pair)

    def settle():
        for sub in (0, 1):
            for h, lanes in enumerate(halves):
                for way in (0, 1):
                    place = moving.at[way, 0, pl.ds(8 * sub, 8), lanes]
                    await_bytes(place, rs_recv.at[way, 0, 2 * sub + h])
                rows16(rall, here.z, here.c, sub)[:, lanes] = (
                    right_own(0, sub, lanes)
                    + moving[0, 0, 8 * sub : 8 * sub + 8, lanes]
                    + moving[1, 0, 8 * sub : 8 * sub + 8, lanes]
                )
        collect.begin()

    def halve(n):
        collect.shared(n)
        place = pl.ds(pl.multiple_of(32 * here.chip(offset_of(n)), 32), 32)
        rsplit[0, place, :], rsplit[1, place, :] = split(rall[place, :])

    def onward(step, sub):
        collect.step(step, sub)

        @pl.when(2 * step - 5 + sub >= 0)
        def _():
            halve(2 * step - 5 + sub)

    block = rank // peers
    half = block // 2
    each = half // chips
    mine = pl.ds(pl.multiple_of(block * here.t, block), block)
    theirs = pl.ds(pl.multiple_of(half * (1 - here.c), half), half)
    keep = pl.ds(pl.multiple_of(half * here.c, half), half)

    def gram_pair():
        return remote(
            gpart.at[theirs], gpair, g_send.at[0], g_recv.at[0], here.partner()
        )

    def gram_own():
        gpart[...] = dot(pt[mine, :], pt[...].T, NN, HIGHEST)
        gram_pair().start()

    def gram_scatter():
        gram_pair().wait()
        chip_sum = gpart[keep, :] + gpair[...]
        for k in range(chips):
            gsplit[k] = chip_sum[each * k : each * (k + 1), :]

        @pl.loop(1, chips)
        def _(k):
            remote(
                gsplit.at[here.chip(k)],
                gsplits.at[k],
                g_send.at[1],
                g_recv.at[1],
                here.at(k),
            ).start()

        gsplits[0] = gsplit[here.z]

    def gram_gather():
        await_bytes(gsplits.at[pl.ds(1, chips - 1)], g_recv.at[1])
        gsums[here.z] = jnp.sum(gsplits[...], axis=0)

        @pl.loop(1, chips)
        def _(k):
            place = gsums.at[here.z]
            remote(place, place, g_send.at[2], g_recv.at[2], here.at(k)).start()

    def gram_spread():
        await_bytes(gsums.at[pl.ds(0, chips - 1)], g_recv.at[2])
        gram[here.t, here.c] = gsums[...].reshape(half, rank)

        @pl.loop(1, peers)
        def _(k):
            place = gram.at[here.t, here.c]
            remote(
                place, place, g_send.at[3], g_recv.at[3], {"tensor": here.peer(k)}
            ).start()

    gram_steps = (gram_own, gram_scatter, gram_gather, gram_spread)

    @pl.loop(0, groups)
    def _(turn):
        g = last - turn
        right_product(g)
        for i, step in enumerate(gram_steps):
            if i < groups:

                @pl.when(turn == i)
                def _():
                    step()

        await_bytes(rpair.at[pl.ds(4 * g, 4)], pair_recv.at[g])
        for k in (2 * g + 2, 2 * g + 1):
            for sub in (0, 1):
                scatter(k, sub)

    for i, step in enumerate(gram_steps):
        if i >= groups:
            step()
    psplit[0], psplit[1] = split(pt[...])
    await_bytes(gram.at[pl.ds(0, peers - 1), 0], g_recv.at[3])
    ours = gram.at[:, here.c]
    pair = remote(ours, ours, g_send.at[4], g_recv.at[4], here.partner())
    pair.start()
    settle()
    pair.wait()
    m_ref[...] = gram[...].reshape(rank, rank)
    invert_factor(m_ref, block_ref, wsplit, onward)

    @pl.loop(chips - 3, chips)
    def _(n):
        halve(n)

    sums[...] = jnp.zeros_like(sums)

    def right_tile(at, width):
        columns = pl.ds(at, width)
        blocks = []
        for row in range(0, rank, 256):
            stop = row + 256
            blocks.append(
                dot3(
                    (wsplit[0, row:stop, 0:stop], wsplit[1, row:stop, 0:stop]),
                    (rsplit[0, 0:stop, columns], rsplit[1, 0:stop, columns]),
                    NN,
                )
            )
        right = jnp.concatenate(blocks, axis=0)
        for lane in range(0, width, 128):
            one = right[:, lane : lane + 128]
            sums[...] = sums[...] + one * one
        rsplit[0, :, columns], rsplit[1, :, columns] = split(right)
        pltpu.make_async_copy(
            rsplit.at[:, :, columns], r_hbm.at[:, :, columns], out_sem
        ).start()

    full = 256 * (b_ref.shape[1] // 256)

    @pl.loop(0, full // 256)
    def _(i):
        right_tile(pl.multiple_of(256 * i, 256), 256)

    if full < b_ref.shape[1]:
        right_tile(full, b_ref.shape[1] - full)
    squares[0] = jnp.sum(sums[...].T, axis=0, keepdims=True)

    @pl.loop(1, peers)
    def _(k):
        remote(
            squares.at[0], squares.at[k], sq_send, sq_recv, {"tensor": here.peer(k)}
        ).start()

    blocks = []
    for row in range(0, rank, 256):
        stop = row + 256
        blocks.append(
            dot3(
                (wsplit[0, row:stop, 0:stop], wsplit[1, row:stop, 0:stop]),
                (psplit[0, 0:stop, :], psplit[1, 0:stop, :]),
                NN,
            )
        )
    q = jnp.concatenate(blocks, axis=0).T
    qlow_ref[...] = (q * -0.05).astype(jnp.bfloat16)
    await_bytes(squares.at[pl.ds(1, peers - 1)], sq_recv)
    scales = lax.rsqrt(jnp.sum(squares[...], axis=0) * mean + 1e-06)
    qsplit_ref[0], qsplit_ref[1] = split(q * (scales * gain))
    lanes = lax.broadcasted_iota(jnp.int32, (32, rank), 1)
    rows = lax.broadcasted_iota(jnp.int32, (32, rank), 0) + 32 * here.z
    picked = jnp.where(lanes == rows, jnp.broadcast_to(scales, (32, rank)), 0.0)
    place = pl.ds(pl.multiple_of(32 * here.z, 32), 32)
    ours = (
        rsplit[0, place, :].astype(jnp.float32) + rsplit[1, place, :].astype(jnp.float32)
    ) * jnp.sum(picked, axis=1, keepdims=True)
    factor_ref[...] = jnp.where(here.c == 0, ours[0:16], ours[16:32])

    await_bytes(rsplit, out_sem)
    gather.end()
    collect.end()
    if last:
        for turn in (0, 1):
            await_bytes(first_parts.at[pl.ds(1, peers - 1)], p_send.at[turn])
    for turn in (2, 3):
        await_bytes(last_parts.at[pl.ds(1, peers - 1)], p_send.at[turn])
    await_bytes(gsplits.at[pl.ds(1, chips - 1)], g_send.at[1])
    await_bytes(gsums.at[pl.ds(0, chips - 1)], g_send.at[2])
    await_bytes(gram.at[pl.ds(0, peers - 1), 0], g_send.at[3])
    await_bytes(rpart.at[pl.ds(0, rank // 2)], pair_send)
    await_bytes(rall.at[pl.ds(0, 16 * (chips - 1))], rs_send)
    await_bytes(squares.at[pl.ds(1, peers - 1)], sq_send)


def finish(b_ref, qlow_ref, qsplit_ref, rsplit_ref, f_ref, momentum_ref, update_ref, factor_ref):
    right = (rsplit_ref[0], rsplit_ref[1])
    momentum_ref[...] = b_ref[...] + dot(qlow_ref[...], right[0], NN, None)
    update_ref[...] = dot3((qsplit_ref[0], qsplit_ref[1]), right, NN).astype(jnp.bfloat16)
    factor_ref[...] = f_ref[...]


def body(chips, peers, buffer, factor):
    rows, columns = buffer.shape
    rank = 32 * chips
    half = rank // peers // 2
    each = half // chips
    total_columns = columns * peers
    groups = chips // 4
    ring = chips // 2
    f32, bf16 = jnp.float32, jnp.bfloat16
    dma = pltpu.SemaphoreType.DMA
    vmem = pl.BlockSpec(memory_space=pltpu.VMEM)
    anywhere = pl.BlockSpec(memory_space=pl.ANY)
    qlow, qsplit, rsplit, factor_t = pl.pallas_call(
        functools.partial(
            kernel,
            chips,
            peers,
            1.0 / math.sqrt(total_columns),
            1.0 / total_columns,
            math.sqrt(rows * 2 * chips / rank),
        ),
        out_shape=(
            jax.ShapeDtypeStruct((rows, rank), bf16),
            jax.ShapeDtypeStruct((2, rows, rank), bf16),
            jax.ShapeDtypeStruct((2, rank, columns), bf16),
            jax.ShapeDtypeStruct((16, columns), f32),
        ),
        in_specs=[anywhere, vmem],
        out_specs=(vmem, vmem, anywhere, vmem),
        scratch_shapes=[
            pltpu.VMEM((rows, columns), f32),
            pltpu.VMEM((2, rank, columns), bf16),
            pltpu.VMEM((2, rows, columns), bf16),
            pltpu.VMEM((2, columns, rows), bf16),
            pltpu.VMEM((rank, columns), f32),
            pltpu.VMEM((2, 128, columns), bf16),
            pltpu.VMEM((rank, rows), f32),
            pltpu.VMEM((peers, max(groups - 1, 1) * 128 // peers, rows), f32),
            pltpu.VMEM((peers, 128 // peers, rows), f32),
            pltpu.VMEM((rank, rows), f32),
            pltpu.VMEM((rank, rows), f32),
            pltpu.VMEM((2, rank, rows), bf16),
            pltpu.VMEM((2 * half, rank), f32),
            pltpu.VMEM((half, rank), f32),
            pltpu.VMEM((chips, each, rank), f32),
            pltpu.VMEM((chips, each, rank), f32),
            pltpu.VMEM((chips, each, rank), f32),
            pltpu.VMEM((peers, 2, half, rank), f32),
            pltpu.VMEM((rank, rank), f32),
            pltpu.VMEM((128, 128), f32),
            pltpu.VMEM((2, rank, rank), bf16),
            pltpu.VMEM((rank, columns), f32),
            pltpu.VMEM((chips, 16, columns), f32),
            pltpu.VMEM((2, ring + 1, 16, columns), f32),
            pltpu.VMEM((rank, columns), f32),
            pltpu.VMEM((rank, 128), f32),
            pltpu.VMEM((peers, 1, rank), f32),
            dma,
            dma((2, ring, 4)),
            dma((chips,)),
            dma((4,)),
            dma((4,)),
            dma((5,)),
            dma((5,)),
            dma,
            dma((groups,)),
            dma,
            dma((2, ring, 4)),
            dma,
            dma((2, ring, 4)),
            dma((chips,)),
            dma,
            dma,
            dma,
            dma,
        ],
        compiler_params=pltpu.CompilerParams(
            collective_id=0, has_side_effects=True, vmem_limit_bytes=LIMIT
        ),
        name="low_rank_update",
    )(buffer, factor.T)

    def whole(*shape):
        return pl.BlockSpec(shape, lambda i: (0,) * len(shape))

    def tile(*lead):
        return pl.BlockSpec((*lead, 256), lambda i: (0,) * len(lead) + (i,))

    momentum, update, factor_t = pl.pallas_call(
        finish,
        grid=(pl.cdiv(columns, 256),),
        out_shape=(
            jax.ShapeDtypeStruct((rows, columns), f32),
            jax.ShapeDtypeStruct((rows, columns), bf16),
            jax.ShapeDtypeStruct((16, columns), f32),
        ),
        in_specs=[
            tile(rows),
            whole(rows, rank),
            whole(2, rows, rank),
            tile(2, rank),
            tile(16),
        ],
        out_specs=(tile(rows), tile(rows), tile(16)),
        compiler_params=pltpu.CompilerParams(vmem_limit_bytes=LIMIT),
        name="finish",
    )(buffer, qlow, qsplit, rsplit, factor_t)
    return momentum, update, factor_t.T


def solution(mesh):
    chips, peers = mesh.shape["dp"] // 2, mesh.shape["tensor"]
    placed = (P("dp", "tensor"), P("tensor", "dp"))
    return jax.shard_map(
        functools.partial(body, chips, peers),
        mesh=mesh,
        in_specs=placed,
        out_specs=(P("dp", "tensor"), P("dp", "tensor"), P("tensor", "dp")),
        check_vma=False,
    )
```

```python
import functools
import math

import jax
import jax.numpy as jnp
from jax import lax
from jax.experimental import pallas as pl
from jax.experimental.pallas import tpu as pltpu
from jax.sharding import PartitionSpec as P

MESH = pl.DeviceIdType.MESH
HIGHEST = lax.Precision.HIGHEST
NN = (((1,), (0,)), ((), ()))
LIMIT = 56 * 1024 * 1024


def dot(a, b, dims, precision):
    return lax.dot_general(
        a, b, dims, precision=precision, preferred_element_type=jnp.float32
    )


class Place:
    def __init__(self, chips, peers):
        dp = lax.axis_index("dp")
        self.z, self.c = dp // 2, dp % 2
        self.t = lax.axis_index("tensor")
        self.chips, self.peers = chips, peers
        self.next = {"dp": 2 * self.chip(1) + self.c}
        self.back = {"dp": 2 * self.chip(-1) + self.c}
        self.other = {"dp": 2 * self.z + 1 - self.c}

    def chip(self, offset):
        return lax.rem(self.z + offset + self.chips, self.chips)

    def at(self, offset):
        return {"dp": 2 * self.chip(offset) + self.c}

    def partner(self):
        return self.other

    def neighbour(self, way):
        return self.back if way else self.next

    def peer(self, k):
        return lax.rem(self.t + k, self.peers)


def remote(src, dst, send, recv, device):
    return pltpu.make_async_remote_copy(
        src_ref=src,
        dst_ref=dst,
        send_sem=send,
        recv_sem=recv,
        device_id=device,
        device_id_type=MESH,
    )


def await_bytes(ref, sem):
    pltpu.make_async_copy(ref, ref, sem).wait()


def enter(here, ring):
    barrier = pltpu.get_barrier_semaphore()

    def greet(device):
        pl.semaphore_signal(barrier, inc=1, device_id=device, device_id_type=MESH)

    @pl.loop(1, here.peers)
    def _(k):
        greet({"tensor": here.peer(k)})

    greet(here.partner())
    if ring:

        @pl.loop(1, here.chips)
        def _(k):
            greet(here.at(k))

        count = here.chips - 1
    else:
        greet(here.at(1))
        greet(here.at(-1))
        count = 2
    pl.semaphore_wait(barrier, here.peers - 1 + 1 + count)


def offset_of(n):
    return ((n + 1) // 2) * (2 * (n % 2) - 1)


def rows16(ref, chip, core, sub=None):
    start = 32 * chip + 16 * core
    if sub is None:
        return ref.at[pl.ds(pl.multiple_of(start, 16), 16)]
    return ref.at[pl.ds(pl.multiple_of(start + 8 * sub, 8), 8)]


def lane_parts(columns, count):
    tiles = columns // 128
    cuts = [128 * (tiles * i // count) for i in range(count + 1)]
    return [pl.ds(a, b - a) for a, b in zip(cuts, cuts[1:]) if b > a]


class Gather:
    def __init__(self, here, buf, parts, send, recv, pair_recv):
        self.here, self.buf, self.parts = here, buf, parts
        self.send, self.recv, self.pair_recv = send, recv, pair_recv
        self.half = here.chips // 2

    def forward(self, step, way, sub, h):
        here, sign = self.here, 1 - 2 * way
        rows = rows16(self.buf, here.chip(-sign * (step - 1)), here.c, sub)
        ref = rows.at[:, self.parts[h]]
        recv = self.recv.at[way, step - 1, 2 * sub + h]
        remote(ref, ref, self.send, recv, here.neighbour(way)).start()

    def share(self, offset, slot):
        here = self.here
        ref = rows16(self.buf, here.chip(offset), here.c)
        remote(ref, ref, self.send, self.pair_recv.at[slot], here.partner()).start()

    def begin(self):
        for sub in (0, 1):
            for h in range(len(self.parts)):
                for way in (0, 1):
                    self.forward(1, way, sub, h)
        self.share(0, 0)

    def step(self, step, sub):
        here = self.here

        def take(way, h):
            sign = 1 - 2 * way
            rows = rows16(self.buf, here.chip(-sign * step), here.c, sub)
            await_bytes(
                rows.at[:, self.parts[h]], self.recv.at[way, step - 1, 2 * sub + h]
            )

            @pl.when(step + 1 < self.half + (sub == way))
            def _():
                self.forward(step + 1, way, sub, h)

        for h in range(len(self.parts)):
            take(sub, h)

            @pl.when(step < self.half)
            def _():
                take(1 - sub, h)

        if sub == 1:
            self.share(step, 2 * step - 1)

            @pl.when(step < self.half)
            def _():
                self.share(-step, 2 * step)

    def shared(self, n):
        here = self.here
        ref = rows16(self.buf, here.chip(offset_of(n)), 1 - here.c)
        await_bytes(ref, self.pair_recv.at[n])

    def end(self):
        rows = 16 * (2 * self.here.chips - 1)
        await_bytes(self.buf.at[pl.ds(0, rows)], self.send)


def split(value):
    high = value.astype(jnp.bfloat16)
    return high, (value - high.astype(jnp.float32)).astype(jnp.bfloat16)


def dot3(a, b, dims):
    return (
        dot(a[0], b[0], dims, None) + dot(a[0], b[1], dims, None)
    ) + dot(a[1], b[0], dims, None)


def splat(value):
    return jnp.broadcast_to(value, (8, 128))


def eliminate(turn, carry, w_ref):
    s = carry
    lane = lax.broadcasted_iota(jnp.int32, (8, 128), 1)
    sublane = lax.broadcasted_iota(jnp.int32, (8, 128), 0)
    for half in (0, 8):
        block = (lane >= half) & (lane < half + 8)
        columns = [
            jnp.broadcast_to(s[:, half + j : half + j + 1], s.shape) for j in range(8)
        ]
        d = {
            (i, j): splat(columns[j][i : i + 1, :]) for j in range(8) for i in range(j, 8)
        }
        top = jnp.where(block, jnp.where(lane == sublane + half, 1.0, 0.0), s[0:8])
        r = [splat(top[i : i + 1, :]) for i in range(8)]
        root, inverse, t = [], [], {}
        for k in range(8):
            root.append(lax.rsqrt(d[k, k]))
            inverse.append(root[k] * root[k])
            for i in range(k + 1, 8):
                t[i, k] = d[i, k] * inverse[k]
                for j in range(k + 1, i + 1):
                    d[i, j] = d[i, j] - t[i, k] * d[j, k]
                r[i] = r[i] - t[i, k] * r[k]
        done = r[0] * root[0]
        for k in range(1, 8):
            done = jnp.where(sublane == k, r[k] * root[k], done)
        keep = (lane >= 128 - 16 * turn) | (lane < half + 8)
        w_ref[pl.ds(pl.multiple_of(16 * turn + half, 8), 8), :] = jnp.where(
            keep, done, 0.0
        )
        for k in range(7, -1, -1):
            r[k] = r[k] * inverse[k]
            for i in range(7, k, -1):
                r[k] = r[k] - t[i, k] * r[i]
        lanes = lax.broadcasted_iota(jnp.int32, (s.shape[0] - 8, 128), 1)
        s = jnp.where((lanes >= half) & (lanes < half + 8), 0.0, s[8:])
        for j in range(8):
            s = s - columns[j][8:] * r[j][0:1, :]
    blank = jnp.zeros((16, 128), jnp.float32)
    return pltpu.roll(jnp.concatenate([s, blank], axis=0), 112, 1)


def invert_factor(m_ref, block_ref, wsplit, between):
    rank = m_ref.shape[0]

    @pl.loop(0, rank // 128)
    def _(panel):
        here = pl.ds(pl.multiple_of(128 * panel, 128), 128)

        carry = m_ref[here, here]
        for first in (0, 2, 4, 6):
            carry = lax.fori_loop(
                first,
                first + 2,
                functools.partial(eliminate, w_ref=block_ref),
                carry[: 128 - 16 * first],
            )
            between(2 * panel + first // 4 + 1, first // 2 % 2)
        w = jnp.concatenate(
            [block_ref[0:16, :]]
            + [pltpu.roll(block_ref[16 * i : 16 * i + 16, :], 16 * i, 1) for i in range(1, 8)],
            axis=0,
        )
        m_ref[here, :] = dot(w, m_ref[here, :], NN, HIGHEST)
        m_ref[here, here] = w

        for last in range(rank // 128 - 1):

            @pl.when(panel == last)
            def _():
                start, stop = 128 * last, 128 * last + 128
                lower = m_ref[start:stop, stop:rank].T
                m_ref[stop:rank, start:stop] = jnp.zeros((rank - stop, 128), jnp.float32)
                m_ref[stop:rank, :] = m_ref[stop:rank, :] - dot(
                    lower, m_ref[start:stop, :], NN, HIGHEST
                )

        lanes = lax.broadcasted_iota(jnp.int32, (128, rank), 1)
        wsplit[0, here, :], wsplit[1, here, :] = split(
            jnp.where(lanes < 128 * panel + 128, m_ref[here, :], 0.0)
        )


def column_tiles(columns):
    return [(at, min(256, columns - at)) for at in range(0, columns, 256)]


def kernel(
    chips,
    peers,
    scale,
    mean,
    gain,
    b_hbm,
    f_ref,
    qlow_ref,
    qsplit_ref,
    r_hbm,
    factor_ref,
    b_ref,
    rsplit,
    bsplit,
    tsplit,
    fall,
    fsplit,
    part,
    first_parts,
    last_parts,
    arrived,
    pt,
    psplit,
    gpart,
    gpair,
    gsplit,
    gsplits,
    gsums,
    gram,
    m_ref,
    block_ref,
    wsplit,
    rpart,
    rpair,
    moving,
    rall,
    sums,
    squares,
    f_send,
    f_recv,
    f_pair,
    p_send,
    p_recv,
    g_send,
    g_recv,
    pair_send,
    pair_recv,
    rs_send,
    rs_recv,
    ag_send,
    ag_recv,
    ag_pair,
    sq_send,
    sq_recv,
    in_sem,
    out_sem,
):
    here = Place(chips, peers)
    rank = 32 * chips
    ring = chips // 2
    groups = chips // 4
    last = groups - 1
    tiles = column_tiles(b_ref.shape[1])
    load = pltpu.make_async_copy(b_hbm, b_ref, in_sem)
    load.start()
    own = rows16(fall, here.z, here.c)
    own[...] = f_ref[...]
    enter(here, True)
    halves = lane_parts(b_ref.shape[1], 2)
    gather = Gather(here, fall, halves, f_send, f_recv, f_pair)
    gather.begin()
    load.wait()

    def tile(i):
        return pl.ds(pl.multiple_of(128 * i, 128), 128)

    count = b_ref.shape[1] // 128

    def transpose(quarter):
        low, high = quarter * count // 4, (quarter + 1) * count // 4

        @pl.loop(low, high)
        def _(i):
            tsplit[0, tile(i), :], tsplit[1, tile(i), :] = split(b_ref[:, tile(i)].T)

    def straight(low, high):
        @pl.loop(low, high)
        def _(i):
            bsplit[0, :, tile(i)], bsplit[1, :, tile(i)] = split(b_ref[:, tile(i)])

    def join(g):
        order = [4 * g + n for n in range(4)]
        for n in order:
            gather.shared(n)
        rows = [
            fall[pl.ds(pl.multiple_of(32 * here.chip(offset_of(n)), 32), 32), :]
            for n in order
        ]
        fsplit[0], fsplit[1] = split(jnp.concatenate(rows, axis=0))

    def product(g, turn):
        rows = tile(g)
        one = dot(fsplit[turn // 2], tsplit[turn % 2], NN, None)
        part[rows, :] = part[rows, :] + one if turn else one

    def spread(base, rows, parts, turn):
        piece = rows // peers

        @pl.loop(1, peers)
        def _(k):
            other = here.peer(k)
            start = pl.multiple_of(base + piece * other, 8)
            remote(
                part.at[pl.ds(start, piece)],
                parts.at[k],
                p_send.at[turn],
                p_recv.at[turn],
                {"tensor": other},
            ).start()

    def total(base, rows, parts, turn):
        piece = rows // peers
        mine = pl.ds(pl.multiple_of(base + piece * here.t, 8), piece)
        parts[0] = part[mine, :]
        await_bytes(parts.at[pl.ds(1, peers - 1)], p_recv.at[turn])
        arrived[mine, :] = jnp.sum(parts[...], axis=0) * scale

        @pl.loop(1, peers)
        def _(k):
            place = arrived.at[mine]
            remote(
                place,
                place,
                p_send.at[turn + 1],
                p_recv.at[turn + 1],
                {"tensor": here.peer(k)},
            ).start()

    early = 128 * last

    def piece(g, i):
        if i == 0:
            join(g)
        else:
            product(g, i - 1)

    @pl.loop(0, groups)
    def _(g):
        for i in range(4):
            gather.step(2 * g + 1 + i // 2, i % 2)

            @pl.when(g == 0)
            def _():
                transpose(i)

            @pl.when(g > 0)
            def _():
                piece(g - 1, i)

    if last:
        spread(0, early, first_parts, 0)
    for i in range(4):
        piece(last, i)
    spread(early, 128, last_parts, 2)
    if last:
        total(0, early, first_parts, 0)
    straight(0, count // 2)
    total(early, 128, last_parts, 2)
    straight(count // 2, count)
    if last:
        await_bytes(first_parts.at[pl.ds(1, peers - 1)], p_recv.at[1])
    await_bytes(last_parts.at[pl.ds(1, peers - 1)], p_recv.at[3])

    @pl.loop(0, chips)
    def _(n):
        place = pl.ds(pl.multiple_of(32 * here.chip(offset_of(n)), 32), 32)
        pt[place, :] = arrived[pl.ds(pl.multiple_of(32 * n, 32), 32), :]

    def right_product(g):
        chipped = [here.chip(offset_of(4 * g + n)) for n in range(4)]
        p = split(arrived[tile(g), :])
        for at, width in tiles:
            b = (bsplit[0, :, at : at + width], bsplit[1, :, at : at + width])
            r = dot3(p, b, NN)
            for n, i in enumerate(chipped):
                place = pl.ds(pl.multiple_of(32 * i, 32), 32)
                rpart[place, at : at + width] = r[32 * n : 32 * n + 32, :]
        for n, i in enumerate(chipped):
            remote(
                rows16(rpart, i, 1 - here.c),
                rpair.at[4 * g + n],
                pair_send,
                pair_recv.at[g],
                here.partner(),
            ).start()

    def right_own(n, sub, lanes):
        chip = here.chip(offset_of(n))
        rows = rows16(rpart, chip, here.c, sub)
        return rows[:, lanes] + rpair[n, 8 * sub : 8 * sub + 8, lanes]

    def scatter(k, sub):
        def pass_on(way, come, h):
            lanes = halves[h]
            place = moving.at[way, k, pl.ds(8 * sub, 8), lanes]
            n = 2 * k - 1 if way == 0 else 2 * k - 2 * k // chips

            @pl.when(come)
            def _():
                await_bytes(place, rs_recv.at[way, k, 2 * sub + h])
                place[...] = place[...] + right_own(n, sub, lanes)

            @pl.when(jnp.logical_not(come))
            def _():
                place[...] = right_own(n, sub, lanes)

            remote(
                place,
                moving.at[way, k - 1, pl.ds(8 * sub, 8), lanes],
                rs_send,
                rs_recv.at[way, k - 1, 2 * sub + h],
                here.neighbour(way),
            ).start()

        for h in range(len(halves)):
            pass_on(sub, k < ring, h)

            @pl.when(k < ring)
            def _():
                pass_on(1 - sub, k < ring - 1, h)

    collect = Gather(here, rall, lane_parts(b_ref.shape[1], 1), ag_send, ag_recv, ag_pair)

    def settle():
        for sub in (0, 1):
            for h, lanes in enumerate(halves):
                for way in (0, 1):
                    place = moving.at[way, 0, pl.ds(8 * sub, 8), lanes]
                    await_bytes(place, rs_recv.at[way, 0, 2 * sub + h])
                rows16(rall, here.z, here.c, sub)[:, lanes] = (
                    right_own(0, sub, lanes)
                    + moving[0, 0, 8 * sub : 8 * sub + 8, lanes]
                    + moving[1, 0, 8 * sub : 8 * sub + 8, lanes]
                )
        collect.begin()

    def halve(n):
        collect.shared(n)
        place = pl.ds(pl.multiple_of(32 * here.chip(offset_of(n)), 32), 32)
        rsplit[0, place, :], rsplit[1, place, :] = split(rall[place, :])

    def onward(step, sub):
        collect.step(step, sub)

        @pl.when(2 * step - 5 + sub >= 0)
        def _():
            halve(2 * step - 5 + sub)

    block = rank // peers
    half = block // 2
    each = half // chips
    mine = pl.ds(pl.multiple_of(block * here.t, block), block)
    theirs = pl.ds(pl.multiple_of(half * (1 - here.c), half), half)
    keep = pl.ds(pl.multiple_of(half * here.c, half), half)

    def gram_pair():
        return remote(
            gpart.at[theirs], gpair, g_send.at[0], g_recv.at[0], here.partner()
        )

    def gram_own():
        gpart[...] = dot(pt[mine, :], pt[...].T, NN, HIGHEST)
        gram_pair().start()

    def gram_scatter():
        gram_pair().wait()
        chip_sum = gpart[keep, :] + gpair[...]
        for k in range(chips):
            gsplit[k] = chip_sum[each * k : each * (k + 1), :]

        @pl.loop(1, chips)
        def _(k):
            remote(
                gsplit.at[here.chip(k)],
                gsplits.at[k],
                g_send.at[1],
                g_recv.at[1],
                here.at(k),
            ).start()

        gsplits[0] = gsplit[here.z]

    def gram_gather():
        await_bytes(gsplits.at[pl.ds(1, chips - 1)], g_recv.at[1])
        gsums[here.z] = jnp.sum(gsplits[...], axis=0)

        @pl.loop(1, chips)
        def _(k):
            place = gsums.at[here.z]
            remote(place, place, g_send.at[2], g_recv.at[2], here.at(k)).start()

    def gram_spread():
        await_bytes(gsums.at[pl.ds(0, chips - 1)], g_recv.at[2])
        gram[here.t, here.c] = gsums[...].reshape(half, rank)

        @pl.loop(1, peers)
        def _(k):
            place = gram.at[here.t, here.c]
            remote(
                place, place, g_send.at[3], g_recv.at[3], {"tensor": here.peer(k)}
            ).start()

    def gram_pass():
        ours = gram.at[:, here.c]
        return remote(ours, ours, g_send.at[4], g_recv.at[4], here.partner())

    def gram_share():
        await_bytes(gram.at[pl.ds(0, peers - 1), 0], g_recv.at[3])
        gram_pass().start()

    gram_steps = (gram_scatter, gram_gather, gram_spread, gram_share)
    right_product(last)
    gram_own()

    @pl.loop(0, groups)
    def _(turn):
        g = last - turn
        await_bytes(rpair.at[pl.ds(4 * g, 4)], pair_recv.at[g])
        for sub in (0, 1):
            scatter(2 * g + 2, sub)

        @pl.when(g > 0)
        def _():
            right_product(g - 1)

        for i, step in enumerate(gram_steps):
            if i < groups:

                @pl.when(turn == i)
                def _():
                    step()

        for sub in (0, 1):
            scatter(2 * g + 1, sub)

    for i, step in enumerate(gram_steps):
        if i >= groups:
            step()
    psplit[0], psplit[1] = split(pt[...])
    settle()
    gram_pass().wait()
    m_ref[...] = gram[...].reshape(rank, rank)
    invert_factor(m_ref, block_ref, wsplit, onward)

    @pl.loop(chips - 3, chips)
    def _(n):
        halve(n)

    sums[...] = jnp.zeros_like(sums)

    def right_tile(at, width):
        columns = pl.ds(at, width)
        blocks = []
        for row in range(0, rank, 256):
            stop = row + 256
            blocks.append(
                dot3(
                    (wsplit[0, row:stop, 0:stop], wsplit[1, row:stop, 0:stop]),
                    (rsplit[0, 0:stop, columns], rsplit[1, 0:stop, columns]),
                    NN,
                )
            )
        right = jnp.concatenate(blocks, axis=0)
        for lane in range(0, width, 128):
            one = right[:, lane : lane + 128]
            sums[...] = sums[...] + one * one
        rsplit[0, :, columns], rsplit[1, :, columns] = split(right)
        pltpu.make_async_copy(
            rsplit.at[:, :, columns], r_hbm.at[:, :, columns], out_sem
        ).start()

    full = 256 * (b_ref.shape[1] // 256)

    @pl.loop(0, full // 256)
    def _(i):
        right_tile(pl.multiple_of(256 * i, 256), 256)

    if full < b_ref.shape[1]:
        right_tile(full, b_ref.shape[1] - full)
    squares[0] = jnp.sum(sums[...].T, axis=0, keepdims=True)

    @pl.loop(1, peers)
    def _(k):
        remote(
            squares.at[0], squares.at[k], sq_send, sq_recv, {"tensor": here.peer(k)}
        ).start()

    blocks = []
    for row in range(0, rank, 256):
        stop = row + 256
        blocks.append(
            dot3(
                (wsplit[0, row:stop, 0:stop], wsplit[1, row:stop, 0:stop]),
                (psplit[0, 0:stop, :], psplit[1, 0:stop, :]),
                NN,
            )
        )
    q = jnp.concatenate(blocks, axis=0).T
    qlow_ref[...] = (q * -0.05).astype(jnp.bfloat16)
    await_bytes(squares.at[pl.ds(1, peers - 1)], sq_recv)
    scales = lax.rsqrt(jnp.sum(squares[...], axis=0) * mean + 1e-06)
    qsplit_ref[0], qsplit_ref[1] = split(q * (scales * gain))
    lanes = lax.broadcasted_iota(jnp.int32, (32, rank), 1)
    rows = lax.broadcasted_iota(jnp.int32, (32, rank), 0) + 32 * here.z
    picked = jnp.where(lanes == rows, jnp.broadcast_to(scales, (32, rank)), 0.0)
    place = pl.ds(pl.multiple_of(32 * here.z, 32), 32)
    ours = (
        rsplit[0, place, :].astype(jnp.float32) + rsplit[1, place, :].astype(jnp.float32)
    ) * jnp.sum(picked, axis=1, keepdims=True)
    factor_ref[...] = jnp.where(here.c == 0, ours[0:16], ours[16:32])

    await_bytes(rsplit, out_sem)
    gather.end()
    collect.end()
    if last:
        for turn in (0, 1):
            await_bytes(first_parts.at[pl.ds(1, peers - 1)], p_send.at[turn])
    for turn in (2, 3):
        await_bytes(last_parts.at[pl.ds(1, peers - 1)], p_send.at[turn])
    await_bytes(gsplits.at[pl.ds(1, chips - 1)], g_send.at[1])
    await_bytes(gsums.at[pl.ds(0, chips - 1)], g_send.at[2])
    await_bytes(gram.at[pl.ds(0, peers - 1), 0], g_send.at[3])
    await_bytes(rpart.at[pl.ds(0, rank // 2)], pair_send)
    await_bytes(rall.at[pl.ds(0, 16 * (chips - 1))], rs_send)
    await_bytes(squares.at[pl.ds(1, peers - 1)], sq_send)


def finish(b_ref, qlow_ref, qsplit_ref, rsplit_ref, f_ref, momentum_ref, update_ref, factor_ref):
    right = (rsplit_ref[0], rsplit_ref[1])
    momentum_ref[...] = b_ref[...] + dot(qlow_ref[...], right[0], NN, None)
    update_ref[...] = dot3((qsplit_ref[0], qsplit_ref[1]), right, NN).astype(jnp.bfloat16)
    factor_ref[...] = f_ref[...]


def body(chips, peers, buffer, factor):
    rows, columns = buffer.shape
    rank = 32 * chips
    half = rank // peers // 2
    each = half // chips
    total_columns = columns * peers
    groups = chips // 4
    ring = chips // 2
    f32, bf16 = jnp.float32, jnp.bfloat16
    dma = pltpu.SemaphoreType.DMA
    vmem = pl.BlockSpec(memory_space=pltpu.VMEM)
    anywhere = pl.BlockSpec(memory_space=pl.ANY)
    qlow, qsplit, rsplit, factor_t = pl.pallas_call(
        functools.partial(
            kernel,
            chips,
            peers,
            1.0 / math.sqrt(total_columns),
            1.0 / total_columns,
            math.sqrt(rows * 2 * chips / rank),
        ),
        out_shape=(
            jax.ShapeDtypeStruct((rows, rank), bf16),
            jax.ShapeDtypeStruct((2, rows, rank), bf16),
            jax.ShapeDtypeStruct((2, rank, columns), bf16),
            jax.ShapeDtypeStruct((16, columns), f32),
        ),
        in_specs=[anywhere, vmem],
        out_specs=(vmem, vmem, anywhere, vmem),
        scratch_shapes=[
            pltpu.VMEM((rows, columns), f32),
            pltpu.VMEM((2, rank, columns), bf16),
            pltpu.VMEM((2, rows, columns), bf16),
            pltpu.VMEM((2, columns, rows), bf16),
            pltpu.VMEM((rank, columns), f32),
            pltpu.VMEM((2, 128, columns), bf16),
            pltpu.VMEM((rank, rows), f32),
            pltpu.VMEM((peers, max(groups - 1, 1) * 128 // peers, rows), f32),
            pltpu.VMEM((peers, 128 // peers, rows), f32),
            pltpu.VMEM((rank, rows), f32),
            pltpu.VMEM((rank, rows), f32),
            pltpu.VMEM((2, rank, rows), bf16),
            pltpu.VMEM((2 * half, rank), f32),
            pltpu.VMEM((half, rank), f32),
            pltpu.VMEM((chips, each, rank), f32),
            pltpu.VMEM((chips, each, rank), f32),
            pltpu.VMEM((chips, each, rank), f32),
            pltpu.VMEM((peers, 2, half, rank), f32),
            pltpu.VMEM((rank, rank), f32),
            pltpu.VMEM((128, 128), f32),
            pltpu.VMEM((2, rank, rank), bf16),
            pltpu.VMEM((rank, columns), f32),
            pltpu.VMEM((chips, 16, columns), f32),
            pltpu.VMEM((2, ring + 1, 16, columns), f32),
            pltpu.VMEM((rank, columns), f32),
            pltpu.VMEM((rank, 128), f32),
            pltpu.VMEM((peers, 1, rank), f32),
            dma,
            dma((2, ring, 4)),
            dma((chips,)),
            dma((4,)),
            dma((4,)),
            dma((5,)),
            dma((5,)),
            dma,
            dma((groups,)),
            dma,
            dma((2, ring, 4)),
            dma,
            dma((2, ring, 4)),
            dma((chips,)),
            dma,
            dma,
            dma,
            dma,
        ],
        compiler_params=pltpu.CompilerParams(
            collective_id=0, has_side_effects=True, vmem_limit_bytes=LIMIT
        ),
        name="low_rank_update",
    )(buffer, factor.T)

    def whole(*shape):
        return pl.BlockSpec(shape, lambda i: (0,) * len(shape))

    def tile(*lead):
        return pl.BlockSpec((*lead, 256), lambda i: (0,) * len(lead) + (i,))

    momentum, update, factor_t = pl.pallas_call(
        finish,
        grid=(pl.cdiv(columns, 256),),
        out_shape=(
            jax.ShapeDtypeStruct((rows, columns), f32),
            jax.ShapeDtypeStruct((rows, columns), bf16),
            jax.ShapeDtypeStruct((16, columns), f32),
        ),
        in_specs=[
            tile(rows),
            whole(rows, rank),
            whole(2, rows, rank),
            tile(2, rank),
            tile(16),
        ],
        out_specs=(tile(rows), tile(rows), tile(16)),
        compiler_params=pltpu.CompilerParams(vmem_limit_bytes=LIMIT),
        name="finish",
    )(buffer, qlow, qsplit, rsplit, factor_t)
    return momentum, update, factor_t.T


def solution(mesh):
    chips, peers = mesh.shape["dp"] // 2, mesh.shape["tensor"]
    placed = (P("dp", "tensor"), P("tensor", "dp"))
    return jax.shard_map(
        functools.partial(body, chips, peers),
        mesh=mesh,
        in_specs=placed,
        out_specs=(P("dp", "tensor"), P("dp", "tensor"), P("tensor", "dp")),
        check_vma=False,
    )
```

```python
import functools
import math

import jax
import jax.numpy as jnp
from jax import lax
from jax.experimental import pallas as pl
from jax.experimental.pallas import tpu as pltpu
from jax.sharding import PartitionSpec as P

MESH = pl.DeviceIdType.MESH
HIGHEST = lax.Precision.HIGHEST
NN = (((1,), (0,)), ((), ()))
LIMIT = 56 * 1024 * 1024


def dot(a, b, dims, precision):
    return lax.dot_general(
        a, b, dims, precision=precision, preferred_element_type=jnp.float32
    )


class Place:
    def __init__(self, chips, peers):
        dp = lax.axis_index("dp")
        self.z, self.c = dp // 2, dp % 2
        self.t = lax.axis_index("tensor")
        self.chips, self.peers = chips, peers
        self.next = {"dp": 2 * self.chip(1) + self.c}
        self.back = {"dp": 2 * self.chip(-1) + self.c}
        self.other = {"dp": 2 * self.z + 1 - self.c}

    def chip(self, offset):
        return lax.rem(self.z + offset + self.chips, self.chips)

    def at(self, offset):
        return {"dp": 2 * self.chip(offset) + self.c}

    def partner(self):
        return self.other

    def neighbour(self, way):
        return self.back if way else self.next

    def peer(self, k):
        return lax.rem(self.t + k, self.peers)


def remote(src, dst, send, recv, device):
    return pltpu.make_async_remote_copy(
        src_ref=src,
        dst_ref=dst,
        send_sem=send,
        recv_sem=recv,
        device_id=device,
        device_id_type=MESH,
    )


def await_bytes(ref, sem):
    pltpu.make_async_copy(ref, ref, sem).wait()


def enter(here, ring):
    barrier = pltpu.get_barrier_semaphore()

    def greet(device):
        pl.semaphore_signal(barrier, inc=1, device_id=device, device_id_type=MESH)

    @pl.loop(1, here.peers)
    def _(k):
        greet({"tensor": here.peer(k)})

    greet(here.partner())
    if ring:

        @pl.loop(1, here.chips)
        def _(k):
            greet(here.at(k))

        count = here.chips - 1
    else:
        greet(here.at(1))
        greet(here.at(-1))
        count = 2
    pl.semaphore_wait(barrier, here.peers - 1 + 1 + count)


def offset_of(n):
    return ((n + 1) // 2) * (2 * (n % 2) - 1)


def rows16(ref, chip, core, sub=None):
    start = 32 * chip + 16 * core
    if sub is None:
        return ref.at[pl.ds(pl.multiple_of(start, 16), 16)]
    return ref.at[pl.ds(pl.multiple_of(start + 8 * sub, 8), 8)]


def lane_parts(columns, count):
    tiles = columns // 128
    cuts = [128 * (tiles * i // count) for i in range(count + 1)]
    return [pl.ds(a, b - a) for a, b in zip(cuts, cuts[1:]) if b > a]


class Gather:
    def __init__(self, here, buf, parts, send, recv, pair_recv):
        self.here, self.buf, self.parts = here, buf, parts
        self.send, self.recv, self.pair_recv = send, recv, pair_recv
        self.half = here.chips // 2

    def forward(self, step, way, sub, h):
        here, sign = self.here, 1 - 2 * way
        rows = rows16(self.buf, here.chip(-sign * (step - 1)), here.c, sub)
        ref = rows.at[:, self.parts[h]]
        recv = self.recv.at[way, step - 1, 2 * sub + h]
        remote(ref, ref, self.send, recv, here.neighbour(way)).start()

    def share(self, offset, slot):
        here = self.here
        ref = rows16(self.buf, here.chip(offset), here.c)
        remote(ref, ref, self.send, self.pair_recv.at[slot], here.partner()).start()

    def begin(self):
        for sub in (0, 1):
            for h in range(len(self.parts)):
                for way in (0, 1):
                    self.forward(1, way, sub, h)
        self.share(0, 0)

    def step(self, step, sub):
        here = self.here

        def take(way, h):
            sign = 1 - 2 * way
            rows = rows16(self.buf, here.chip(-sign * step), here.c, sub)
            await_bytes(
                rows.at[:, self.parts[h]], self.recv.at[way, step - 1, 2 * sub + h]
            )

            @pl.when(step + 1 < self.half + (sub == way))
            def _():
                self.forward(step + 1, way, sub, h)

        for h in range(len(self.parts)):
            take(sub, h)

            @pl.when(step < self.half)
            def _():
                take(1 - sub, h)

        if sub == 1:
            self.share(step, 2 * step - 1)

            @pl.when(step < self.half)
            def _():
                self.share(-step, 2 * step)

    def shared(self, n):
        here = self.here
        ref = rows16(self.buf, here.chip(offset_of(n)), 1 - here.c)
        await_bytes(ref, self.pair_recv.at[n])

    def end(self):
        rows = 16 * (2 * self.here.chips - 1)
        await_bytes(self.buf.at[pl.ds(0, rows)], self.send)


def split(value):
    high = value.astype(jnp.bfloat16)
    return high, (value - high.astype(jnp.float32)).astype(jnp.bfloat16)


def dot3(a, b, dims):
    return (
        dot(a[0], b[0], dims, None) + dot(a[0], b[1], dims, None)
    ) + dot(a[1], b[0], dims, None)


def splat(value):
    return jnp.broadcast_to(value, (8, 128))


def eliminate(turn, carry, w_ref):
    s = carry
    lane = lax.broadcasted_iota(jnp.int32, (8, 128), 1)
    sublane = lax.broadcasted_iota(jnp.int32, (8, 128), 0)
    for half in (0, 8):
        block = (lane >= half) & (lane < half + 8)
        columns = [
            jnp.broadcast_to(s[:, half + j : half + j + 1], s.shape) for j in range(8)
        ]
        d = {
            (i, j): splat(columns[j][i : i + 1, :]) for j in range(8) for i in range(j, 8)
        }
        top = jnp.where(block, jnp.where(lane == sublane + half, 1.0, 0.0), s[0:8])
        r = [splat(top[i : i + 1, :]) for i in range(8)]
        root, inverse, t = [], [], {}
        for k in range(8):
            root.append(lax.rsqrt(d[k, k]))
            inverse.append(root[k] * root[k])
            for i in range(k + 1, 8):
                t[i, k] = d[i, k] * inverse[k]
                for j in range(k + 1, i + 1):
                    d[i, j] = d[i, j] - t[i, k] * d[j, k]
                r[i] = r[i] - t[i, k] * r[k]
        done = r[0] * root[0]
        for k in range(1, 8):
            done = jnp.where(sublane == k, r[k] * root[k], done)
        keep = (lane >= 128 - 16 * turn) | (lane < half + 8)
        w_ref[pl.ds(pl.multiple_of(16 * turn + half, 8), 8), :] = jnp.where(
            keep, done, 0.0
        )
        for k in range(7, -1, -1):
            r[k] = r[k] * inverse[k]
            for i in range(7, k, -1):
                r[k] = r[k] - t[i, k] * r[i]
        lanes = lax.broadcasted_iota(jnp.int32, (s.shape[0] - 8, 128), 1)
        s = jnp.where((lanes >= half) & (lanes < half + 8), 0.0, s[8:])
        for j in range(8):
            s = s - columns[j][8:] * r[j][0:1, :]
    blank = jnp.zeros((16, 128), jnp.float32)
    return pltpu.roll(jnp.concatenate([s, blank], axis=0), 112, 1)


def invert_factor(m_ref, block_ref, wsplit, between):
    rank = m_ref.shape[0]

    @pl.loop(0, rank // 128)
    def _(panel):
        here = pl.ds(pl.multiple_of(128 * panel, 128), 128)

        carry = m_ref[here, here]
        for first in (0, 2, 4, 6):
            carry = lax.fori_loop(
                first,
                first + 2,
                functools.partial(eliminate, w_ref=block_ref),
                carry[: 128 - 16 * first],
            )
            between(2 * panel + first // 4 + 1, first // 2 % 2)
        w = jnp.concatenate(
            [block_ref[0:16, :]]
            + [pltpu.roll(block_ref[16 * i : 16 * i + 16, :], 16 * i, 1) for i in range(1, 8)],
            axis=0,
        )
        m_ref[here, :] = dot(w, m_ref[here, :], NN, HIGHEST)
        m_ref[here, here] = w

        for last in range(rank // 128 - 1):

            @pl.when(panel == last)
            def _():
                start, stop = 128 * last, 128 * last + 128
                lower = m_ref[start:stop, stop:rank].T
                m_ref[stop:rank, start:stop] = jnp.zeros((rank - stop, 128), jnp.float32)
                m_ref[stop:rank, :] = m_ref[stop:rank, :] - dot(
                    lower, m_ref[start:stop, :], NN, HIGHEST
                )

        lanes = lax.broadcasted_iota(jnp.int32, (128, rank), 1)
        wsplit[0, here, :], wsplit[1, here, :] = split(
            jnp.where(lanes < 128 * panel + 128, m_ref[here, :], 0.0)
        )


def column_tiles(columns):
    return [(at, min(256, columns - at)) for at in range(0, columns, 256)]


def kernel(
    chips,
    peers,
    scale,
    mean,
    gain,
    b_hbm,
    f_ref,
    qlow_ref,
    qsplit_ref,
    r_hbm,
    factor_ref,
    b_ref,
    rsplit,
    bsplit,
    tsplit,
    fall,
    fsplit,
    part,
    first_parts,
    last_parts,
    arrived,
    pt,
    psplit,
    gpart,
    gpair,
    gsplit,
    gsplits,
    gsums,
    gram,
    m_ref,
    block_ref,
    wsplit,
    rpart,
    rpair,
    moving,
    rall,
    sums,
    squares,
    f_send,
    f_recv,
    f_pair,
    p_send,
    p_recv,
    g_send,
    g_recv,
    pair_send,
    pair_recv,
    rs_send,
    rs_recv,
    ag_send,
    ag_recv,
    ag_pair,
    sq_send,
    sq_recv,
    in_sem,
    out_sem,
):
    here = Place(chips, peers)
    rank = 32 * chips
    ring = chips // 2
    groups = chips // 4
    last = groups - 1
    tiles = column_tiles(b_ref.shape[1])
    load = pltpu.make_async_copy(b_hbm, b_ref, in_sem)
    load.start()
    own = rows16(fall, here.z, here.c)
    own[...] = f_ref[...]
    enter(here, True)
    halves = lane_parts(b_ref.shape[1], 1)
    gather = Gather(here, fall, halves, f_send, f_recv, f_pair)
    gather.begin()
    load.wait()

    def tile(i):
        return pl.ds(pl.multiple_of(128 * i, 128), 128)

    count = b_ref.shape[1] // 128

    def transpose(quarter):
        low, high = quarter * count // 4, (quarter + 1) * count // 4

        @pl.loop(low, high)
        def _(i):
            tsplit[0, tile(i), :], tsplit[1, tile(i), :] = split(b_ref[:, tile(i)].T)

    def straight(low, high):
        @pl.loop(low, high)
        def _(i):
            bsplit[0, :, tile(i)], bsplit[1, :, tile(i)] = split(b_ref[:, tile(i)])

    def join(g):
        order = [4 * g + n for n in range(4)]
        for n in order:
            gather.shared(n)
        rows = [
            fall[pl.ds(pl.multiple_of(32 * here.chip(offset_of(n)), 32), 32), :]
            for n in order
        ]
        fsplit[0], fsplit[1] = split(jnp.concatenate(rows, axis=0))

    def product(g, turn):
        rows = tile(g)
        one = dot(fsplit[turn // 2], tsplit[turn % 2], NN, None)
        part[rows, :] = part[rows, :] + one if turn else one

    def spread(base, rows, parts, turn):
        piece = rows // peers

        @pl.loop(1, peers)
        def _(k):
            other = here.peer(k)
            start = pl.multiple_of(base + piece * other, 8)
            remote(
                part.at[pl.ds(start, piece)],
                parts.at[k],
                p_send.at[turn],
                p_recv.at[turn],
                {"tensor": other},
            ).start()

    def total(base, rows, parts, turn):
        piece = rows // peers
        mine = pl.ds(pl.multiple_of(base + piece * here.t, 8), piece)
        parts[0] = part[mine, :]
        await_bytes(parts.at[pl.ds(1, peers - 1)], p_recv.at[turn])
        arrived[mine, :] = jnp.sum(parts[...], axis=0) * scale

        @pl.loop(1, peers)
        def _(k):
            place = arrived.at[mine]
            remote(
                place,
                place,
                p_send.at[turn + 1],
                p_recv.at[turn + 1],
                {"tensor": here.peer(k)},
            ).start()

    early = 128 * last

    def piece(g, i):
        if i == 0:
            join(g)
        else:
            product(g, i - 1)

    @pl.loop(0, groups)
    def _(g):
        for i in range(4):
            gather.step(2 * g + 1 + i // 2, i % 2)

            @pl.when(g == 0)
            def _():
                transpose(i)

            @pl.when(g > 0)
            def _():
                piece(g - 1, i)

    if last:
        spread(0, early, first_parts, 0)
    for i in range(4):
        piece(last, i)
    spread(early, 128, last_parts, 2)
    if last:
        total(0, early, first_parts, 0)
    straight(0, count // 2)
    total(early, 128, last_parts, 2)
    straight(count // 2, count)
    if last:
        await_bytes(first_parts.at[pl.ds(1, peers - 1)], p_recv.at[1])
    await_bytes(last_parts.at[pl.ds(1, peers - 1)], p_recv.at[3])

    @pl.loop(0, chips)
    def _(n):
        place = pl.ds(pl.multiple_of(32 * here.chip(offset_of(n)), 32), 32)
        pt[place, :] = arrived[pl.ds(pl.multiple_of(32 * n, 32), 32), :]

    def right_product(g):
        chipped = [here.chip(offset_of(4 * g + n)) for n in range(4)]
        p = split(arrived[tile(g), :])
        for at, width in tiles:
            b = (bsplit[0, :, at : at + width], bsplit[1, :, at : at + width])
            r = dot3(p, b, NN)
            for n, i in enumerate(chipped):
                place = pl.ds(pl.multiple_of(32 * i, 32), 32)
                rpart[place, at : at + width] = r[32 * n : 32 * n + 32, :]
        for n, i in enumerate(chipped):
            remote(
                rows16(rpart, i, 1 - here.c),
                rpair.at[4 * g + n],
                pair_send,
                pair_recv.at[g],
                here.partner(),
            ).start()

    def right_own(n, sub, lanes):
        chip = here.chip(offset_of(n))
        rows = rows16(rpart, chip, here.c, sub)
        return rows[:, lanes] + rpair[n, 8 * sub : 8 * sub + 8, lanes]

    def scatter(k, sub):
        def pass_on(way, come, h):
            lanes = halves[h]
            place = moving.at[way, k, pl.ds(8 * sub, 8), lanes]
            n = 2 * k - 1 if way == 0 else 2 * k - 2 * k // chips

            @pl.when(come)
            def _():
                await_bytes(place, rs_recv.at[way, k, 2 * sub + h])
                place[...] = place[...] + right_own(n, sub, lanes)

            @pl.when(jnp.logical_not(come))
            def _():
                place[...] = right_own(n, sub, lanes)

            remote(
                place,
                moving.at[way, k - 1, pl.ds(8 * sub, 8), lanes],
                rs_send,
                rs_recv.at[way, k - 1, 2 * sub + h],
                here.neighbour(way),
            ).start()

        for h in range(len(halves)):
            pass_on(sub, k < ring, h)

            @pl.when(k < ring)
            def _():
                pass_on(1 - sub, k < ring - 1, h)

    collect = Gather(here, rall, lane_parts(b_ref.shape[1], 1), ag_send, ag_recv, ag_pair)

    def settle():
        for sub in (0, 1):
            for h, lanes in enumerate(halves):
                for way in (0, 1):
                    place = moving.at[way, 0, pl.ds(8 * sub, 8), lanes]
                    await_bytes(place, rs_recv.at[way, 0, 2 * sub + h])
                rows16(rall, here.z, here.c, sub)[:, lanes] = (
                    right_own(0, sub, lanes)
                    + moving[0, 0, 8 * sub : 8 * sub + 8, lanes]
                    + moving[1, 0, 8 * sub : 8 * sub + 8, lanes]
                )
        collect.begin()

    def halve(n):
        collect.shared(n)
        place = pl.ds(pl.multiple_of(32 * here.chip(offset_of(n)), 32), 32)
        rsplit[0, place, :], rsplit[1, place, :] = split(rall[place, :])

    def onward(step, sub):
        collect.step(step, sub)

        @pl.when(2 * step - 5 + sub >= 0)
        def _():
            halve(2 * step - 5 + sub)

    block = rank // peers
    half = block // 2
    each = half // chips
    mine = pl.ds(pl.multiple_of(block * here.t, block), block)
    theirs = pl.ds(pl.multiple_of(half * (1 - here.c), half), half)
    keep = pl.ds(pl.multiple_of(half * here.c, half), half)

    def gram_pair():
        return remote(
            gpart.at[theirs], gpair, g_send.at[0], g_recv.at[0], here.partner()
        )

    def gram_own():
        gpart[...] = dot(pt[mine, :], pt[...].T, NN, HIGHEST)
        gram_pair().start()

    def gram_scatter():
        gram_pair().wait()
        chip_sum = gpart[keep, :] + gpair[...]
        for k in range(chips):
            gsplit[k] = chip_sum[each * k : each * (k + 1), :]

        @pl.loop(1, chips)
        def _(k):
            remote(
                gsplit.at[here.chip(k)],
                gsplits.at[k],
                g_send.at[1],
                g_recv.at[1],
                here.at(k),
            ).start()

        gsplits[0] = gsplit[here.z]

    def gram_gather():
        await_bytes(gsplits.at[pl.ds(1, chips - 1)], g_recv.at[1])
        gsums[here.z] = jnp.sum(gsplits[...], axis=0)

        @pl.loop(1, chips)
        def _(k):
            place = gsums.at[here.z]
            remote(place, place, g_send.at[2], g_recv.at[2], here.at(k)).start()

    def gram_spread():
        await_bytes(gsums.at[pl.ds(0, chips - 1)], g_recv.at[2])
        gram[here.t, here.c] = gsums[...].reshape(half, rank)

        @pl.loop(1, peers)
        def _(k):
            place = gram.at[here.t, here.c]
            remote(
                place, place, g_send.at[3], g_recv.at[3], {"tensor": here.peer(k)}
            ).start()

    def gram_pass():
        ours = gram.at[:, here.c]
        return remote(ours, ours, g_send.at[4], g_recv.at[4], here.partner())

    def gram_share():
        await_bytes(gram.at[pl.ds(0, peers - 1), 0], g_recv.at[3])
        gram_pass().start()

    gram_steps = (gram_scatter, gram_gather, gram_spread, gram_share)
    right_product(last)
    gram_own()

    @pl.loop(0, groups)
    def _(turn):
        g = last - turn
        await_bytes(rpair.at[pl.ds(4 * g, 4)], pair_recv.at[g])
        for sub in (0, 1):
            scatter(2 * g + 2, sub)

        @pl.when(g > 0)
        def _():
            right_product(g - 1)

        for i, step in enumerate(gram_steps):
            if i < groups:

                @pl.when(turn == i)
                def _():
                    step()

        for sub in (0, 1):
            scatter(2 * g + 1, sub)

    for i, step in enumerate(gram_steps):
        if i >= groups:
            step()
    psplit[0], psplit[1] = split(pt[...])
    settle()
    gram_pass().wait()
    m_ref[...] = gram[...].reshape(rank, rank)
    invert_factor(m_ref, block_ref, wsplit, onward)

    @pl.loop(chips - 3, chips)
    def _(n):
        halve(n)

    sums[...] = jnp.zeros_like(sums)

    def right_tile(at, width):
        columns = pl.ds(at, width)
        blocks = []
        for row in range(0, rank, 256):
            stop = row + 256
            blocks.append(
                dot3(
                    (wsplit[0, row:stop, 0:stop], wsplit[1, row:stop, 0:stop]),
                    (rsplit[0, 0:stop, columns], rsplit[1, 0:stop, columns]),
                    NN,
                )
            )
        right = jnp.concatenate(blocks, axis=0)
        for lane in range(0, width, 128):
            one = right[:, lane : lane + 128]
            sums[...] = sums[...] + one * one
        rsplit[0, :, columns], rsplit[1, :, columns] = split(right)
        pltpu.make_async_copy(
            rsplit.at[:, :, columns], r_hbm.at[:, :, columns], out_sem
        ).start()

    full = 256 * (b_ref.shape[1] // 256)

    @pl.loop(0, full // 256)
    def _(i):
        right_tile(pl.multiple_of(256 * i, 256), 256)

    if full < b_ref.shape[1]:
        right_tile(full, b_ref.shape[1] - full)
    squares[0] = jnp.sum(sums[...].T, axis=0, keepdims=True)

    @pl.loop(1, peers)
    def _(k):
        remote(
            squares.at[0], squares.at[k], sq_send, sq_recv, {"tensor": here.peer(k)}
        ).start()

    blocks = []
    for row in range(0, rank, 256):
        stop = row + 256
        blocks.append(
            dot3(
                (wsplit[0, row:stop, 0:stop], wsplit[1, row:stop, 0:stop]),
                (psplit[0, 0:stop, :], psplit[1, 0:stop, :]),
                NN,
            )
        )
    q = jnp.concatenate(blocks, axis=0).T
    qlow_ref[...] = (q * -0.05).astype(jnp.bfloat16)
    await_bytes(squares.at[pl.ds(1, peers - 1)], sq_recv)
    scales = lax.rsqrt(jnp.sum(squares[...], axis=0) * mean + 1e-06)
    qsplit_ref[0], qsplit_ref[1] = split(q * (scales * gain))
    lanes = lax.broadcasted_iota(jnp.int32, (32, rank), 1)
    rows = lax.broadcasted_iota(jnp.int32, (32, rank), 0) + 32 * here.z
    picked = jnp.where(lanes == rows, jnp.broadcast_to(scales, (32, rank)), 0.0)
    place = pl.ds(pl.multiple_of(32 * here.z, 32), 32)
    ours = (
        rsplit[0, place, :].astype(jnp.float32) + rsplit[1, place, :].astype(jnp.float32)
    ) * jnp.sum(picked, axis=1, keepdims=True)
    factor_ref[...] = jnp.where(here.c == 0, ours[0:16], ours[16:32])

    await_bytes(rsplit, out_sem)
    gather.end()
    collect.end()
    if last:
        for turn in (0, 1):
            await_bytes(first_parts.at[pl.ds(1, peers - 1)], p_send.at[turn])
    for turn in (2, 3):
        await_bytes(last_parts.at[pl.ds(1, peers - 1)], p_send.at[turn])
    await_bytes(gsplits.at[pl.ds(1, chips - 1)], g_send.at[1])
    await_bytes(gsums.at[pl.ds(0, chips - 1)], g_send.at[2])
    await_bytes(gram.at[pl.ds(0, peers - 1), 0], g_send.at[3])
    await_bytes(rpart.at[pl.ds(0, rank // 2)], pair_send)
    await_bytes(rall.at[pl.ds(0, 16 * (chips - 1))], rs_send)
    await_bytes(squares.at[pl.ds(1, peers - 1)], sq_send)


def finish(b_ref, qlow_ref, qsplit_ref, rsplit_ref, f_ref, momentum_ref, update_ref, factor_ref):
    right = (rsplit_ref[0], rsplit_ref[1])
    momentum_ref[...] = b_ref[...] + dot(qlow_ref[...], right[0], NN, None)
    update_ref[...] = dot3((qsplit_ref[0], qsplit_ref[1]), right, NN).astype(jnp.bfloat16)
    factor_ref[...] = f_ref[...]


def body(chips, peers, buffer, factor):
    rows, columns = buffer.shape
    rank = 32 * chips
    half = rank // peers // 2
    each = half // chips
    total_columns = columns * peers
    groups = chips // 4
    ring = chips // 2
    f32, bf16 = jnp.float32, jnp.bfloat16
    dma = pltpu.SemaphoreType.DMA
    vmem = pl.BlockSpec(memory_space=pltpu.VMEM)
    anywhere = pl.BlockSpec(memory_space=pl.ANY)
    qlow, qsplit, rsplit, factor_t = pl.pallas_call(
        functools.partial(
            kernel,
            chips,
            peers,
            1.0 / math.sqrt(total_columns),
            1.0 / total_columns,
            math.sqrt(rows * 2 * chips / rank),
        ),
        out_shape=(
            jax.ShapeDtypeStruct((rows, rank), bf16),
            jax.ShapeDtypeStruct((2, rows, rank), bf16),
            jax.ShapeDtypeStruct((2, rank, columns), bf16),
            jax.ShapeDtypeStruct((16, columns), f32),
        ),
        in_specs=[anywhere, vmem],
        out_specs=(vmem, vmem, anywhere, vmem),
        scratch_shapes=[
            pltpu.VMEM((rows, columns), f32),
            pltpu.VMEM((2, rank, columns), bf16),
            pltpu.VMEM((2, rows, columns), bf16),
            pltpu.VMEM((2, columns, rows), bf16),
            pltpu.VMEM((rank, columns), f32),
            pltpu.VMEM((2, 128, columns), bf16),
            pltpu.VMEM((rank, rows), f32),
            pltpu.VMEM((peers, max(groups - 1, 1) * 128 // peers, rows), f32),
            pltpu.VMEM((peers, 128 // peers, rows), f32),
            pltpu.VMEM((rank, rows), f32),
            pltpu.VMEM((rank, rows), f32),
            pltpu.VMEM((2, rank, rows), bf16),
            pltpu.VMEM((2 * half, rank), f32),
            pltpu.VMEM((half, rank), f32),
            pltpu.VMEM((chips, each, rank), f32),
            pltpu.VMEM((chips, each, rank), f32),
            pltpu.VMEM((chips, each, rank), f32),
            pltpu.VMEM((peers, 2, half, rank), f32),
            pltpu.VMEM((rank, rank), f32),
            pltpu.VMEM((128, 128), f32),
            pltpu.VMEM((2, rank, rank), bf16),
            pltpu.VMEM((rank, columns), f32),
            pltpu.VMEM((chips, 16, columns), f32),
            pltpu.VMEM((2, ring + 1, 16, columns), f32),
            pltpu.VMEM((rank, columns), f32),
            pltpu.VMEM((rank, 128), f32),
            pltpu.VMEM((peers, 1, rank), f32),
            dma,
            dma((2, ring, 4)),
            dma((chips,)),
            dma((4,)),
            dma((4,)),
            dma((5,)),
            dma((5,)),
            dma,
            dma((groups,)),
            dma,
            dma((2, ring, 4)),
            dma,
            dma((2, ring, 4)),
            dma((chips,)),
            dma,
            dma,
            dma,
            dma,
        ],
        compiler_params=pltpu.CompilerParams(
            collective_id=0, has_side_effects=True, vmem_limit_bytes=LIMIT
        ),
        name="low_rank_update",
    )(buffer, factor.T)

    def whole(*shape):
        return pl.BlockSpec(shape, lambda i: (0,) * len(shape))

    def tile(*lead):
        return pl.BlockSpec((*lead, 512), lambda i: (0,) * len(lead) + (i,))

    momentum, update, factor_t = pl.pallas_call(
        finish,
        grid=(pl.cdiv(columns, 512),),
        out_shape=(
            jax.ShapeDtypeStruct((rows, columns), f32),
            jax.ShapeDtypeStruct((rows, columns), bf16),
            jax.ShapeDtypeStruct((16, columns), f32),
        ),
        in_specs=[
            tile(rows),
            whole(rows, rank),
            whole(2, rows, rank),
            tile(2, rank),
            tile(16),
        ],
        out_specs=(tile(rows), tile(rows), tile(16)),
        compiler_params=pltpu.CompilerParams(vmem_limit_bytes=LIMIT),
        name="finish",
    )(buffer, qlow, qsplit, rsplit, factor_t)
    return momentum, update, factor_t.T


def solution(mesh):
    chips, peers = mesh.shape["dp"] // 2, mesh.shape["tensor"]
    placed = (P("dp", "tensor"), P("tensor", "dp"))
    return jax.shard_map(
        functools.partial(body, chips, peers),
        mesh=mesh,
        in_specs=placed,
        out_specs=(P("dp", "tensor"), P("dp", "tensor"), P("tensor", "dp")),
        check_vma=False,
    )
```

```python
import functools
import math

import jax
import jax.numpy as jnp
from jax import lax
from jax.experimental import pallas as pl
from jax.experimental.pallas import tpu as pltpu
from jax.sharding import PartitionSpec as P

MESH = pl.DeviceIdType.MESH
HIGHEST = lax.Precision.HIGHEST
NN = (((1,), (0,)), ((), ()))
LIMIT = 56 * 1024 * 1024


def dot(a, b, dims, precision):
    return lax.dot_general(
        a, b, dims, precision=precision, preferred_element_type=jnp.float32
    )


class Place:
    def __init__(self, chips, peers):
        dp = lax.axis_index("dp")
        self.z, self.c = dp // 2, dp % 2
        self.t = lax.axis_index("tensor")
        self.chips, self.peers = chips, peers
        self.next = {"dp": 2 * self.chip(1) + self.c}
        self.back = {"dp": 2 * self.chip(-1) + self.c}
        self.other = {"dp": 2 * self.z + 1 - self.c}

    def chip(self, offset):
        return lax.rem(self.z + offset + self.chips, self.chips)

    def at(self, offset):
        return {"dp": 2 * self.chip(offset) + self.c}

    def partner(self):
        return self.other

    def neighbour(self, way):
        return self.back if way else self.next

    def peer(self, k):
        return lax.rem(self.t + k, self.peers)


def remote(src, dst, send, recv, device):
    return pltpu.make_async_remote_copy(
        src_ref=src,
        dst_ref=dst,
        send_sem=send,
        recv_sem=recv,
        device_id=device,
        device_id_type=MESH,
    )


def await_bytes(ref, sem):
    pltpu.make_async_copy(ref, ref, sem).wait()


def enter(here, ring):
    barrier = pltpu.get_barrier_semaphore()

    def greet(device):
        pl.semaphore_signal(barrier, inc=1, device_id=device, device_id_type=MESH)

    @pl.loop(1, here.peers)
    def _(k):
        greet({"tensor": here.peer(k)})

    greet(here.partner())
    if ring:

        @pl.loop(1, here.chips)
        def _(k):
            greet(here.at(k))

        count = here.chips - 1
    else:
        greet(here.at(1))
        greet(here.at(-1))
        count = 2
    pl.semaphore_wait(barrier, here.peers - 1 + 1 + count)


def offset_of(n):
    return ((n + 1) // 2) * (2 * (n % 2) - 1)


def rows16(ref, chip, core, sub=None):
    start = 32 * chip + 16 * core
    if sub is None:
        return ref.at[pl.ds(pl.multiple_of(start, 16), 16)]
    return ref.at[pl.ds(pl.multiple_of(start + 8 * sub, 8), 8)]


def lane_parts(columns, count):
    tiles = columns // 128
    cuts = [128 * (tiles * i // count) for i in range(count + 1)]
    return [pl.ds(a, b - a) for a, b in zip(cuts, cuts[1:]) if b > a]


class Gather:
    def __init__(self, here, buf, parts, send, recv, pair_recv):
        self.here, self.buf, self.parts = here, buf, parts
        self.send, self.recv, self.pair_recv = send, recv, pair_recv
        self.half = here.chips // 2

    def forward(self, step, way, sub, h):
        here, sign = self.here, 1 - 2 * way
        rows = rows16(self.buf, here.chip(-sign * (step - 1)), here.c, sub)
        ref = rows.at[:, self.parts[h]]
        recv = self.recv.at[way, step - 1, 2 * sub + h]
        remote(ref, ref, self.send, recv, here.neighbour(way)).start()

    def share(self, offset, slot):
        here = self.here
        ref = rows16(self.buf, here.chip(offset), here.c)
        remote(ref, ref, self.send, self.pair_recv.at[slot], here.partner()).start()

    def begin(self):
        for sub in (0, 1):
            for h in range(len(self.parts)):
                for way in (0, 1):
                    self.forward(1, way, sub, h)
        self.share(0, 0)

    def step(self, step, sub):
        here = self.here

        def take(way, h):
            sign = 1 - 2 * way
            rows = rows16(self.buf, here.chip(-sign * step), here.c, sub)
            await_bytes(
                rows.at[:, self.parts[h]], self.recv.at[way, step - 1, 2 * sub + h]
            )

            @pl.when(step + 1 < self.half + (sub == way))
            def _():
                self.forward(step + 1, way, sub, h)

        for h in range(len(self.parts)):
            take(sub, h)

            @pl.when(step < self.half)
            def _():
                take(1 - sub, h)

        if sub == 1:
            self.share(step, 2 * step - 1)

            @pl.when(step < self.half)
            def _():
                self.share(-step, 2 * step)

    def shared(self, n):
        here = self.here
        ref = rows16(self.buf, here.chip(offset_of(n)), 1 - here.c)
        await_bytes(ref, self.pair_recv.at[n])

    def end(self):
        rows = 16 * (2 * self.here.chips - 1)
        await_bytes(self.buf.at[pl.ds(0, rows)], self.send)


def split(value):
    high = value.astype(jnp.bfloat16)
    return high, (value - high.astype(jnp.float32)).astype(jnp.bfloat16)


def dot3(a, b, dims):
    return (
        dot(a[0], b[0], dims, None) + dot(a[0], b[1], dims, None)
    ) + dot(a[1], b[0], dims, None)


def splat(value):
    return jnp.broadcast_to(value, (8, 128))


def eliminate(turn, carry, w_ref):
    s = carry
    lane = lax.broadcasted_iota(jnp.int32, (8, 128), 1)
    sublane = lax.broadcasted_iota(jnp.int32, (8, 128), 0)
    for half in (0, 8):
        block = (lane >= half) & (lane < half + 8)
        columns = [
            jnp.broadcast_to(s[:, half + j : half + j + 1], s.shape) for j in range(8)
        ]
        d = {
            (i, j): splat(columns[j][i : i + 1, :]) for j in range(8) for i in range(j, 8)
        }
        top = jnp.where(block, jnp.where(lane == sublane + half, 1.0, 0.0), s[0:8])
        r = [splat(top[i : i + 1, :]) for i in range(8)]
        root, inverse, t = [], [], {}
        for k in range(8):
            root.append(lax.rsqrt(d[k, k]))
            inverse.append(root[k] * root[k])
            for i in range(k + 1, 8):
                t[i, k] = d[i, k] * inverse[k]
                for j in range(k + 1, i + 1):
                    d[i, j] = d[i, j] - t[i, k] * d[j, k]
                r[i] = r[i] - t[i, k] * r[k]
        done = r[0] * root[0]
        for k in range(1, 8):
            done = jnp.where(sublane == k, r[k] * root[k], done)
        keep = (lane >= 128 - 16 * turn) | (lane < half + 8)
        w_ref[pl.ds(pl.multiple_of(16 * turn + half, 8), 8), :] = jnp.where(
            keep, done, 0.0
        )
        for k in range(7, -1, -1):
            r[k] = r[k] * inverse[k]
            for i in range(7, k, -1):
                r[k] = r[k] - t[i, k] * r[i]
        lanes = lax.broadcasted_iota(jnp.int32, (s.shape[0] - 8, 128), 1)
        s = jnp.where((lanes >= half) & (lanes < half + 8), 0.0, s[8:])
        for j in range(8):
            s = s - columns[j][8:] * r[j][0:1, :]
    blank = jnp.zeros((16, 128), jnp.float32)
    return pltpu.roll(jnp.concatenate([s, blank], axis=0), 112, 1)


def invert_factor(m_ref, block_ref, wsplit, between):
    rank = m_ref.shape[0]

    @pl.loop(0, rank // 128)
    def _(panel):
        here = pl.ds(pl.multiple_of(128 * panel, 128), 128)

        carry = m_ref[here, here]
        for first in (0, 2, 4, 6):
            carry = lax.fori_loop(
                first,
                first + 2,
                functools.partial(eliminate, w_ref=block_ref),
                carry[: 128 - 16 * first],
            )
            between(2 * panel + first // 4 + 1, first // 2 % 2)
        w = jnp.concatenate(
            [block_ref[0:16, :]]
            + [pltpu.roll(block_ref[16 * i : 16 * i + 16, :], 16 * i, 1) for i in range(1, 8)],
            axis=0,
        )
        m_ref[here, :] = dot(w, m_ref[here, :], NN, HIGHEST)
        m_ref[here, here] = w

        for last in range(rank // 128 - 1):

            @pl.when(panel == last)
            def _():
                start, stop = 128 * last, 128 * last + 128
                lower = m_ref[start:stop, stop:rank].T
                m_ref[stop:rank, start:stop] = jnp.zeros((rank - stop, 128), jnp.float32)
                m_ref[stop:rank, :] = m_ref[stop:rank, :] - dot(
                    lower, m_ref[start:stop, :], NN, HIGHEST
                )

        lanes = lax.broadcasted_iota(jnp.int32, (128, rank), 1)
        wsplit[0, here, :], wsplit[1, here, :] = split(
            jnp.where(lanes < 128 * panel + 128, m_ref[here, :], 0.0)
        )


def column_tiles(columns):
    return [(at, min(256, columns - at)) for at in range(0, columns, 256)]


def kernel(
    chips,
    peers,
    scale,
    mean,
    gain,
    b_hbm,
    f_ref,
    qlow_ref,
    qsplit_ref,
    r_hbm,
    factor_ref,
    b_ref,
    rsplit,
    bsplit,
    tsplit,
    fall,
    fsplit,
    part,
    first_parts,
    last_parts,
    arrived,
    pt,
    psplit,
    gpart,
    gpair,
    gsplit,
    gsplits,
    gsums,
    gram,
    m_ref,
    block_ref,
    wsplit,
    rpart,
    rpair,
    moving,
    rall,
    sums,
    squares,
    f_send,
    f_recv,
    f_pair,
    p_send,
    p_recv,
    g_send,
    g_recv,
    pair_send,
    pair_recv,
    rs_send,
    rs_recv,
    ag_send,
    ag_recv,
    ag_pair,
    sq_send,
    sq_recv,
    in_sem,
    out_sem,
):
    here = Place(chips, peers)
    rank = 32 * chips
    ring = chips // 2
    groups = chips // 4
    last = groups - 1
    tiles = column_tiles(b_ref.shape[1])
    load = pltpu.make_async_copy(b_hbm, b_ref, in_sem)
    load.start()
    own = rows16(fall, here.z, here.c)
    own[...] = f_ref[...]
    enter(here, True)
    halves = lane_parts(b_ref.shape[1], 2)
    gather = Gather(here, fall, halves, f_send, f_recv, f_pair)
    gather.begin()
    load.wait()

    def tile(i):
        return pl.ds(pl.multiple_of(128 * i, 128), 128)

    count = b_ref.shape[1] // 128

    def transpose(quarter):
        low, high = quarter * count // 4, (quarter + 1) * count // 4

        @pl.loop(low, high)
        def _(i):
            tsplit[0, tile(i), :], tsplit[1, tile(i), :] = split(b_ref[:, tile(i)].T)

    def straight(low, high):
        @pl.loop(low, high)
        def _(i):
            bsplit[0, :, tile(i)], bsplit[1, :, tile(i)] = split(b_ref[:, tile(i)])

    def join(g):
        order = [4 * g + n for n in range(4)]
        for n in order:
            gather.shared(n)
        rows = [
            fall[pl.ds(pl.multiple_of(32 * here.chip(offset_of(n)), 32), 32), :]
            for n in order
        ]
        fsplit[0], fsplit[1] = split(jnp.concatenate(rows, axis=0))

    def product(g, turn):
        rows = tile(g)
        one = dot(fsplit[turn // 2], tsplit[turn % 2], NN, None)
        part[rows, :] = part[rows, :] + one if turn else one

    def spread(base, rows, parts, turn):
        piece = rows // peers

        @pl.loop(1, peers)
        def _(k):
            other = here.peer(k)
            start = pl.multiple_of(base + piece * other, 8)
            remote(
                part.at[pl.ds(start, piece)],
                parts.at[k],
                p_send.at[turn],
                p_recv.at[turn],
                {"tensor": other},
            ).start()

    def total(base, rows, parts, turn):
        piece = rows // peers
        mine = pl.ds(pl.multiple_of(base + piece * here.t, 8), piece)
        parts[0] = part[mine, :]
        await_bytes(parts.at[pl.ds(1, peers - 1)], p_recv.at[turn])
        arrived[mine, :] = jnp.sum(parts[...], axis=0) * scale

        @pl.loop(1, peers)
        def _(k):
            place = arrived.at[mine]
            remote(
                place,
                place,
                p_send.at[turn + 1],
                p_recv.at[turn + 1],
                {"tensor": here.peer(k)},
            ).start()

    early = 128 * last

    def piece(g, i):
        if i == 0:
            join(g)
        else:
            product(g, i - 1)

    @pl.loop(0, groups)
    def _(g):
        for i in range(4):
            gather.step(2 * g + 1 + i // 2, i % 2)

            @pl.when(g == 0)
            def _():
                transpose(i)

            @pl.when(g > 0)
            def _():
                piece(g - 1, i)

    if last:
        spread(0, early, first_parts, 0)
    for i in range(4):
        piece(last, i)
    spread(early, 128, last_parts, 2)
    if last:
        total(0, early, first_parts, 0)
    straight(0, count // 2)
    total(early, 128, last_parts, 2)
    straight(count // 2, count)
    if last:
        await_bytes(first_parts.at[pl.ds(1, peers - 1)], p_recv.at[1])
    await_bytes(last_parts.at[pl.ds(1, peers - 1)], p_recv.at[3])

    @pl.loop(0, chips)
    def _(n):
        place = pl.ds(pl.multiple_of(32 * here.chip(offset_of(n)), 32), 32)
        pt[place, :] = arrived[pl.ds(pl.multiple_of(32 * n, 32), 32), :]

    def right_product(g):
        chipped = [here.chip(offset_of(4 * g + n)) for n in range(4)]
        p = split(arrived[tile(g), :])
        for at, width in tiles:
            b = (bsplit[0, :, at : at + width], bsplit[1, :, at : at + width])
            r = dot3(p, b, NN)
            for n, i in enumerate(chipped):
                place = pl.ds(pl.multiple_of(32 * i, 32), 32)
                rpart[place, at : at + width] = r[32 * n : 32 * n + 32, :]
        for n, i in enumerate(chipped):
            remote(
                rows16(rpart, i, 1 - here.c),
                rpair.at[4 * g + n],
                pair_send,
                pair_recv.at[g],
                here.partner(),
            ).start()

    def right_own(n, sub, lanes):
        chip = here.chip(offset_of(n))
        rows = rows16(rpart, chip, here.c, sub)
        return rows[:, lanes] + rpair[n, 8 * sub : 8 * sub + 8, lanes]

    def scatter(k, sub):
        def pass_on(way, come, h):
            lanes = halves[h]
            place = moving.at[way, k, pl.ds(8 * sub, 8), lanes]
            n = 2 * k - 1 if way == 0 else 2 * k - 2 * k // chips

            @pl.when(come)
            def _():
                await_bytes(place, rs_recv.at[way, k, 2 * sub + h])
                place[...] = place[...] + right_own(n, sub, lanes)

            @pl.when(jnp.logical_not(come))
            def _():
                place[...] = right_own(n, sub, lanes)

            remote(
                place,
                moving.at[way, k - 1, pl.ds(8 * sub, 8), lanes],
                rs_send,
                rs_recv.at[way, k - 1, 2 * sub + h],
                here.neighbour(way),
            ).start()

        for h in range(len(halves)):
            pass_on(sub, k < ring, h)

            @pl.when(k < ring)
            def _():
                pass_on(1 - sub, k < ring - 1, h)

    collect = Gather(here, rall, lane_parts(b_ref.shape[1], 1), ag_send, ag_recv, ag_pair)

    def settle():
        for sub in (0, 1):
            for h, lanes in enumerate(halves):
                for way in (0, 1):
                    place = moving.at[way, 0, pl.ds(8 * sub, 8), lanes]
                    await_bytes(place, rs_recv.at[way, 0, 2 * sub + h])
                rows16(rall, here.z, here.c, sub)[:, lanes] = (
                    right_own(0, sub, lanes)
                    + moving[0, 0, 8 * sub : 8 * sub + 8, lanes]
                    + moving[1, 0, 8 * sub : 8 * sub + 8, lanes]
                )
        collect.begin()

    def halve(n):
        collect.shared(n)
        place = pl.ds(pl.multiple_of(32 * here.chip(offset_of(n)), 32), 32)
        rsplit[0, place, :], rsplit[1, place, :] = split(rall[place, :])

    def onward(step, sub):
        collect.step(step, sub)

        @pl.when(2 * step - 5 + sub >= 0)
        def _():
            halve(2 * step - 5 + sub)

    block = rank // peers
    half = block // 2
    each = half // chips
    mine = pl.ds(pl.multiple_of(block * here.t, block), block)
    theirs = pl.ds(pl.multiple_of(half * (1 - here.c), half), half)
    keep = pl.ds(pl.multiple_of(half * here.c, half), half)

    def gram_pair():
        return remote(
            gpart.at[theirs], gpair, g_send.at[0], g_recv.at[0], here.partner()
        )

    def gram_own():
        gpart[...] = dot(pt[mine, :], pt[...].T, NN, HIGHEST)
        gram_pair().start()

    def gram_scatter():
        gram_pair().wait()
        chip_sum = gpart[keep, :] + gpair[...]
        for k in range(chips):
            gsplit[k] = chip_sum[each * k : each * (k + 1), :]

        @pl.loop(1, chips)
        def _(k):
            remote(
                gsplit.at[here.chip(k)],
                gsplits.at[k],
                g_send.at[1],
                g_recv.at[1],
                here.at(k),
            ).start()

        gsplits[0] = gsplit[here.z]

    def gram_gather():
        await_bytes(gsplits.at[pl.ds(1, chips - 1)], g_recv.at[1])
        gsums[here.z] = jnp.sum(gsplits[...], axis=0)

        @pl.loop(1, chips)
        def _(k):
            place = gsums.at[here.z]
            remote(place, place, g_send.at[2], g_recv.at[2], here.at(k)).start()

    def gram_spread():
        await_bytes(gsums.at[pl.ds(0, chips - 1)], g_recv.at[2])
        gram[here.t, here.c] = gsums[...].reshape(half, rank)

        @pl.loop(1, peers)
        def _(k):
            place = gram.at[here.t, here.c]
            remote(
                place, place, g_send.at[3], g_recv.at[3], {"tensor": here.peer(k)}
            ).start()

    def gram_pass():
        ours = gram.at[:, here.c]
        return remote(ours, ours, g_send.at[4], g_recv.at[4], here.partner())

    def gram_share():
        await_bytes(gram.at[pl.ds(0, peers - 1), 0], g_recv.at[3])
        gram_pass().start()

    gram_steps = (gram_scatter, gram_gather, gram_spread, gram_share)
    right_product(last)
    gram_own()

    @pl.loop(0, groups)
    def _(turn):
        g = last - turn
        await_bytes(rpair.at[pl.ds(4 * g, 4)], pair_recv.at[g])
        for sub in (0, 1):
            scatter(2 * g + 2, sub)

        @pl.when(g > 0)
        def _():
            right_product(g - 1)

        for i, step in enumerate(gram_steps):
            if i < groups:

                @pl.when(turn == i)
                def _():
                    step()

        for sub in (0, 1):
            scatter(2 * g + 1, sub)

    for i, step in enumerate(gram_steps):
        if i >= groups:
            step()
    psplit[0], psplit[1] = split(pt[...])
    settle()
    gram_pass().wait()
    m_ref[...] = gram[...].reshape(rank, rank)
    invert_factor(m_ref, block_ref, wsplit, onward)

    @pl.loop(chips - 3, chips)
    def _(n):
        halve(n)

    sums[...] = jnp.zeros_like(sums)

    def right_tile(at, width):
        columns = pl.ds(at, width)
        blocks = []
        for row in range(0, rank, 256):
            stop = row + 256
            blocks.append(
                dot3(
                    (wsplit[0, row:stop, 0:stop], wsplit[1, row:stop, 0:stop]),
                    (rsplit[0, 0:stop, columns], rsplit[1, 0:stop, columns]),
                    NN,
                )
            )
        right = jnp.concatenate(blocks, axis=0)
        for lane in range(0, width, 128):
            one = right[:, lane : lane + 128]
            sums[...] = sums[...] + one * one
        rsplit[0, :, columns], rsplit[1, :, columns] = split(right)
        pltpu.make_async_copy(
            rsplit.at[:, :, columns], r_hbm.at[:, :, columns], out_sem
        ).start()

    full = 256 * (b_ref.shape[1] // 256)

    @pl.loop(0, full // 256)
    def _(i):
        right_tile(pl.multiple_of(256 * i, 256), 256)

    if full < b_ref.shape[1]:
        right_tile(full, b_ref.shape[1] - full)
    squares[0] = jnp.sum(sums[...].T, axis=0, keepdims=True)

    @pl.loop(1, peers)
    def _(k):
        remote(
            squares.at[0], squares.at[k], sq_send, sq_recv, {"tensor": here.peer(k)}
        ).start()

    blocks = []
    for row in range(0, rank, 256):
        stop = row + 256
        blocks.append(
            dot3(
                (wsplit[0, row:stop, 0:stop], wsplit[1, row:stop, 0:stop]),
                (psplit[0, 0:stop, :], psplit[1, 0:stop, :]),
                NN,
            )
        )
    q = jnp.concatenate(blocks, axis=0).T
    qlow_ref[...] = (q * -0.05).astype(jnp.bfloat16)
    await_bytes(squares.at[pl.ds(1, peers - 1)], sq_recv)
    scales = lax.rsqrt(jnp.sum(squares[...], axis=0) * mean + 1e-06)
    qsplit_ref[0], qsplit_ref[1] = split(q * (scales * gain))
    lanes = lax.broadcasted_iota(jnp.int32, (32, rank), 1)
    rows = lax.broadcasted_iota(jnp.int32, (32, rank), 0) + 32 * here.z
    picked = jnp.where(lanes == rows, jnp.broadcast_to(scales, (32, rank)), 0.0)
    place = pl.ds(pl.multiple_of(32 * here.z, 32), 32)
    ours = (
        rsplit[0, place, :].astype(jnp.float32) + rsplit[1, place, :].astype(jnp.float32)
    ) * jnp.sum(picked, axis=1, keepdims=True)
    factor_ref[...] = jnp.where(here.c == 0, ours[0:16], ours[16:32])

    await_bytes(rsplit, out_sem)
    gather.end()
    collect.end()
    if last:
        for turn in (0, 1):
            await_bytes(first_parts.at[pl.ds(1, peers - 1)], p_send.at[turn])
    for turn in (2, 3):
        await_bytes(last_parts.at[pl.ds(1, peers - 1)], p_send.at[turn])
    await_bytes(gsplits.at[pl.ds(1, chips - 1)], g_send.at[1])
    await_bytes(gsums.at[pl.ds(0, chips - 1)], g_send.at[2])
    await_bytes(gram.at[pl.ds(0, peers - 1), 0], g_send.at[3])
    await_bytes(rpart.at[pl.ds(0, rank // 2)], pair_send)
    await_bytes(rall.at[pl.ds(0, 16 * (chips - 1))], rs_send)
    await_bytes(squares.at[pl.ds(1, peers - 1)], sq_send)


def finish(b_ref, qlow_ref, qsplit_ref, rsplit_ref, f_ref, momentum_ref, update_ref, factor_ref):
    right = (rsplit_ref[0], rsplit_ref[1])
    momentum_ref[...] = b_ref[...] + dot(qlow_ref[...], right[0], NN, None)
    update_ref[...] = dot3((qsplit_ref[0], qsplit_ref[1]), right, NN).astype(jnp.bfloat16)
    factor_ref[...] = f_ref[...]


def body(chips, peers, buffer, factor):
    rows, columns = buffer.shape
    rank = 32 * chips
    half = rank // peers // 2
    each = half // chips
    total_columns = columns * peers
    groups = chips // 4
    ring = chips // 2
    f32, bf16 = jnp.float32, jnp.bfloat16
    dma = pltpu.SemaphoreType.DMA
    vmem = pl.BlockSpec(memory_space=pltpu.VMEM)
    anywhere = pl.BlockSpec(memory_space=pl.ANY)
    qlow, qsplit, rsplit, factor_t = pl.pallas_call(
        functools.partial(
            kernel,
            chips,
            peers,
            1.0 / math.sqrt(total_columns),
            1.0 / total_columns,
            math.sqrt(rows * 2 * chips / rank),
        ),
        out_shape=(
            jax.ShapeDtypeStruct((rows, rank), bf16),
            jax.ShapeDtypeStruct((2, rows, rank), bf16),
            jax.ShapeDtypeStruct((2, rank, columns), bf16),
            jax.ShapeDtypeStruct((16, columns), f32),
        ),
        in_specs=[anywhere, vmem],
        out_specs=(vmem, vmem, anywhere, vmem),
        scratch_shapes=[
            pltpu.VMEM((rows, columns), f32),
            pltpu.VMEM((2, rank, columns), bf16),
            pltpu.VMEM((2, rows, columns), bf16),
            pltpu.VMEM((2, columns, rows), bf16),
            pltpu.VMEM((rank, columns), f32),
            pltpu.VMEM((2, 128, columns), bf16),
            pltpu.VMEM((rank, rows), f32),
            pltpu.VMEM((peers, max(groups - 1, 1) * 128 // peers, rows), f32),
            pltpu.VMEM((peers, 128 // peers, rows), f32),
            pltpu.VMEM((rank, rows), f32),
            pltpu.VMEM((rank, rows), f32),
            pltpu.VMEM((2, rank, rows), bf16),
            pltpu.VMEM((2 * half, rank), f32),
            pltpu.VMEM((half, rank), f32),
            pltpu.VMEM((chips, each, rank), f32),
            pltpu.VMEM((chips, each, rank), f32),
            pltpu.VMEM((chips, each, rank), f32),
            pltpu.VMEM((peers, 2, half, rank), f32),
            pltpu.VMEM((rank, rank), f32),
            pltpu.VMEM((128, 128), f32),
            pltpu.VMEM((2, rank, rank), bf16),
            pltpu.VMEM((rank, columns), f32),
            pltpu.VMEM((chips, 16, columns), f32),
            pltpu.VMEM((2, ring + 1, 16, columns), f32),
            pltpu.VMEM((rank, columns), f32),
            pltpu.VMEM((rank, 128), f32),
            pltpu.VMEM((peers, 1, rank), f32),
            dma,
            dma((2, ring, 4)),
            dma((chips,)),
            dma((4,)),
            dma((4,)),
            dma((5,)),
            dma((5,)),
            dma,
            dma((groups,)),
            dma,
            dma((2, ring, 4)),
            dma,
            dma((2, ring, 4)),
            dma((chips,)),
            dma,
            dma,
            dma,
            dma,
        ],
        compiler_params=pltpu.CompilerParams(
            collective_id=0, has_side_effects=True, vmem_limit_bytes=LIMIT
        ),
        name="low_rank_update",
    )(buffer, factor.T)

    def whole(*shape):
        return pl.BlockSpec(shape, lambda i: (0,) * len(shape))

    def tile(*lead):
        return pl.BlockSpec((*lead, 512), lambda i: (0,) * len(lead) + (i,))

    momentum, update, factor_t = pl.pallas_call(
        finish,
        grid=(pl.cdiv(columns, 512),),
        out_shape=(
            jax.ShapeDtypeStruct((rows, columns), f32),
            jax.ShapeDtypeStruct((rows, columns), bf16),
            jax.ShapeDtypeStruct((16, columns), f32),
        ),
        in_specs=[
            tile(rows),
            whole(rows, rank),
            whole(2, rows, rank),
            tile(2, rank),
            tile(16),
        ],
        out_specs=(tile(rows), tile(rows), tile(16)),
        compiler_params=pltpu.CompilerParams(vmem_limit_bytes=LIMIT),
        name="finish",
    )(buffer, qlow, qsplit, rsplit, factor_t)
    return momentum, update, factor_t.T


def solution(mesh):
    chips, peers = mesh.shape["dp"] // 2, mesh.shape["tensor"]
    placed = (P("dp", "tensor"), P("tensor", "dp"))
    return jax.shard_map(
        functools.partial(body, chips, peers),
        mesh=mesh,
        in_specs=placed,
        out_specs=(P("dp", "tensor"), P("dp", "tensor"), P("tensor", "dp")),
        check_vma=False,
    )
```
